32 devices in a mesh: ctx: 8 (over z, x), fsdp: 4 (over y, core).
Axes of the slice: x: 2, y: 2, z: 4, core: 2. Of those that a mesh axis runs over, the one named last changes fastest.
Arguments:
- tokens: bfloat16 [4, 1024, 1024], P('fsdp', 'ctx'), may hold values from -6 to 6
- cotangent: bfloat16 [4, 1024, 1024], P('fsdp', 'ctx'), may hold values from -6 to 6
- segments: int32 [4, 1024], P('fsdp'), may hold values from 0 to 1, as said below
- decay_index: int32 [4, 16, 8], P('fsdp'), may hold values from 0 to 8
- step_index: int32 [4, 16, 8], P('fsdp'), may hold values from 0 to 3
- w_qkv: bfloat16 [1024, 3072], P('fsdp'), may hold values from -0.1875 to 0.1875
- w_gate: bfloat16 [1024, 1024], P('fsdp'), may hold values from -0.1875 to 0.1875
- w_out: bfloat16 [1024, 1024], P('fsdp'), may hold values from -0.5 to 0.5
- w_gu: bfloat16 [1024, 5632], P('fsdp'), may hold values from -0.1875 to 0.1875
- w_down: bfloat16 [2816, 1024], P('fsdp'), may hold values from -0.109375 to 0.109375
- persist_keys: bfloat16 [16, 1024], P('fsdp'), may hold values from -5 to 5
- persist_values: bfloat16 [16, 1024], P('fsdp'), may hold values from -5 to 5
- norm_gain: bfloat16 [1024], P('fsdp'), may hold values from 0.5 to 1.5
- ffn_gain: bfloat16 [1024], P('fsdp'), may hold values from 0.5 to 1.5
Outputs:
- output: bfloat16 [4, 1024, 1024], P('fsdp', 'ctx')
- grad_tokens: float32 [4, 1024, 1024], P('fsdp', 'ctx')
- grad_w_qkv: float32 [1024, 3072], P('fsdp')
- grad_w_gate: float32 [1024, 1024], P('fsdp')
- grad_w_out: float32 [1024, 1024], P('fsdp')
- grad_w_gu: float32 [1024, 5632], P('fsdp')
- grad_w_down: float32 [2816, 1024], P('fsdp')
- grad_persist_keys: float32 [16, 1024], P('fsdp')
- grad_persist_values: float32 [16, 1024], P('fsdp')
- grad_norm_gain: float32 [1024], P('fsdp')
- grad_ffn_gain: float32 [1024], P('fsdp')
The draws below stay inside these ranges and needn't reach their ends.
Inputs may be any that keep to these rules, and one draw needn't show every extreme that they name: `segments`: segment numbers start at 0 and never fall along positions; segment 0 covers at least positions 0 to 511; the last position of every sequence has the largest number, and the last document may be longer than 2000.
All inputs are finite; a program needn't handle non-finite values.
Results may differ from the reference program's by a relative error of at most 0.02.
Values may be sent and summed in bfloat16 or wider, within the bound.
No kernel may reach another device: no remote copies, remote signals or barrier semaphores. Data moves between devices by JAX's collectives and lax.ppermute only.
A program may use at most 384 MiB of HBM per device.

```python
import jax
import jax.numpy as jnp
from jax import lax

D = 1024
HEADS = 8
HEAD_WIDTH_SIZE = 128
FF = 2816
PERSIST = 16
GROUP = 64
DOC_MIN = 200
DOC_MAX = 2000
TOK_DEV = 128
SEQ_LEN = 1024
SEQS = 4
GROUPS = 16
N_CTX = 8


def one_sequence(seq_key):
    first_key, second_key = jax.random.split(seq_key)
    half_rows = TOK_DEV // 2
    long_end = N_CTX * half_rows + jax.random.randint(first_key, (), 0, half_rows, dtype=jnp.int32)
    doc_count = SEQ_LEN // DOC_MIN + 1
    doc_lengths = jax.random.randint(second_key, (doc_count,), DOC_MIN, DOC_MAX + 1, dtype=jnp.int32)
    doc_starts = long_end + jnp.cumsum(doc_lengths) - doc_lengths
    position = jnp.arange(SEQ_LEN, dtype=jnp.int32)
    numbers = jnp.sum((position[:, None] >= doc_starts[None, :]).astype(jnp.int32), axis=1).astype(jnp.int32)
    top_number = 1 + (SEQ_LEN // 2 - TOK_DEV // 2 - 1) // DOC_MAX
    return jnp.minimum(numbers, top_number).astype(jnp.int32)


def draw_segments(key, part):
    key = jax.random.fold_in(key, 11)
    seq_keys = jax.random.split(key, SEQS)
    return jax.vmap(one_sequence)(seq_keys)


def set_ends(values, key, low, high):
    shape = values.shape
    spot = [jax.random.randint(jax.random.fold_in(key, axis), (), 0, shape[axis]) for axis in range(len(shape))]
    values = values.at[tuple(spot)].set(low)
    longest = shape.index(max(shape))
    spot[longest] = (spot[longest] + 1) % shape[longest]
    return values.at[tuple(spot)].set(high)


def block_scale(own_key, extent, cuts, low, top_value):
    level, own = 1.0, jax.random.fold_in(own_key, 6)
    for dim, parts in cuts:
        draws = jnp.exp(jax.random.uniform(jax.random.fold_in(own, dim), (parts,), jnp.float32, low / len(cuts), top_value / len(cuts)))
        level = level * jnp.repeat(draws, extent[dim] // parts).reshape([-1 if axis == dim else 1 for axis in range(len(extent))])
    return level


def bell_draw(stream_key, shape, deviation, limit, pieces=(), held_as=jnp.bfloat16):
    entries = jax.random.normal(stream_key, shape, jnp.float32) * deviation
    if len(pieces) > 0:
        entries = block_scale(stream_key, shape, pieces, -0.22, 0.18) * entries
    return jnp.clip(entries, min=-limit, max=limit).astype(held_as)


def setup_inputs(seed: int = 0) -> dict:
    seeds = jax.random.split(jax.random.key(seed), 15)
    return {
        "tokens": bell_draw(seeds[0], (SEQS, SEQ_LEN, D), 1.0, 6.0, ((0, 4), (1, 8))),
        "cotangent": bell_draw(seeds[1], (SEQS, SEQ_LEN, D), 1.0, 6.0, ((0, 4), (1, 8))),
        "segments": draw_segments(jax.random.fold_in(seeds[14], 71), 0),
        "decay_index": set_ends(jax.random.randint(seeds[3], (SEQS, GROUPS, HEADS), 0, 9), jax.random.fold_in(seeds[3], 1), 0, 8).astype(jnp.int32),
        "step_index": set_ends(jax.random.randint(seeds[4], (SEQS, GROUPS, HEADS), 0, 4), jax.random.fold_in(seeds[4], 1), 0, 3).astype(jnp.int32),
        "w_qkv": bell_draw(seeds[5], (D, 3 * D), D ** -0.5, 0.1875, ((0, 4),)),
        "w_gate": bell_draw(seeds[6], (D, D), D ** -0.5, 0.1875, ((0, 4),)),
        "w_out": bell_draw(seeds[7], (D, D), (D // 8) ** -0.5, 0.5, ((0, 4),)),
        "w_gu": bell_draw(seeds[8], (D, 2 * FF), D ** -0.5, 0.1875, ((0, 4),)),
        "w_down": bell_draw(seeds[9], (FF, D), FF ** -0.5, 0.109375, ((0, 4),)),
        "persist_keys": bell_draw(seeds[10], (PERSIST, D), 1.0, 5.0, ((0, 4),)),
        "persist_values": bell_draw(seeds[11], (PERSIST, D), 1.0, 5.0, ((0, 4),)),
        "norm_gain": jnp.clip(1.0 + 0.1 * jax.random.normal(seeds[12], (D,), jnp.float32), 0.5, 1.5).astype(jnp.bfloat16),
        "ffn_gain": jnp.clip(1.0 + 0.1 * jax.random.normal(seeds[13], (D,), jnp.float32), 0.5, 1.5).astype(jnp.bfloat16),
    }


epsilon = 1e-06
momentum = 0.9
masked_score = -1e+30
highest_precision = lax.Precision.HIGHEST

@jax.custom_vjp
def low(v):
    return lax.optimization_barrier(v.astype(jnp.bfloat16)).astype(jnp.float32)

@jax.custom_vjp
def low_back(v):
    return v

def low_keep(v):
    return (low(v), None)

def low_pass(kept, grad):
    return (grad,)

def back_keep(v):
    return (v, None)

def back_low(kept, grad):
    return (low(grad),)
low.defvjp(low_keep, low_pass)
low_back.defvjp(back_keep, back_low)

def rms_norm(values, gain_vec):
    return values * lax.rsqrt(lax.optimization_barrier(jnp.mean(values * values, axis=-1, keepdims=True)) + epsilon) * gain_vec

def natural_rows(length_all):
    half_rows = TOK_DEV // 2
    position = jnp.arange(length_all, dtype=jnp.int32)
    block_id = position // half_rows
    offset_row = position % half_rows
    is_early = block_id < N_CTX
    owner_dev = jnp.where(is_early, block_id, 2 * N_CTX - 1 - block_id)
    return owner_dev * TOK_DEV + jnp.where(is_early, offset_row, half_rows + offset_row)

def storage_positions(length_all):
    half_rows = TOK_DEV // 2
    row_index = jnp.arange(length_all, dtype=jnp.int32)
    owner_dev = row_index // TOK_DEV
    inner_row = row_index % TOK_DEV
    block_id = jnp.where(inner_row < half_rows, owner_dev, 2 * N_CTX - 1 - owner_dev)
    return block_id * half_rows + inner_row % half_rows

def attention(queries, keys_all, values_all, pkeys, pvalues, segment_row):
    length_all = queries.shape[0]
    block_rows = min(512, length_all)
    scale_factor = HEAD_WIDTH_SIZE ** (-0.5)
    position = jnp.arange(length_all, dtype=jnp.int32)
    every_keys = jnp.concatenate([pkeys, keys_all], axis=0)
    every_values = jnp.concatenate([pvalues, values_all], axis=0)

    def one_block(block_index):
        first_row = block_index * block_rows
        query_block = lax.dynamic_slice_in_dim(queries, first_row, block_rows, 0)
        query_pos = first_row + jnp.arange(block_rows, dtype=jnp.int32)
        query_seg = lax.dynamic_slice_in_dim(segment_row, first_row, block_rows, 0)
        scores = jnp.einsum('qhd,khd->hqk', query_block, every_keys, precision=highest_precision) * scale_factor
        allowed = (segment_row[None, :] == query_seg[:, None]) & (position[None, :] <= query_pos[:, None])
        allowed = jnp.concatenate([jnp.ones((block_rows, PERSIST), dtype=jnp.bool_), allowed], axis=1)
        scores = low_back(jnp.where(allowed[None], scores, masked_score))
        weights = low(jax.nn.softmax(scores, axis=-1))
        return jnp.einsum('hqk,khd->qhd', weights, every_values, precision=highest_precision)
    block_outs = lax.map(jax.checkpoint(one_block), jnp.arange(length_all // block_rows, dtype=jnp.int32))
    return block_outs.reshape(length_all, HEADS * HEAD_WIDTH_SIZE)

def memory_recall(queries, keys_all, values_all, alphas, thetas):
    length_all = queries.shape[0]
    count_groups = length_all // GROUP
    scale_factor = HEAD_WIDTH_SIZE ** (-0.5)
    query_groups = (queries * scale_factor).reshape(count_groups, GROUP, HEADS, HEAD_WIDTH_SIZE)
    key_groups = (keys_all * scale_factor).reshape(count_groups, GROUP, HEADS, HEAD_WIDTH_SIZE)
    value_groups = values_all.reshape(count_groups, GROUP, HEADS, HEAD_WIDTH_SIZE)

    def one_group(carried, inputs):
        current_memory, moment_now = carried
        group_query_rows, group_key_rows, group_value_rows, alpha_row, learning_rate_row = inputs
        recalled_rows = jnp.einsum('ipb,pbx->ipx', group_query_rows, current_memory, precision=highest_precision)
        gram_matrix = jnp.einsum('thk,thj->hkj', group_key_rows, group_key_rows, precision=highest_precision) * learning_rate_row[:, None, None]
        mixed_product = jnp.einsum('qgw,qgc->gwc', group_key_rows, group_value_rows, precision=highest_precision) * learning_rate_row[:, None, None]
        memory_gradient = jnp.einsum('fld,fdi->fli', gram_matrix, current_memory, precision=highest_precision) - mixed_product
        moment_next = momentum * moment_now - memory_gradient
        memory_next = (1.0 - alpha_row)[:, None, None] * current_memory + moment_next
        return ((memory_next, moment_next), recalled_rows)
    zero_state = jnp.zeros((HEADS, HEAD_WIDTH_SIZE, HEAD_WIDTH_SIZE), jnp.float32)
    _, recalled_rows = lax.scan(jax.checkpoint(one_group), (zero_state, zero_state), (query_groups, key_groups, value_groups, alphas, thetas))
    return recalled_rows.reshape(length_all, HEADS * HEAD_WIDTH_SIZE)

def layer(params, tokens_seq, segment_row, decay_row, step_row):
    w_qkv, w_gate, w_out, w_gu, w_down, persist_keys, persist_values, norm_gain, ffn_gain = params
    length_all = tokens_seq.shape[0]
    inputs_nat = tokens_seq[natural_rows(length_all)]
    normed = low(rms_norm(inputs_nat, norm_gain))
    projected = low(low_back(jnp.dot(normed, w_qkv, precision=highest_precision)))
    queries = projected[:, :D]
    keys_all = projected[:, D:2 * D]
    values_all = projected[:, 2 * D:]
    gate_open = jax.nn.sigmoid(low_back(jnp.dot(normed, w_gate, precision=highest_precision)))
    attended = attention(queries.reshape(length_all, HEADS, HEAD_WIDTH_SIZE), keys_all.reshape(length_all, HEADS, HEAD_WIDTH_SIZE), values_all.reshape(length_all, HEADS, HEAD_WIDTH_SIZE), persist_keys.reshape(PERSIST, HEADS, HEAD_WIDTH_SIZE), persist_values.reshape(PERSIST, HEADS, HEAD_WIDTH_SIZE), segment_row)
    alphas = 0.6 * jnp.exp2(-decay_row.astype(jnp.float32))
    thetas = 0.1 * jnp.exp2(-step_row.astype(jnp.float32))
    recall = low_back(memory_recall(queries, keys_all, values_all, alphas, thetas))
    mixed_sum = low(low_back(attended + gate_open * recall))
    residual = inputs_nat + low_back(jnp.dot(mixed_sum, w_out, precision=highest_precision))
    normed_two = low(rms_norm(residual, ffn_gain))
    gate_up = low_back(jnp.dot(normed_two, w_gu, precision=highest_precision))
    active = low(jax.nn.silu(gate_up[:, :FF]) * gate_up[:, FF:])
    result = residual + jnp.dot(active, w_down, precision=highest_precision)
    return result[storage_positions(length_all)]

def reference(tokens, cotangent, segments, decay_index, step_index, w_qkv, w_gate, w_out, w_gu, w_down, persist_keys, persist_values, norm_gain, ffn_gain):
    params = tuple((weight.astype(jnp.float32) for weight in (w_qkv, w_gate, w_out, w_gu, w_down, persist_keys, persist_values, norm_gain, ffn_gain)))
    inputs_all = tokens.astype(jnp.float32)

    def forward(params_now, inputs_now):

        def per_sequence(packed):
            tokens_seq, segment_row, decay_row, step_row = packed
            return layer(params_now, tokens_seq, segment_row, decay_row, step_row)
        return lax.map(per_sequence, (inputs_now, segments, decay_index, step_index))
    result, pull_back = jax.vjp(forward, params, inputs_all)
    grad_params, grad_inputs = pull_back(cotangent.astype(jnp.float32))
    return (result.astype(jnp.bfloat16), grad_inputs, grad_params[0], grad_params[1], grad_params[2], grad_params[3], grad_params[4], grad_params[5], grad_params[6], grad_params[7], grad_params[8])
```

```python
import jax
import jax.numpy as jnp
import numpy as np
from jax import lax
from jax.experimental import pallas as pl
from jax.experimental.pallas import tpu as pltpu
from jax.sharding import PartitionSpec as P

HEADS = 8
HEAD_WIDTH_SIZE = 128
FF = 2816
GROUP = 64


epsilon = 1e-06
momentum = 0.9
masked_score = -1e30
highest_precision = lax.Precision.HIGHEST


def rms_scale(values):
    return lax.rsqrt(jnp.mean(values * values, axis=-1, keepdims=True) + epsilon)


def norm_back(values, inv_rms, gain_vec, grad_normed):
    scaled_grad = grad_normed * gain_vec
    grad_gain = jnp.sum(grad_normed * values * inv_rms, axis=0)
    grad_values = inv_rms * scaled_grad - values * inv_rms * inv_rms * inv_rms * jnp.mean(
        scaled_grad * values, axis=-1, keepdims=True
    )
    return (grad_values, grad_gain)


def place_rows(row_index, shard_rows, dev_count):
    half_rows = shard_rows // 2
    owner_dev = row_index // shard_rows
    inner_row = row_index % shard_rows
    block_id = jnp.where(inner_row < half_rows, owner_dev, 2 * dev_count - 1 - owner_dev)
    return block_id * half_rows + inner_row % half_rows


def position_order(stored, dev_count):
    rows = stored.shape[0]
    rest = stored.shape[1:]
    split = stored.reshape((dev_count, 2, rows // (2 * dev_count)) + rest)
    early = split[:, 0].reshape((-1,) + rest)
    late = split[::-1, 1].reshape((-1,) + rest)
    return jnp.concatenate([early, late], axis=0)


def key_mask(query_pos, query_seg, key_pos, key_seg):
    return (key_seg[None, :] == query_seg[:, None]) & (key_pos[None, :] <= query_pos[:, None])


def head_scores(queries, key_block):
    return jnp.einsum(
        "qhd,khd->hqk", queries, key_block, preferred_element_type=jnp.float32
    ) * HEAD_WIDTH_SIZE ** (-0.5)


def online_step(running, scores, value_block):
    run_max, run_total, accumulated = running
    new_max = jnp.maximum(run_max, jnp.max(scores, axis=-1))
    rescale = jnp.exp(run_max - new_max)
    weights = jnp.exp(scores - new_max[:, :, None])
    run_total = run_total * rescale + jnp.sum(weights, axis=-1)
    update = jnp.einsum(
        "hqk,khd->qhd",
        weights.astype(jnp.bfloat16),
        value_block,
        preferred_element_type=jnp.float32,
    )
    accumulated = accumulated * jnp.transpose(rescale)[:, :, None] + update
    return (new_max, run_total, accumulated)


def fold_keys(running, all_keys, all_values, context):
    queries, query_pos, query_seg, segment_all, shard_rows, dev_count = context
    total_rows = all_keys.shape[0]
    block_rows = min(512, total_rows)

    def fold_one_block(carried, block_index):
        offset_row = block_index * block_rows
        key_block = lax.dynamic_slice_in_dim(all_keys, offset_row, block_rows, 0).reshape(
            block_rows, HEADS, HEAD_WIDTH_SIZE
        )
        value_block = lax.dynamic_slice_in_dim(all_values, offset_row, block_rows, 0).reshape(
            block_rows, HEADS, HEAD_WIDTH_SIZE
        )
        key_pos = place_rows(
            offset_row + jnp.arange(block_rows, dtype=jnp.int32), shard_rows, dev_count
        )
        key_seg = jnp.take(segment_all, key_pos)
        allowed = key_mask(query_pos, query_seg, key_pos, key_seg)
        scores = jnp.where(allowed[None], head_scores(queries, key_block), masked_score)
        carried = online_step(carried, scores, value_block)
        return (carried, None)

    running, _ = lax.scan(
        fold_one_block, running, jnp.arange(total_rows // block_rows, dtype=jnp.int32)
    )
    return running


def back_every_key(grad_query, all_keys, all_values, context, grad_heads, log_total, row_delta):
    queries, query_pos, query_seg, segment_all, shard_rows, dev_count = context
    total_rows = all_keys.shape[0]
    block_rows = min(512, total_rows)
    scale_factor = HEAD_WIDTH_SIZE ** (-0.5)

    def back_one_block(carried, block_index):
        offset_row = block_index * block_rows
        key_block = lax.dynamic_slice_in_dim(all_keys, offset_row, block_rows, 0).reshape(
            block_rows, HEADS, HEAD_WIDTH_SIZE
        )
        value_block = lax.dynamic_slice_in_dim(all_values, offset_row, block_rows, 0).reshape(
            block_rows, HEADS, HEAD_WIDTH_SIZE
        )
        key_pos = place_rows(
            offset_row + jnp.arange(block_rows, dtype=jnp.int32), shard_rows, dev_count
        )
        key_seg = jnp.take(segment_all, key_pos)
        allowed = key_mask(query_pos, query_seg, key_pos, key_seg)
        scores = jnp.where(allowed[None], head_scores(queries, key_block), masked_score)
        prob_block = jnp.exp(scores - log_total[:, :, None])
        grad_prob = jnp.einsum(
            "qhd,khd->hqk", grad_heads, value_block, preferred_element_type=jnp.float32
        )
        grad_scores = (prob_block * (grad_prob - row_delta[:, :, None])).astype(jnp.bfloat16)
        query_grad = (
            carried
            + jnp.einsum("hqk,khd->qhd", grad_scores, key_block, preferred_element_type=jnp.float32)
            * scale_factor
        )
        key_grad = (
            jnp.einsum("hqk,qhd->khd", grad_scores, queries, preferred_element_type=jnp.float32)
            * scale_factor
        )
        value_grad = jnp.einsum(
            "hqk,qhd->khd",
            prob_block.astype(jnp.bfloat16),
            grad_heads,
            preferred_element_type=jnp.float32,
        )
        return (query_grad, (key_grad, value_grad))

    grad_query, (key_grads, value_grads) = lax.scan(
        back_one_block, grad_query, jnp.arange(total_rows // block_rows, dtype=jnp.int32)
    )
    return (
        grad_query,
        key_grads.reshape(total_rows, HEADS, HEAD_WIDTH_SIZE),
        value_grads.reshape(total_rows, HEADS, HEAD_WIDTH_SIZE),
    )


def group_step(stacked_rows, group_key_rows, group_value_rows, alpha_row, learning_rate_row):
    current_memory = stacked_rows[:, :HEAD_WIDTH_SIZE]
    moment_now = stacked_rows[:, HEAD_WIDTH_SIZE:]
    gram_matrix = (
        jnp.einsum("thk,thj->hkj", group_key_rows, group_key_rows, precision=highest_precision)
        * learning_rate_row[:, None, None]
    )
    mixed_product = (
        jnp.einsum("qgw,qgc->gwc", group_key_rows, group_value_rows, precision=highest_precision)
        * learning_rate_row[:, None, None]
    )
    memory_gradient = (
        jnp.einsum("fld,fdi->fli", gram_matrix, current_memory, precision=highest_precision)
        - mixed_product
    )
    moment_next = momentum * moment_now - memory_gradient
    memory_next = (1.0 - alpha_row)[:, None, None] * current_memory + moment_next
    return jnp.concatenate([memory_next, moment_next], axis=1)


def run_block(stacked_rows, query_part, key_part, value_part, alphas, thetas):
    scale_factor = HEAD_WIDTH_SIZE ** (-0.5)
    group_query_rows = query_part * scale_factor
    recalled_rows = [
        jnp.einsum(
            "ipb,pbx->ipx",
            group_query_rows,
            stacked_rows[:, :HEAD_WIDTH_SIZE],
            precision=highest_precision,
        )
    ]
    stacked_rows = group_step(
        stacked_rows, key_part * scale_factor, value_part, alphas[0], thetas[0]
    )
    return (jnp.concatenate(recalled_rows, axis=0), stacked_rows)


def states_before(key_order, value_order, alpha_all, theta_all, early_index, late_index):
    groups = alpha_all.shape[0]
    scale_factor = HEAD_WIDTH_SIZE ** (-0.5)
    key_groups = key_order.reshape(groups, GROUP, HEADS, HEAD_WIDTH_SIZE)
    value_groups = value_order.reshape(groups, GROUP, HEADS, HEAD_WIDTH_SIZE)
    zero_state = jnp.zeros((HEADS, 2 * HEAD_WIDTH_SIZE, HEAD_WIDTH_SIZE), jnp.float32)

    def states_one_group(carried, inputs):
        stacked_rows, into_early, into_late = carried
        group_key_rows, group_value_rows, alpha_row, learning_rate_row, group_index = inputs
        into_early = jnp.where(group_index == early_index, stacked_rows, into_early)
        into_late = jnp.where(group_index == late_index, stacked_rows, into_late)
        current_memory = stacked_rows[:, :HEAD_WIDTH_SIZE]
        moment_now = stacked_rows[:, HEAD_WIDTH_SIZE:]
        gram_matrix = (
            jnp.einsum(
                "thk,thj->hkj", group_key_rows, group_key_rows, preferred_element_type=jnp.float32
            )
            * (learning_rate_row / HEAD_WIDTH_SIZE)[:, None, None]
        )
        mixed_product = (
            jnp.einsum(
                "qgw,qgc->gwc", group_key_rows, group_value_rows, preferred_element_type=jnp.float32
            )
            * (learning_rate_row * scale_factor)[:, None, None]
        )
        memory_gradient = (
            jnp.einsum("fld,fdi->fli", gram_matrix, current_memory, precision=highest_precision)
            - mixed_product
        )
        moment_next = momentum * moment_now - memory_gradient
        memory_next = (1.0 - alpha_row)[:, None, None] * current_memory + moment_next
        stacked_rows = jnp.concatenate([memory_next, moment_next], axis=1)
        return ((stacked_rows, into_early, into_late), None)

    (_, into_early, into_late), _ = lax.scan(
        states_one_group,
        (zero_state, zero_state, zero_state),
        (key_groups, value_groups, alpha_all, theta_all, jnp.arange(groups, dtype=jnp.int32)),
    )
    return (into_early, into_late)


def adjoints_after(
    query_order, key_order, recall_grad_order, alpha_all, theta_all, early_end, late_end
):
    groups = alpha_all.shape[0]
    scale_factor = HEAD_WIDTH_SIZE ** (-0.5)
    query_groups = query_order.reshape(groups, GROUP, HEADS, HEAD_WIDTH_SIZE)
    key_groups = key_order.reshape(groups, GROUP, HEADS, HEAD_WIDTH_SIZE)
    grad_groups = recall_grad_order.reshape(groups, GROUP, HEADS, HEAD_WIDTH_SIZE)
    zero_state = jnp.zeros((HEADS, 2 * HEAD_WIDTH_SIZE, HEAD_WIDTH_SIZE), jnp.float32)

    def adjoints_one_group(carried, inputs):
        adjoint, out_early, out_late = carried
        (
            group_query_rows,
            group_key_rows,
            gradient_group_rows,
            alpha_row,
            learning_rate_row,
            group_index,
        ) = inputs
        out_early = jnp.where(group_index + 1 == early_end, adjoint, out_early)
        out_late = jnp.where(group_index + 1 == late_end, adjoint, out_late)
        gram_matrix = (
            jnp.einsum(
                "thk,thj->hkj", group_key_rows, group_key_rows, preferred_element_type=jnp.float32
            )
            * (learning_rate_row / HEAD_WIDTH_SIZE)[:, None, None]
        )
        query_term = (
            jnp.einsum(
                "qgw,qgc->gwc",
                group_query_rows,
                gradient_group_rows,
                preferred_element_type=jnp.float32,
            )
            * scale_factor
        )
        grad_m = adjoint[:, :HEAD_WIDTH_SIZE]
        summed_rows = grad_m + adjoint[:, HEAD_WIDTH_SIZE:]
        new_m = (
            (1.0 - alpha_row)[:, None, None] * grad_m
            + query_term
            - jnp.einsum("fld,fdi->fli", gram_matrix, summed_rows, precision=highest_precision)
        )
        adjoint = jnp.concatenate([new_m, momentum * summed_rows], axis=1)
        return ((adjoint, out_early, out_late), None)

    (_, out_early, out_late), _ = lax.scan(
        adjoints_one_group,
        (zero_state, zero_state, zero_state),
        (
            query_groups,
            key_groups,
            grad_groups,
            alpha_all,
            theta_all,
            jnp.arange(groups, dtype=jnp.int32),
        ),
        reverse=True,
    )
    return (out_early, out_late)


def on_device(
    tokens,
    cotangent,
    segments,
    decay_index,
    step_index,
    w_qkv,
    w_gate,
    w_out,
    w_gu,
    w_down,
    persist_keys,
    persist_values,
    norm_gain,
    ffn_gain,
):
    shard_rows = tokens.shape[1]
    model_width = tokens.shape[2]
    half_rows = shard_rows // 2
    dev_count = lax.axis_size("ctx")
    device = lax.axis_index("ctx")
    scale_factor = HEAD_WIDTH_SIZE ** (-0.5)
    full_weights = (
        lax.all_gather(w_qkv, "fsdp", axis=0, tiled=True),
        lax.all_gather(w_gate, "fsdp", axis=0, tiled=True),
        lax.all_gather(w_out, "fsdp", axis=0, tiled=True),
        lax.all_gather(w_gu, "fsdp", axis=0, tiled=True),
        lax.all_gather(w_down, "fsdp", axis=0, tiled=True),
        lax.all_gather(persist_keys, "fsdp", axis=0, tiled=True),
        lax.all_gather(persist_values, "fsdp", axis=0, tiled=True),
        lax.all_gather(norm_gain, "fsdp", axis=0, tiled=True),
        lax.all_gather(ffn_gain, "fsdp", axis=0, tiled=True),
    )
    wq_full, wg_full, wo_full, wgu_full, wd_full, pkeys_full, pvalues_full, gain_attn, gain_ffn = (
        full_weights
    )
    gain_attn32 = gain_attn.astype(jnp.float32)
    gain_ffn32 = gain_ffn.astype(jnp.float32)
    pkeys_heads = pkeys_full.reshape(-1, HEADS, HEAD_WIDTH_SIZE)
    pvalues_heads = pvalues_full.reshape(-1, HEADS, HEAD_WIDTH_SIZE)
    inputs32 = tokens[0].astype(jnp.float32)
    inv_rms_one = rms_scale(inputs32)
    normed_low = (inputs32 * inv_rms_one * gain_attn32).astype(jnp.bfloat16)
    projected = jnp.dot(normed_low, wq_full, preferred_element_type=jnp.float32)
    query_flat = projected[:, :model_width].astype(jnp.bfloat16)
    key_flat = projected[:, model_width : 2 * model_width].astype(jnp.bfloat16)
    value_flat = projected[:, 2 * model_width :].astype(jnp.bfloat16)
    query_heads = query_flat.reshape(shard_rows, HEADS, HEAD_WIDTH_SIZE)
    gate_open = jax.nn.sigmoid(jnp.dot(normed_low, wg_full, preferred_element_type=jnp.float32))
    local_rows = jnp.arange(shard_rows, dtype=jnp.int32)
    query_pos = place_rows(device * shard_rows + local_rows, shard_rows, dev_count)
    segment_all = segments[0]
    query_seg = jnp.take(segment_all, query_pos)
    context = (query_heads, query_pos, query_seg, segment_all, shard_rows, dev_count)
    all_keys, all_values = (
        lax.all_gather(key_flat, "ctx", axis=0, tiled=True),
        lax.all_gather(value_flat, "ctx", axis=0, tiled=True),
    )
    persist_scores = head_scores(query_heads, pkeys_heads)
    start_state = (
        jnp.full((HEADS, shard_rows), masked_score, jnp.float32),
        jnp.zeros((HEADS, shard_rows), jnp.float32),
        jnp.zeros((shard_rows, HEADS, HEAD_WIDTH_SIZE), jnp.float32),
    )
    running = online_step(start_state, persist_scores, pvalues_heads)
    running = fold_keys(running, all_keys, all_values, context)
    run_max, run_total, accumulated = running
    attended = accumulated / jnp.transpose(run_total)[:, :, None]
    log_total = run_max + jnp.log(run_total)
    group_count = half_rows // GROUP
    alpha_all = 0.6 * jnp.exp2(-decay_index[0].astype(jnp.float32))
    theta_all = 0.1 * jnp.exp2(-step_index[0].astype(jnp.float32))
    early_first = device * group_count
    late_first = (2 * dev_count - 1 - device) * group_count
    alpha_early = lax.dynamic_slice_in_dim(alpha_all, early_first, group_count, 0)
    theta_early = lax.dynamic_slice_in_dim(theta_all, early_first, group_count, 0)
    alpha_late = lax.dynamic_slice_in_dim(alpha_all, late_first, group_count, 0)
    theta_late = lax.dynamic_slice_in_dim(theta_all, late_first, group_count, 0)
    query_f = query_heads.astype(jnp.float32)
    key_f = key_flat.astype(jnp.float32).reshape(shard_rows, HEADS, HEAD_WIDTH_SIZE)
    value_f = value_flat.astype(jnp.float32).reshape(shard_rows, HEADS, HEAD_WIDTH_SIZE)
    early_parts = (query_f[:half_rows], key_f[:half_rows], value_f[:half_rows])
    late_parts = (query_f[half_rows:], key_f[half_rows:], value_f[half_rows:])

    def early_run(stacked_rows, query_part, key_part, value_part):
        return run_block(stacked_rows, query_part, key_part, value_part, alpha_early, theta_early)

    def late_run(stacked_rows, query_part, key_part, value_part):
        return run_block(stacked_rows, query_part, key_part, value_part, alpha_late, theta_late)

    into_early, into_late = states_before(
        position_order(all_keys, dev_count),
        position_order(all_values, dev_count),
        alpha_all,
        theta_all,
        early_first,
        late_first,
    )
    recall_early, _ = early_run(into_early, early_parts[0], early_parts[1], early_parts[2])
    recall_late, _ = late_run(into_late, late_parts[0], late_parts[1], late_parts[2])
    recall = jnp.concatenate([recall_early, recall_late], axis=0).reshape(shard_rows, model_width)
    mixed_low = (attended.reshape(shard_rows, model_width) + gate_open * recall).astype(
        jnp.bfloat16
    )
    residual = inputs32 + jnp.dot(mixed_low, wo_full, preferred_element_type=jnp.float32)
    inv_rms_two = rms_scale(residual)
    normed_two = (residual * inv_rms_two * gain_ffn32).astype(jnp.bfloat16)
    gate_up = jnp.dot(normed_two, wgu_full, preferred_element_type=jnp.float32)
    gate_part = gate_up[:, :FF]
    up_part = gate_up[:, FF:]
    active = (jax.nn.silu(gate_part) * up_part).astype(jnp.bfloat16)
    result = residual + jnp.dot(active, wd_full, preferred_element_type=jnp.float32)
    cot_low = cotangent[0]
    grad_w_down = jnp.einsum("tf,td->fd", active, cot_low, preferred_element_type=jnp.float32)
    grad_active = jnp.einsum("td,fd->tf", cot_low, wd_full, preferred_element_type=jnp.float32)
    sigma_gate = jax.nn.sigmoid(gate_part)
    grad_gate_part = grad_active * up_part * sigma_gate * (1.0 + gate_part * (1.0 - sigma_gate))
    grad_up_part = grad_active * gate_part * sigma_gate
    grad_gu_low = jnp.concatenate([grad_gate_part, grad_up_part], axis=1).astype(jnp.bfloat16)
    grad_w_gu = jnp.einsum("td,tf->df", normed_two, grad_gu_low, preferred_element_type=jnp.float32)
    grad_normed_two = jnp.einsum(
        "tf,df->td", grad_gu_low, wgu_full, preferred_element_type=jnp.float32
    )
    grad_res_norm, grad_ffn_gain = norm_back(residual, inv_rms_two, gain_ffn32, grad_normed_two)
    grad_residual = cot_low.astype(jnp.float32) + grad_res_norm
    grad_branch = grad_residual.astype(jnp.bfloat16)
    grad_w_out = jnp.einsum("td,te->de", mixed_low, grad_branch, preferred_element_type=jnp.float32)
    grad_mixed_low = jnp.einsum(
        "te,de->td", grad_branch, wo_full, preferred_element_type=jnp.float32
    ).astype(jnp.bfloat16)
    grad_mixed32 = grad_mixed_low.astype(jnp.float32)
    grad_gate_low = (grad_mixed32 * recall * gate_open * (1.0 - gate_open)).astype(jnp.bfloat16)
    grad_w_gate = jnp.einsum(
        "td,tf->df", normed_low, grad_gate_low, preferred_element_type=jnp.float32
    )
    recall_grad_low = (grad_mixed32 * gate_open).astype(jnp.bfloat16)
    grad_recall = recall_grad_low.astype(jnp.float32).reshape(shard_rows, HEADS, HEAD_WIDTH_SIZE)
    grad_heads = grad_mixed_low.reshape(shard_rows, HEADS, HEAD_WIDTH_SIZE)
    row_delta = jnp.transpose(jnp.sum(grad_heads.astype(jnp.float32) * attended, axis=-1))
    memory_queries, all_recall_grads = (
        lax.all_gather(query_flat, "ctx", axis=0, tiled=True),
        lax.all_gather(recall_grad_low, "ctx", axis=0, tiled=True),
    )
    out_early, out_late = adjoints_after(
        position_order(memory_queries, dev_count),
        position_order(all_keys, dev_count),
        position_order(all_recall_grads, dev_count),
        alpha_all,
        theta_all,
        early_first + group_count,
        late_first + group_count,
    )
    _, pull_early = jax.vjp(early_run, into_early, early_parts[0], early_parts[1], early_parts[2])
    _, grad_qe, grad_ke, grad_ve = pull_early((grad_recall[:half_rows], out_early))
    _, pull_late = jax.vjp(late_run, into_late, late_parts[0], late_parts[1], late_parts[2])
    _, grad_ql, grad_kl, grad_vl = pull_late((grad_recall[half_rows:], out_late))
    grad_q_mem = jnp.concatenate([grad_qe, grad_ql], axis=0).reshape(shard_rows, model_width)
    grad_k_mem = jnp.concatenate([grad_ke, grad_kl], axis=0).reshape(shard_rows, model_width)
    grad_v_mem = jnp.concatenate([grad_ve, grad_vl], axis=0).reshape(shard_rows, model_width)
    persist_probs = jnp.exp(persist_scores - log_total[:, :, None])
    persist_grad_prob = jnp.einsum(
        "qhd,phd->hqp", grad_heads, pvalues_heads, preferred_element_type=jnp.float32
    )
    persist_ds = (persist_probs * (persist_grad_prob - row_delta[:, :, None])).astype(jnp.bfloat16)
    grad_query_att = (
        jnp.einsum("hqp,phd->qhd", persist_ds, pkeys_heads, preferred_element_type=jnp.float32)
        * scale_factor
    )
    grad_pkeys = (
        jnp.einsum("hqp,qhd->phd", persist_ds, query_heads, preferred_element_type=jnp.float32)
        * scale_factor
    )
    grad_pvalues = jnp.einsum(
        "hqp,qhd->phd",
        persist_probs.astype(jnp.bfloat16),
        grad_heads,
        preferred_element_type=jnp.float32,
    )
    grad_query_att, key_grads_all, value_grads_all = back_every_key(
        grad_query_att, all_keys, all_values, context, grad_heads, log_total, row_delta
    )
    key_grad_att, value_grad_att = (
        lax.psum_scatter(key_grads_all, "ctx", scatter_dimension=0, tiled=True),
        lax.psum_scatter(value_grads_all, "ctx", scatter_dimension=0, tiled=True),
    )
    grad_query = grad_query_att.reshape(shard_rows, model_width) + grad_q_mem
    grad_key = key_grad_att.reshape(shard_rows, model_width) + grad_k_mem
    grad_value = value_grad_att.reshape(shard_rows, model_width) + grad_v_mem
    grad_qkv_low = jnp.concatenate([grad_query, grad_key, grad_value], axis=1).astype(jnp.bfloat16)
    grad_w_qkv = jnp.einsum(
        "td,tf->df", normed_low, grad_qkv_low, preferred_element_type=jnp.float32
    )
    grad_normed = jnp.einsum(
        "tf,df->td", grad_qkv_low, wq_full, preferred_element_type=jnp.float32
    ) + jnp.einsum("tf,df->td", grad_gate_low, wg_full, preferred_element_type=jnp.float32)
    grad_in_norm, grad_norm_gain = norm_back(inputs32, inv_rms_one, gain_attn32, grad_normed)
    grad_inputs = grad_residual + grad_in_norm
    local_grads = (
        grad_w_qkv,
        grad_w_gate,
        grad_w_out,
        grad_w_gu,
        grad_w_down,
        grad_pkeys.reshape(-1, model_width),
        grad_pvalues.reshape(-1, model_width),
        grad_norm_gain,
        grad_ffn_gain,
    )
    shares = (
        lax.psum_scatter(
            local_grads[0].astype(jnp.bfloat16), "fsdp", scatter_dimension=0, tiled=True
        ).astype(jnp.float32),
        lax.psum_scatter(
            local_grads[1].astype(jnp.bfloat16), "fsdp", scatter_dimension=0, tiled=True
        ).astype(jnp.float32),
        lax.psum_scatter(
            local_grads[2].astype(jnp.bfloat16), "fsdp", scatter_dimension=0, tiled=True
        ).astype(jnp.float32),
        lax.psum_scatter(
            local_grads[3].astype(jnp.bfloat16), "fsdp", scatter_dimension=0, tiled=True
        ).astype(jnp.float32),
        lax.psum_scatter(
            local_grads[4].astype(jnp.bfloat16), "fsdp", scatter_dimension=0, tiled=True
        ).astype(jnp.float32),
        lax.psum_scatter(
            local_grads[5].astype(jnp.bfloat16), "fsdp", scatter_dimension=0, tiled=True
        ).astype(jnp.float32),
        lax.psum_scatter(
            local_grads[6].astype(jnp.bfloat16), "fsdp", scatter_dimension=0, tiled=True
        ).astype(jnp.float32),
        lax.psum_scatter(
            local_grads[7].astype(jnp.bfloat16), "fsdp", scatter_dimension=0, tiled=True
        ).astype(jnp.float32),
        lax.psum_scatter(
            local_grads[8].astype(jnp.bfloat16), "fsdp", scatter_dimension=0, tiled=True
        ).astype(jnp.float32),
    )
    totals = lax.psum(
        (
            shares[0],
            shares[1],
            shares[2],
            shares[3],
            shares[4],
            shares[5],
            shares[6],
            shares[7],
            shares[8],
        ),
        "ctx",
    )
    return (
        result.astype(jnp.bfloat16)[None],
        grad_inputs[None],
        totals[0],
        totals[1],
        totals[2],
        totals[3],
        totals[4],
        totals[5],
        totals[6],
        totals[7],
        totals[8],
    )


PERSIST = 16
PLANES = 4
HIDDEN_PAD = 384
Z_HIDDEN = HIDDEN_PAD // PLANES
VMEM_BYTES = 56 * 1024 * 1024


def head_of(x, f, k):
    return 2 * (f ^ (k & 3)) + (x ^ (k >> 2))


def linear(z, x, f):
    return (2 * z + x) * 4 + f


def shift(value, move):
    pairs = []
    for z in range(4):
        for x in range(2):
            for f in range(4):
                pairs.append((linear(z, x, f), linear(*move(z, x, f))))
    return lax.ppermute(value, ("ctx", "fsdp"), pairs)


def to_plane(value):
    return shift(value, lambda z, x, f: (f, x, z))


def flip(value, dx, df):
    return shift(value, lambda z, x, f: (z, x ^ dx, f ^ df))


def flip_z(value, dz):
    return shift(value, lambda z, x, f: (z ^ dz, x, f))


def gather_plane(block):
    near = [block, flip(block, 0, 2), flip(block, 1, 0), flip(block, 1, 2)]
    far = [flip(b, 0, 1) for b in near]
    return [near[0], far[0], near[1], far[1], near[2], far[2], near[3], far[3]]


def dot_nn(a, b):
    return lax.dot_general(a, b, (((1,), (0,)), ((), ())), preferred_element_type=jnp.float32)


def dot_nt(a, b):
    return lax.dot_general(a, b, (((1,), (1,)), ((), ())), preferred_element_type=jnp.float32)


def dot_tn(a, b):
    return lax.dot_general(a, b, (((0,), (0,)), ((), ())), preferred_element_type=jnp.float32)


def split_two(value):
    high = value.astype(jnp.bfloat16)
    return high, (value - high.astype(jnp.float32)).astype(jnp.bfloat16)


def product_three(a, b_high, b_low):
    a_high, a_low = split_two(a)
    return dot_nn(a_high, b_high) + dot_nn(a_low, b_high) + dot_nn(a_high, b_low)


def vspec():
    return pl.BlockSpec(memory_space=pltpu.VMEM)


def sspec():
    return pl.BlockSpec(memory_space=pltpu.SMEM)


def call(kernel, smem, operands, outs, scratch=(), flops=0, name=None):
    moved = sum(o.size * o.dtype.itemsize for o in operands) + sum(
        int(np.prod(s)) * jnp.dtype(d).itemsize for s, d in outs
    )
    return pl.pallas_call(
        kernel,
        out_shape=[jax.ShapeDtypeStruct(s, d) for s, d in outs],
        in_specs=[sspec()] * len(smem) + [vspec()] * len(operands),
        out_specs=[vspec()] * len(outs),
        scratch_shapes=[pltpu.VMEM(s, d) for s, d in scratch],
        compiler_params=pltpu.CompilerParams(vmem_limit_bytes=VMEM_BYTES),
        cost_estimate=pl.CostEstimate(flops=flops, bytes_accessed=moved, transcendentals=0),
        name=name,
    )(*smem, *operands)


def pack_qkvg_kernel(idx, wq, wg, o0, o1, o2, o3):
    x, f = idx[1], idx[2]
    for j, out in enumerate((o0, o1, o2, o3)):
        head = 2 * (f ^ j) + x
        start = pl.multiple_of(head * 128, 128)
        for part in range(3):
            out[:, part * 128 : part * 128 + 128] = wq[
                :, pl.ds(pl.multiple_of(part * 1024 + start, 128), 128)
            ]
        out[:, 384:512] = wg[:, pl.ds(start, 128)]


def pack_gu_kernel(idx, wgu, o0, o1, o2, o3):
    x, f = idx[1], idx[2]
    width = FF // 8
    pad = jnp.zeros((wgu.shape[0], HIDDEN_PAD - width), jnp.bfloat16)
    for j, out in enumerate((o0, o1, o2, o3)):
        head = 2 * (f ^ j) + x
        for h in range(8):

            @pl.when(head == h)
            def _():
                for part in range(2):
                    first = part * FF + h * width
                    at = part * HIDDEN_PAD
                    out[:, at : at + HIDDEN_PAD] = jnp.concatenate(
                        [wgu[:, first : first + width], pad], axis=1
                    )


def mixer_forward_kernel(idx, rates, ints, *refs):
    blocks = refs[0:8]
    parts = refs[8:12]
    gain, wo, pk, pv = refs[12:16]
    send, keep, normed, w_full, qkv, gate, att, rec, probs, pprobs, states, mixed = refs[16:28]
    x, f = idx[1], idx[2]
    head = 2 * f + x
    scale = HEAD_WIDTH_SIZE ** (-0.5)
    gain_row = gain[...]
    for j in range(4):
        w_full[pl.ds(pl.multiple_of((f ^ j) * 256, 256), 256), :] = parts[j][...]
    for k in range(8):
        values = blocks[k][...].astype(jnp.float32)
        normed_block = (values * rms_scale(values) * gain_row).astype(jnp.bfloat16)
        hk = head_of(x, f, k)
        normed[pl.ds(pl.multiple_of(hk * 64, 64), 64), :] = normed_block[:64]
        normed[pl.ds(pl.multiple_of((15 - hk) * 64, 64), 64), :] = normed_block[64:]
    for t in range(4):
        rows = slice(t * 256, t * 256 + 256)
        product = dot_nn(normed[rows, :], w_full[...])
        qkv[rows, :] = product[:, :384].astype(jnp.bfloat16)
        gate[rows, :] = jax.nn.sigmoid(product[:, 384:])
    state = jnp.zeros((128, 128), jnp.float32)
    moment = jnp.zeros((128, 128), jnp.float32)
    for t in range(8):
        rows = slice(t * 128, t * 128 + 128)
        width = (t + 1) * 128
        query = qkv[rows, 0:128]
        scores = dot_nt(query, qkv[0:width, 128:256]) * scale
        row_seg = jnp.transpose(jnp.broadcast_to(ints[t : t + 1, :], (128, 128)))[:, 0:1]
        col_seg = jnp.concatenate([ints[u : u + 1, :] for u in range(t + 1)], axis=1)
        row_pos = lax.broadcasted_iota(jnp.int32, (128, width), 0) + t * 128
        col_pos = lax.broadcasted_iota(jnp.int32, (128, width), 1)
        allowed = (row_seg == col_seg) & (col_pos <= row_pos)
        scores = jnp.where(allowed, scores, masked_score)
        pscores = dot_nt(query, pk[...]) * scale
        top = jnp.maximum(
            jnp.max(scores, axis=-1, keepdims=True), jnp.max(pscores, axis=-1, keepdims=True)
        )
        weights = jnp.exp(scores - top)
        pweights = jnp.exp(pscores - top)
        inverse = 1.0 / (
            jnp.sum(weights, axis=-1, keepdims=True) + jnp.sum(pweights, axis=-1, keepdims=True)
        )
        weights = (weights * inverse).astype(jnp.bfloat16)
        pweights = (pweights * inverse).astype(jnp.bfloat16)
        probs[rows, 0:width] = weights
        pprobs[rows, :] = pweights
        att[rows, :] = dot_nn(weights, qkv[0:width, 256:384]) + dot_nn(pweights, pv[...])
        for c in (2 * t, 2 * t + 1):
            grows = slice(c * 64, c * 64 + 64)
            alpha = rates[0, c * 8 + head]
            theta = rates[1, c * 8 + head]
            high, low = split_two(state)
            states[c] = high
            recalled = dot_nt(qkv[grows, 0:128], high) + dot_nt(qkv[grows, 0:128], low)
            rec[grows, :] = recalled * scale
            both = dot_tn(qkv[grows, 128:384], qkv[grows, 128:256])
            gram_high, gram_low = split_two(both[:128] * (theta / HEAD_WIDTH_SIZE))
            change = (
                dot_nn(high, gram_high) + dot_nn(low, gram_high) + dot_nn(high, gram_low)
            ) - both[128:] * (theta * scale)
            moment = momentum * moment - change
            state = (1.0 - alpha) * state + moment
        mixed[rows, :] = (att[rows, :] + gate[rows, :] * rec[rows, :]).astype(jnp.bfloat16)
    for k in range(8):
        hk = head_of(x, f, k)
        piece = jnp.concatenate(
            [
                mixed[pl.ds(pl.multiple_of(hk * 64, 64), 64), :],
                mixed[pl.ds(pl.multiple_of((15 - hk) * 64, 64), 64), :],
            ],
            axis=0,
        )
        out = send if k & 1 else keep
        out[k >> 1] = dot_nn(piece, wo[...]).astype(jnp.bfloat16)


def mixer_backward_kernel(idx, rates, *refs):
    blocks = refs[0:8]
    wo, w_full, qkv, gate, att, rec, probs, pprobs, states, pk, pv = refs[8:19]
    send, keep, dqkvg, branch, gpk, gpv = refs[19:25]
    gm, dy, delta, ds, dk, dv, dsp = refs[25:32]
    x, f = idx[1], idx[2]
    head = 2 * f + x
    scale = HEAD_WIDTH_SIZE ** (-0.5)
    for k in range(8):
        hk = head_of(x, f, k)
        early = pl.ds(pl.multiple_of(hk * 64, 64), 64)
        late = pl.ds(pl.multiple_of((15 - hk) * 64, 64), 64)
        block = blocks[k][...]
        grad = dot_nt(block, wo[...]).astype(jnp.bfloat16)
        gm[early, :] = grad[:64]
        gm[late, :] = grad[64:]
        branch[early, :] = block[:64]
        branch[late, :] = block[64:]
    for t in range(8):
        rows = slice(t * 128, t * 128 + 128)
        width = (t + 1) * 128
        grad_low = gm[rows, :]
        grad = grad_low.astype(jnp.float32)
        opened = gate[rows, :]
        dqkvg[rows, 384:512] = (grad * rec[rows, :] * opened * (1.0 - opened)).astype(jnp.bfloat16)
        dy[rows, :] = (grad * opened).astype(jnp.bfloat16)
        row_delta = jnp.sum(grad * att[rows, :], axis=-1, keepdims=True)
        grad_probs = dot_nt(grad_low, qkv[0:width, 256:384])
        ds_tile = (probs[rows, 0:width].astype(jnp.float32) * (grad_probs - row_delta)).astype(
            jnp.bfloat16
        )
        ds[rows, 0:width] = ds_tile
        grad_pprobs = dot_nt(grad_low, pv[...])
        dsp_tile = (pprobs[rows, :].astype(jnp.float32) * (grad_pprobs - row_delta)).astype(
            jnp.bfloat16
        )
        dsp[rows, :] = dsp_tile
        delta[rows, :] = (
            dot_nn(ds_tile, qkv[0:width, 128:256]) + dot_nn(dsp_tile, pk[...])
        ) * scale
    gpk[...] = dot_tn(dsp[...], qkv[:, 0:128]) * scale
    gpv[...] = dot_tn(pprobs[...], gm[...])
    grad_state = jnp.zeros((128, 128), jnp.float32)
    grad_moment = jnp.zeros((128, 128), jnp.float32)
    for t in range(7, -1, -1):
        rows = slice(t * 128, t * 128 + 128)
        rest = slice(t * 128, 1024)
        dk[rows, :] = dot_tn(ds[rest, rows], qkv[rest, 0:128]) * scale
        dv[rows, :] = dot_tn(probs[rest, rows], gm[rest, :])
        for c in (2 * t + 1, 2 * t):
            grows = slice(c * 64, c * 64 + 64)
            alpha = rates[0, c * 8 + head]
            theta = rates[1, c * 8 + head]
            query, key, value = qkv[grows, 0:128], qkv[grows, 128:256], qkv[grows, 256:384]
            dy_rows = dy[grows, :]
            state = states[c]
            summed = grad_state + grad_moment
            high, low = split_two(summed)
            key_summed = dot_nt(key, high) * scale
            error = value.astype(jnp.float32) - dot_nt(key, state) * scale
            grad_value = dv[grows, :] + theta * key_summed
            grad_key = dk[grows, :] + (theta * scale) * (
                dot_nn(error.astype(jnp.bfloat16), high)
                - dot_nn(key_summed.astype(jnp.bfloat16), state)
            )
            grad_query = delta[grows, :] + dot_nn(dy_rows, state) * scale
            dqkvg[grows, 0:128] = grad_query.astype(jnp.bfloat16)
            dqkvg[grows, 128:256] = grad_key.astype(jnp.bfloat16)
            dqkvg[grows, 256:384] = grad_value.astype(jnp.bfloat16)
            gram_high, gram_low = split_two(dot_tn(key, key) * (theta / HEAD_WIDTH_SIZE))
            product = dot_nn(high, gram_high) + dot_nn(low, gram_high) + dot_nn(high, gram_low)
            grad_state = (
                dot_tn(dy_rows, query) * scale + (1.0 - alpha) * grad_state - product
            )
            grad_moment = momentum * summed
    for k in range(8):
        hk = head_of(x, f, k)
        piece = jnp.concatenate(
            [
                dqkvg[pl.ds(pl.multiple_of(hk * 64, 64), 64), :],
                dqkvg[pl.ds(pl.multiple_of((15 - hk) * 64, 64), 64), :],
            ],
            axis=0,
        )
        out = send if k & 1 else keep
        out[k >> 1] = dot_nt(piece, w_full[...]).astype(jnp.bfloat16)


def mixer_weights_kernel(idx, normed, dqkvg, mixed, branch, *refs):
    outs, outs_o = refs[0:4], refs[4:8]
    total, total_o = refs[8:10]
    z, f = idx[0], idx[2]
    for t in range(4):
        total[...] = dot_tn(normed[:, t * 256 : t * 256 + 256], dqkvg[...])
        for j in range(4):
            outs[j][t ^ f] = total[pl.ds(pl.multiple_of((z ^ j) * 64, 64), 64), :].astype(
                jnp.bfloat16
            )
    total_o[...] = dot_tn(mixed[...], branch[...])
    for j in range(4):
        outs_o[j][...] = total_o[pl.ds(pl.multiple_of((z ^ j) * 32, 32), 32), :].astype(
            jnp.bfloat16
        )


def feed_kernel(idx, *refs):
    blocks, cots, parts = refs[0:8], refs[8:16], refs[16:20]
    wd = refs[20]
    send_g, keep_g, send_d, keep_d, active, dgu, feeds, cot_all = refs[21:29]
    w_full = refs[29]
    f = idx[2]
    for j in range(4):
        w_full[pl.ds(pl.multiple_of((f ^ j) * 256, 256), 256), :] = parts[j][...]
    for k in range(4):
        rows = slice(k * 256, k * 256 + 256)
        feed = jnp.concatenate([blocks[2 * k][...], blocks[2 * k + 1][...]], axis=0)
        cot = jnp.concatenate([cots[2 * k][...], cots[2 * k + 1][...]], axis=0)
        feeds[rows, :] = feed
        cot_all[rows, :] = cot
        gate_up = dot_nn(feed, w_full[...])
        g, u = gate_up[:, :HIDDEN_PAD], gate_up[:, HIDDEN_PAD:]
        sigma = jax.nn.sigmoid(g)
        active_low = (g * sigma * u).astype(jnp.bfloat16)
        active[rows, :] = active_low
        grad_active = dot_nt(cot, wd[...])
        grad_g = (grad_active * u * sigma * (1.0 + g * (1.0 - sigma))).astype(jnp.bfloat16)
        grad_u = (grad_active * g * sigma).astype(jnp.bfloat16)
        grad_low = jnp.concatenate([grad_g, grad_u], axis=1)
        dgu[rows, :] = grad_low
        grad_feed = dot_nt(grad_low, w_full[...]).astype(jnp.bfloat16)
        keep_g[k] = grad_feed[:128]
        send_g[k] = grad_feed[128:]
        down = dot_nn(active_low, wd[...]).astype(jnp.bfloat16)
        keep_d[k] = down[:128]
        send_d[k] = down[128:]


def feed_weights_kernel(idx, feeds, dgu, active, cots, *refs):
    outs, outs_d = refs[0:4], refs[4:8]
    total, total_d = refs[8:10]
    z, f = idx[0], idx[2]
    for t in range(4):
        total[...] = dot_tn(feeds[:, t * 256 : t * 256 + 256], dgu[...])
        for j in range(4):
            outs[j][t ^ f] = total[pl.ds(pl.multiple_of((z ^ j) * 64, 64), 64), :].astype(
                jnp.bfloat16
            )
    total_d[...] = dot_tn(active[...], cots[...])
    for j in range(4):
        first = pl.multiple_of((z ^ j) * Z_HIDDEN, 32)
        outs_d[j][...] = total_d[pl.ds(first, Z_HIDDEN), :].astype(jnp.bfloat16)


def add_kernel(keep, received, s0, s1, s2, s3):
    s0[...] = keep[0].astype(jnp.float32) + received[0].astype(jnp.float32)
    for k, out in ((1, s1), (2, s2), (3, s3)):
        out[...] = (keep[k].astype(jnp.float32) + received[k].astype(jnp.float32)).astype(
            jnp.bfloat16
        )


def total_of(refs):
    return (
        refs[0][...]
        + refs[1][...].astype(jnp.float32)
        + refs[2][...].astype(jnp.float32)
        + refs[3][...].astype(jnp.float32)
    )


def residual_kernel(x, gain, s0, r1, r2, r3, residual, feed):
    values = x[...].astype(jnp.float32) + total_of((s0, r1, r2, r3))
    residual[...] = values
    feed[...] = (values * rms_scale(values) * gain[...]).astype(jnp.bfloat16)


def norm_grad(values, gain, grad):
    inv = rms_scale(values)
    scaled = grad * gain
    return inv * scaled - values * (inv * inv * inv) * jnp.mean(
        scaled * values, axis=-1, keepdims=True
    )


def branch_kernel(residual, gain, cot, s0, r1, r2, r3, grad_residual, branch):
    grad = total_of((s0, r1, r2, r3))
    total = cot[...].astype(jnp.float32) + norm_grad(residual[...], gain[...], grad)
    grad_residual[...] = total
    branch[...] = total.astype(jnp.bfloat16)


def tokens_kernel(x, gain, grad_residual, s0, r1, r2, r3, out):
    grad = total_of((s0, r1, r2, r3))
    values = x[...].astype(jnp.float32)
    out[...] = (grad_residual[...] + norm_grad(values, gain[...], grad)).astype(jnp.bfloat16)


def output_kernel(residual, s0, r1, r2, r3, out):
    out[...] = (residual[...] + total_of((s0, r1, r2, r3))).astype(jnp.bfloat16)


def sum_parts_kernel(*refs):
    wide, rows, outs, out_rows = refs[0:4], refs[4:8], refs[8:12], refs[12]
    total = wide[0][...].astype(jnp.float32)
    for part in wide[1:]:
        total = total + part[...].astype(jnp.float32)
    for j in range(4):
        outs[j][...] = total[j].astype(jnp.bfloat16)
    total = rows[0][...].astype(jnp.float32)
    for part in rows[1:]:
        total = total + part[...].astype(jnp.float32)
    out_rows[...] = total.astype(jnp.bfloat16)


def join_kernel(*refs):
    parts, rows, out = refs[0:4], refs[4], refs[5]
    width = out.shape[1]
    for j in range(4):
        out[j * 64 : j * 64 + 64, :] = parts[j][...]
    count = rows.shape[0]
    out[256 : 256 + count, :] = rows[:, 0:width]
    left = 1024 - width
    if left == width:
        out[256 + count : 256 + 2 * count, :] = rows[:, width:1024]
    else:
        third = count * left // width
        for i in range(count // third):
            out[256 + count : 256 + count + third, i * left : (i + 1) * left] = rows[
                i * third : (i + 1) * third, width:1024
            ]


def row_sums(products, out):
    out[...] = jnp.sum(jnp.transpose(products), axis=0, keepdims=True)


def feed_unpack_kernel(idx, *refs):
    parts = refs[0:8]
    wgu, gain = refs[8:10]
    out_gu, out_down, out_gain = refs[10:13]
    z, x, f = idx[0], idx[1], idx[2]
    width = FF // 8
    for j in range(4):
        for dx in range(2):
            part = parts[2 * j + dx]
            zj, xj = z ^ j, x ^ dx
            rows = pl.ds(pl.multiple_of(zj * 64, 64), 64)
            for jf in range(4):
                head = 2 * (f ^ jf) + xj
                for h in range(8):

                    @pl.when(head == h)
                    def _():
                        for side in range(2):
                            first = side * FF + h * width
                            out_gu[rows, first : first + width] = part[
                                jf * 64 : jf * 64 + 64, side * HIDDEN_PAD : side * HIDDEN_PAD + width
                            ].astype(jnp.float32)

            lower = part[256:352, :].astype(jnp.float32)
            upper = part[352:384, :].astype(jnp.float32)
            valid = 64
            base = pl.multiple_of(xj * 352 + zj * Z_HIDDEN, 32)

            def put(first, count):
                at = pl.ds(pl.multiple_of(base + first, 32), count)
                out_down[at, 0:768] = lower[first : first + count]
                for i in range(first // 32, (first + count) // 32):
                    spot = pl.ds(pl.multiple_of(base + 32 * i, 32), 32)
                    out_down[spot, 768:1024] = upper[:, i * 256 : (i + 1) * 256]

            put(0, valid)

            @pl.when(zj < 3)
            def _():
                put(64, 32)

    sums = jnp.zeros((256, 128), jnp.float32)
    for t in range(2 * FF // 128):
        cols = slice(t * 128, t * 128 + 128)
        sums = sums + out_gu[:, cols] * wgu[:, cols].astype(jnp.float32)
    row_sums(sums, out_gain)
    out_gain[...] = out_gain[...] / gain[...].astype(jnp.float32)


def mixer_unpack_kernel(idx, *refs):
    parts = refs[0:8]
    wq, wg, gain = refs[8:11]
    out_qkv, out_gate, out_out, out_gain = refs[11:15]
    z, x, f = idx[0], idx[1], idx[2]
    for j in range(4):
        for dx in range(2):
            part = parts[2 * j + dx]
            zj, xj = z ^ j, x ^ dx
            rows = pl.ds(pl.multiple_of(zj * 64, 64), 64)
            for jf in range(4):
                head = 2 * (f ^ jf) + xj
                start = pl.multiple_of(head * 128, 128)
                for side in range(3):
                    out_qkv[rows, pl.ds(pl.multiple_of(side * 1024 + start, 128), 128)] = part[
                        jf * 64 : jf * 64 + 64, side * 128 : side * 128 + 128
                    ].astype(jnp.float32)
                out_gate[rows, pl.ds(start, 128)] = part[jf * 64 : jf * 64 + 64, 384:512].astype(
                    jnp.float32
                )
            spot = pl.ds(pl.multiple_of(xj * 128 + zj * 32, 32), 32)
            out_out[spot, 0:512] = part[256:288, :].astype(jnp.float32)
            out_out[spot, 512:1024] = part[288:320, :].astype(jnp.float32)
    sums = jnp.zeros((256, 128), jnp.float32)
    for t in range(24):
        cols = slice(t * 128, t * 128 + 128)
        sums = sums + out_qkv[:, cols] * wq[:, cols].astype(jnp.float32)
    for t in range(8):
        cols = slice(t * 128, t * 128 + 128)
        sums = sums + out_gate[:, cols] * wg[:, cols].astype(jnp.float32)
    row_sums(sums, out_gain)
    out_gain[...] = out_gain[...] / gain[...].astype(jnp.float32)


def scatter_plane(keep, send):
    received = flip(send, 0, 1)
    block = (128, 1024)
    s0, s1, s2, s3 = call(
        add_kernel,
        (),
        (keep, received),
        [(block, jnp.float32)] + [(block, jnp.bfloat16)] * 3,
        name="core_sum",
    )
    return s0, flip(s1, 0, 2), flip(s2, 1, 0), flip(s3, 1, 2)


def reduce_parts(wide, rows, width, name):
    wide = [wide[0]] + [flip_z(wide[j], j) for j in range(1, 4)]
    rows = [rows[0]] + [flip_z(rows[j], j) for j in range(1, 4)]
    count = rows[0].shape[0]
    *parts, row_total = call(
        sum_parts_kernel,
        (),
        (*wide, *rows),
        [((64, width), jnp.bfloat16)] * 4 + [((count, 1024), jnp.bfloat16)],
        name=name + "_sum",
    )
    parts = [parts[0]] + [flip(parts[j], 0, j) for j in range(1, 4)]
    extra = count * 1024 // width
    (joined,) = call(
        join_kernel,
        (),
        (*parts, row_total),
        [((256 + extra, width), jnp.bfloat16)],
        name=name + "_join",
    )
    near = [joined] + [flip_z(joined, j) for j in range(1, 4)]
    result = []
    for piece in near:
        result += [piece, flip(piece, 1, 0)]
    return result


def in_planes(
    tokens,
    cotangent,
    segments,
    decay_index,
    step_index,
    w_qkv,
    w_gate,
    w_out,
    w_gu,
    w_down,
    persist_keys,
    persist_values,
    norm_gain,
    ffn_gain,
):
    bf16, f32 = jnp.bfloat16, jnp.float32
    ctx = lax.axis_index("ctx")
    f = lax.axis_index("fsdp")
    z, x = ctx // 2, ctx % 2
    head = 2 * f + x
    idx = jnp.stack([z, x, f, head]).astype(jnp.int32)

    own = to_plane(tokens[0])
    ints = to_plane(
        jnp.concatenate([segments[0], decay_index[0].reshape(-1), step_index[0].reshape(-1)]).reshape(
            10, 128
        )
    )
    small = jnp.concatenate(
        [
            persist_keys,
            persist_values,
            jnp.concatenate([norm_gain, ffn_gain, norm_gain, ffn_gain]).reshape(1, 1024),
            jnp.zeros((7, 1024), bf16),
        ],
        axis=0,
    )
    wq_parts = call(
        pack_qkvg_kernel, (idx,), (w_qkv, w_gate), [((256, 512), bf16)] * 4, name="pack_qkvg"
    )
    wq_parts = [wq_parts[0]] + [flip(wq_parts[j], 0, j) for j in range(1, 4)]
    smalls = jnp.stack([small] + [flip(small, 0, j) for j in range(1, 4)])
    blocks = gather_plane(own)
    own_cot = to_plane(cotangent[0])
    gu_parts = call(pack_gu_kernel, (idx,), (w_gu,), [((256, 768), bf16)] * 4, name="pack_gu")
    gu_parts = [gu_parts[0]] + [flip(gu_parts[j], 0, j) for j in range(1, 4)]
    cots = gather_plane(own_cot)

    smalls = jnp.stack(
        [lax.dynamic_index_in_dim(smalls, f ^ j, 0, keepdims=False) for j in range(4)]
    )
    gain_one = smalls[:, 8, 0:256].reshape(1, 1024).astype(f32)
    gain_two = smalls[:, 8, 256:512].reshape(1, 1024).astype(f32)
    pk = lax.dynamic_slice_in_dim(smalls[:, 0:4].reshape(16, 1024), head * 128, 128, 1)
    pv = lax.dynamic_slice_in_dim(smalls[:, 4:8].reshape(16, 1024), head * 128, 128, 1)
    rates = jnp.stack(
        [0.6 * jnp.exp2(-ints[8].astype(f32)), 0.1 * jnp.exp2(-ints[9].astype(f32))]
    )
    wo = lax.dynamic_slice_in_dim(w_out, x * 128, 128, 0)
    wd = jnp.pad(
        lax.dynamic_slice_in_dim(w_down, x * 352, 352, 0), ((0, HIDDEN_PAD - 352), (0, 0))
    )

    quad = ((4, 128, 1024), bf16)
    (
        send,
        keep,
        normed,
        w_full,
        qkv,
        gate,
        att,
        rec,
        probs,
        pprobs,
        states,
        mixed,
    ) = call(
        mixer_forward_kernel,
        (idx, rates),
        (ints, *blocks, *wq_parts, gain_one, wo, pk, pv),
        [
            quad,
            quad,
            ((1024, 1024), bf16),
            ((1024, 512), bf16),
            ((1024, 384), bf16),
            ((1024, 128), f32),
            ((1024, 128), f32),
            ((1024, 128), f32),
            ((1024, 1024), bf16),
            ((1024, 16), bf16),
            ((16, 128, 128), bf16),
            ((1024, 128), bf16),
        ],
        flops=3 * 10**9,
        name="mixer_forward",
    )
    shares = scatter_plane(keep, send)
    block = (128, 1024)
    residual, feed = call(
        residual_kernel,
        (),
        (own, gain_two, *shares),
        [(block, f32), (block, bf16)],
        name="residual",
    )
    feeds = gather_plane(feed)
    send_g, keep_g, send_d, keep_d, active, dgu, feed_all, cot_all = call(
        feed_kernel,
        (idx,),
        (*feeds, *cots, *gu_parts, wd),
        [
            quad,
            quad,
            quad,
            quad,
            ((1024, HIDDEN_PAD), bf16),
            ((1024, 2 * HIDDEN_PAD), bf16),
            ((1024, 1024), bf16),
            ((1024, 1024), bf16),
        ],
        scratch=[((1024, 2 * HIDDEN_PAD), bf16)],
        flops=5 * 10**9,
        name="feed",
    )
    shares = scatter_plane(keep_g, send_g)
    grad_residual, branch = call(
        branch_kernel,
        (),
        (residual, gain_two, own_cot, *shares),
        [(block, f32), (block, bf16)],
        name="branch",
    )
    branches = gather_plane(branch)

    feed_parts = call(
        feed_weights_kernel,
        (idx,),
        (feed_all, dgu, active, cot_all),
        [((4, 64, 768), bf16)] * 4 + [((Z_HIDDEN, 1024), bf16)] * 4,
        scratch=[((256, 768), f32), ((HIDDEN_PAD, 1024), f32)],
        flops=3 * 10**9,
        name="feed_weights",
    )
    feed_pieces = reduce_parts(feed_parts[0:4], feed_parts[4:8], 768, "feed")

    shares = scatter_plane(keep_d, send_d)
    (result,) = call(output_kernel, (), (residual, *shares), [(block, bf16)], name="output")
    result = to_plane(result)

    send, keep, dqkvg, branch_all, gpk, gpv = call(
        mixer_backward_kernel,
        (idx, rates),
        (*branches, wo, w_full, qkv, gate, att, rec, probs, pprobs, states, pk, pv),
        [
            quad,
            quad,
            ((1024, 512), bf16),
            ((1024, 1024), bf16),
            ((16, 128), f32),
            ((16, 128), f32),
        ],
        scratch=[
            ((1024, 128), bf16),
            ((1024, 128), bf16),
            ((1024, 128), f32),
            ((1024, 1024), bf16),
            ((1024, 128), f32),
            ((1024, 128), f32),
            ((1024, 16), bf16),
        ],
        flops=4 * 10**9,
        name="mixer_backward",
    )
    mixer_parts = call(
        mixer_weights_kernel,
        (idx,),
        (normed, dqkvg, mixed, branch_all),
        [((4, 64, 512), bf16)] * 4 + [((32, 1024), bf16)] * 4,
        scratch=[((256, 512), f32), ((128, 1024), f32)],
        flops=2 * 10**9,
        name="mixer_weights",
    )
    shares = scatter_plane(keep, send)
    mixer_pieces = reduce_parts(mixer_parts[0:4], mixer_parts[4:8], 512, "mixer")
    (grad_tokens,) = call(
        tokens_kernel, (), (own, gain_one, grad_residual, *shares), [(block, bf16)], name="tokens"
    )
    grad_tokens = to_plane(grad_tokens)

    persist = jnp.concatenate([gpk, gpv], axis=0)
    persist = lax.dynamic_update_slice_in_dim(
        jnp.zeros((32, 1024), f32), persist, head * 128, 1
    )
    persist = lax.psum(persist, ("ctx", "fsdp"))
    grad_pk = lax.dynamic_slice_in_dim(persist, f * 4, 4, 0)
    grad_pv = lax.dynamic_slice_in_dim(persist, 16 + f * 4, 4, 0)

    grad_gu, grad_down, grad_ffn = call(
        feed_unpack_kernel,
        (idx,),
        (*feed_pieces, w_gu, ffn_gain.reshape(1, 256)),
        [((256, 2 * FF), f32), ((FF // 4, 1024), f32), ((1, 256), f32)],
        name="feed_unpack",
    )
    grad_qkv, grad_gate, grad_out, grad_norm = call(
        mixer_unpack_kernel,
        (idx,),
        (*mixer_pieces, w_qkv, w_gate, norm_gain.reshape(1, 256)),
        [((256, 3072), f32), ((256, 1024), f32), ((256, 1024), f32), ((1, 256), f32)],
        name="mixer_unpack",
    )
    return (
        result[None],
        grad_tokens.astype(f32)[None],
        grad_qkv,
        grad_gate,
        grad_out,
        grad_gu,
        grad_down,
        grad_pk,
        grad_pv,
        grad_norm.reshape(256),
        grad_ffn.reshape(256),
    )


def solution(mesh):
    in_specs = (
        P("fsdp", "ctx", None),
        P("fsdp", "ctx", None),
        P("fsdp", None),
        P("fsdp", None, None),
        P("fsdp", None, None),
        P("fsdp", None),
        P("fsdp", None),
        P("fsdp", None),
        P("fsdp", None),
        P("fsdp", None),
        P("fsdp", None),
        P("fsdp", None),
        P("fsdp"),
        P("fsdp"),
    )
    out_specs = (
        P("fsdp", "ctx", None),
        P("fsdp", "ctx", None),
        P("fsdp", None),
        P("fsdp", None),
        P("fsdp", None),
        P("fsdp", None),
        P("fsdp", None),
        P("fsdp", None),
        P("fsdp", None),
        P("fsdp"),
        P("fsdp"),
    )
    planes = dict(mesh.shape) == {"ctx": HEADS, "fsdp": PLANES}
    return jax.shard_map(
        in_planes if planes else on_device, mesh=mesh, in_specs=in_specs, out_specs=out_specs, check_vma=False
    )
```

```python
import functools

import jax
import jax.numpy as jnp
import numpy as np
from jax import lax
from jax.experimental import pallas as pl
from jax.experimental.pallas import tpu as pltpu
from jax.sharding import PartitionSpec as P

HEADS = 8
HEAD_WIDTH_SIZE = 128
FF = 2816
GROUP = 64


epsilon = 1e-06
momentum = 0.9
masked_score = -1e30
highest_precision = lax.Precision.HIGHEST


def rms_scale(values):
    return lax.rsqrt(jnp.mean(values * values, axis=-1, keepdims=True) + epsilon)


def norm_back(values, inv_rms, gain_vec, grad_normed):
    scaled_grad = grad_normed * gain_vec
    grad_gain = jnp.sum(grad_normed * values * inv_rms, axis=0)
    grad_values = inv_rms * scaled_grad - values * inv_rms * inv_rms * inv_rms * jnp.mean(
        scaled_grad * values, axis=-1, keepdims=True
    )
    return (grad_values, grad_gain)


def place_rows(row_index, shard_rows, dev_count):
    half_rows = shard_rows // 2
    owner_dev = row_index // shard_rows
    inner_row = row_index % shard_rows
    block_id = jnp.where(inner_row < half_rows, owner_dev, 2 * dev_count - 1 - owner_dev)
    return block_id * half_rows + inner_row % half_rows


def position_order(stored, dev_count):
    rows = stored.shape[0]
    rest = stored.shape[1:]
    split = stored.reshape((dev_count, 2, rows // (2 * dev_count)) + rest)
    early = split[:, 0].reshape((-1,) + rest)
    late = split[::-1, 1].reshape((-1,) + rest)
    return jnp.concatenate([early, late], axis=0)


def key_mask(query_pos, query_seg, key_pos, key_seg):
    return (key_seg[None, :] == query_seg[:, None]) & (key_pos[None, :] <= query_pos[:, None])


def head_scores(queries, key_block):
    return jnp.einsum(
        "qhd,khd->hqk", queries, key_block, preferred_element_type=jnp.float32
    ) * HEAD_WIDTH_SIZE ** (-0.5)


def online_step(running, scores, value_block):
    run_max, run_total, accumulated = running
    new_max = jnp.maximum(run_max, jnp.max(scores, axis=-1))
    rescale = jnp.exp(run_max - new_max)
    weights = jnp.exp(scores - new_max[:, :, None])
    run_total = run_total * rescale + jnp.sum(weights, axis=-1)
    update = jnp.einsum(
        "hqk,khd->qhd",
        weights.astype(jnp.bfloat16),
        value_block,
        preferred_element_type=jnp.float32,
    )
    accumulated = accumulated * jnp.transpose(rescale)[:, :, None] + update
    return (new_max, run_total, accumulated)


def fold_keys(running, all_keys, all_values, context):
    queries, query_pos, query_seg, segment_all, shard_rows, dev_count = context
    total_rows = all_keys.shape[0]
    block_rows = min(512, total_rows)

    def fold_one_block(carried, block_index):
        offset_row = block_index * block_rows
        key_block = lax.dynamic_slice_in_dim(all_keys, offset_row, block_rows, 0).reshape(
            block_rows, HEADS, HEAD_WIDTH_SIZE
        )
        value_block = lax.dynamic_slice_in_dim(all_values, offset_row, block_rows, 0).reshape(
            block_rows, HEADS, HEAD_WIDTH_SIZE
        )
        key_pos = place_rows(
            offset_row + jnp.arange(block_rows, dtype=jnp.int32), shard_rows, dev_count
        )
        key_seg = jnp.take(segment_all, key_pos)
        allowed = key_mask(query_pos, query_seg, key_pos, key_seg)
        scores = jnp.where(allowed[None], head_scores(queries, key_block), masked_score)
        carried = online_step(carried, scores, value_block)
        return (carried, None)

    running, _ = lax.scan(
        fold_one_block, running, jnp.arange(total_rows // block_rows, dtype=jnp.int32)
    )
    return running


def back_every_key(grad_query, all_keys, all_values, context, grad_heads, log_total, row_delta):
    queries, query_pos, query_seg, segment_all, shard_rows, dev_count = context
    total_rows = all_keys.shape[0]
    block_rows = min(512, total_rows)
    scale_factor = HEAD_WIDTH_SIZE ** (-0.5)

    def back_one_block(carried, block_index):
        offset_row = block_index * block_rows
        key_block = lax.dynamic_slice_in_dim(all_keys, offset_row, block_rows, 0).reshape(
            block_rows, HEADS, HEAD_WIDTH_SIZE
        )
        value_block = lax.dynamic_slice_in_dim(all_values, offset_row, block_rows, 0).reshape(
            block_rows, HEADS, HEAD_WIDTH_SIZE
        )
        key_pos = place_rows(
            offset_row + jnp.arange(block_rows, dtype=jnp.int32), shard_rows, dev_count
        )
        key_seg = jnp.take(segment_all, key_pos)
        allowed = key_mask(query_pos, query_seg, key_pos, key_seg)
        scores = jnp.where(allowed[None], head_scores(queries, key_block), masked_score)
        prob_block = jnp.exp(scores - log_total[:, :, None])
        grad_prob = jnp.einsum(
            "qhd,khd->hqk", grad_heads, value_block, preferred_element_type=jnp.float32
        )
        grad_scores = (prob_block * (grad_prob - row_delta[:, :, None])).astype(jnp.bfloat16)
        query_grad = (
            carried
            + jnp.einsum("hqk,khd->qhd", grad_scores, key_block, preferred_element_type=jnp.float32)
            * scale_factor
        )
        key_grad = (
            jnp.einsum("hqk,qhd->khd", grad_scores, queries, preferred_element_type=jnp.float32)
            * scale_factor
        )
        value_grad = jnp.einsum(
            "hqk,qhd->khd",
            prob_block.astype(jnp.bfloat16),
            grad_heads,
            preferred_element_type=jnp.float32,
        )
        return (query_grad, (key_grad, value_grad))

    grad_query, (key_grads, value_grads) = lax.scan(
        back_one_block, grad_query, jnp.arange(total_rows // block_rows, dtype=jnp.int32)
    )
    return (
        grad_query,
        key_grads.reshape(total_rows, HEADS, HEAD_WIDTH_SIZE),
        value_grads.reshape(total_rows, HEADS, HEAD_WIDTH_SIZE),
    )


def group_step(stacked_rows, group_key_rows, group_value_rows, alpha_row, learning_rate_row):
    current_memory = stacked_rows[:, :HEAD_WIDTH_SIZE]
    moment_now = stacked_rows[:, HEAD_WIDTH_SIZE:]
    gram_matrix = (
        jnp.einsum("thk,thj->hkj", group_key_rows, group_key_rows, precision=highest_precision)
        * learning_rate_row[:, None, None]
    )
    mixed_product = (
        jnp.einsum("qgw,qgc->gwc", group_key_rows, group_value_rows, precision=highest_precision)
        * learning_rate_row[:, None, None]
    )
    memory_gradient = (
        jnp.einsum("fld,fdi->fli", gram_matrix, current_memory, precision=highest_precision)
        - mixed_product
    )
    moment_next = momentum * moment_now - memory_gradient
    memory_next = (1.0 - alpha_row)[:, None, None] * current_memory + moment_next
    return jnp.concatenate([memory_next, moment_next], axis=1)


def run_block(stacked_rows, query_part, key_part, value_part, alphas, thetas):
    scale_factor = HEAD_WIDTH_SIZE ** (-0.5)
    group_query_rows = query_part * scale_factor
    recalled_rows = [
        jnp.einsum(
            "ipb,pbx->ipx",
            group_query_rows,
            stacked_rows[:, :HEAD_WIDTH_SIZE],
            precision=highest_precision,
        )
    ]
    stacked_rows = group_step(
        stacked_rows, key_part * scale_factor, value_part, alphas[0], thetas[0]
    )
    return (jnp.concatenate(recalled_rows, axis=0), stacked_rows)


def states_before(key_order, value_order, alpha_all, theta_all, early_index, late_index):
    groups = alpha_all.shape[0]
    scale_factor = HEAD_WIDTH_SIZE ** (-0.5)
    key_groups = key_order.reshape(groups, GROUP, HEADS, HEAD_WIDTH_SIZE)
    value_groups = value_order.reshape(groups, GROUP, HEADS, HEAD_WIDTH_SIZE)
    zero_state = jnp.zeros((HEADS, 2 * HEAD_WIDTH_SIZE, HEAD_WIDTH_SIZE), jnp.float32)

    def states_one_group(carried, inputs):
        stacked_rows, into_early, into_late = carried
        group_key_rows, group_value_rows, alpha_row, learning_rate_row, group_index = inputs
        into_early = jnp.where(group_index == early_index, stacked_rows, into_early)
        into_late = jnp.where(group_index == late_index, stacked_rows, into_late)
        current_memory = stacked_rows[:, :HEAD_WIDTH_SIZE]
        moment_now = stacked_rows[:, HEAD_WIDTH_SIZE:]
        gram_matrix = (
            jnp.einsum(
                "thk,thj->hkj", group_key_rows, group_key_rows, preferred_element_type=jnp.float32
            )
            * (learning_rate_row / HEAD_WIDTH_SIZE)[:, None, None]
        )
        mixed_product = (
            jnp.einsum(
                "qgw,qgc->gwc", group_key_rows, group_value_rows, preferred_element_type=jnp.float32
            )
            * (learning_rate_row * scale_factor)[:, None, None]
        )
        memory_gradient = (
            jnp.einsum("fld,fdi->fli", gram_matrix, current_memory, precision=highest_precision)
            - mixed_product
        )
        moment_next = momentum * moment_now - memory_gradient
        memory_next = (1.0 - alpha_row)[:, None, None] * current_memory + moment_next
        stacked_rows = jnp.concatenate([memory_next, moment_next], axis=1)
        return ((stacked_rows, into_early, into_late), None)

    (_, into_early, into_late), _ = lax.scan(
        states_one_group,
        (zero_state, zero_state, zero_state),
        (key_groups, value_groups, alpha_all, theta_all, jnp.arange(groups, dtype=jnp.int32)),
    )
    return (into_early, into_late)


def adjoints_after(
    query_order, key_order, recall_grad_order, alpha_all, theta_all, early_end, late_end
):
    groups = alpha_all.shape[0]
    scale_factor = HEAD_WIDTH_SIZE ** (-0.5)
    query_groups = query_order.reshape(groups, GROUP, HEADS, HEAD_WIDTH_SIZE)
    key_groups = key_order.reshape(groups, GROUP, HEADS, HEAD_WIDTH_SIZE)
    grad_groups = recall_grad_order.reshape(groups, GROUP, HEADS, HEAD_WIDTH_SIZE)
    zero_state = jnp.zeros((HEADS, 2 * HEAD_WIDTH_SIZE, HEAD_WIDTH_SIZE), jnp.float32)

    def adjoints_one_group(carried, inputs):
        adjoint, out_early, out_late = carried
        (
            group_query_rows,
            group_key_rows,
            gradient_group_rows,
            alpha_row,
            learning_rate_row,
            group_index,
        ) = inputs
        out_early = jnp.where(group_index + 1 == early_end, adjoint, out_early)
        out_late = jnp.where(group_index + 1 == late_end, adjoint, out_late)
        gram_matrix = (
            jnp.einsum(
                "thk,thj->hkj", group_key_rows, group_key_rows, preferred_element_type=jnp.float32
            )
            * (learning_rate_row / HEAD_WIDTH_SIZE)[:, None, None]
        )
        query_term = (
            jnp.einsum(
                "qgw,qgc->gwc",
                group_query_rows,
                gradient_group_rows,
                preferred_element_type=jnp.float32,
            )
            * scale_factor
        )
        grad_m = adjoint[:, :HEAD_WIDTH_SIZE]
        summed_rows = grad_m + adjoint[:, HEAD_WIDTH_SIZE:]
        new_m = (
            (1.0 - alpha_row)[:, None, None] * grad_m
            + query_term
            - jnp.einsum("fld,fdi->fli", gram_matrix, summed_rows, precision=highest_precision)
        )
        adjoint = jnp.concatenate([new_m, momentum * summed_rows], axis=1)
        return ((adjoint, out_early, out_late), None)

    (_, out_early, out_late), _ = lax.scan(
        adjoints_one_group,
        (zero_state, zero_state, zero_state),
        (
            query_groups,
            key_groups,
            grad_groups,
            alpha_all,
            theta_all,
            jnp.arange(groups, dtype=jnp.int32),
        ),
        reverse=True,
    )
    return (out_early, out_late)


def on_device(
    tokens,
    cotangent,
    segments,
    decay_index,
    step_index,
    w_qkv,
    w_gate,
    w_out,
    w_gu,
    w_down,
    persist_keys,
    persist_values,
    norm_gain,
    ffn_gain,
):
    shard_rows = tokens.shape[1]
    model_width = tokens.shape[2]
    half_rows = shard_rows // 2
    dev_count = lax.axis_size("ctx")
    device = lax.axis_index("ctx")
    scale_factor = HEAD_WIDTH_SIZE ** (-0.5)
    full_weights = (
        lax.all_gather(w_qkv, "fsdp", axis=0, tiled=True),
        lax.all_gather(w_gate, "fsdp", axis=0, tiled=True),
        lax.all_gather(w_out, "fsdp", axis=0, tiled=True),
        lax.all_gather(w_gu, "fsdp", axis=0, tiled=True),
        lax.all_gather(w_down, "fsdp", axis=0, tiled=True),
        lax.all_gather(persist_keys, "fsdp", axis=0, tiled=True),
        lax.all_gather(persist_values, "fsdp", axis=0, tiled=True),
        lax.all_gather(norm_gain, "fsdp", axis=0, tiled=True),
        lax.all_gather(ffn_gain, "fsdp", axis=0, tiled=True),
    )
    wq_full, wg_full, wo_full, wgu_full, wd_full, pkeys_full, pvalues_full, gain_attn, gain_ffn = (
        full_weights
    )
    gain_attn32 = gain_attn.astype(jnp.float32)
    gain_ffn32 = gain_ffn.astype(jnp.float32)
    pkeys_heads = pkeys_full.reshape(-1, HEADS, HEAD_WIDTH_SIZE)
    pvalues_heads = pvalues_full.reshape(-1, HEADS, HEAD_WIDTH_SIZE)
    inputs32 = tokens[0].astype(jnp.float32)
    inv_rms_one = rms_scale(inputs32)
    normed_low = (inputs32 * inv_rms_one * gain_attn32).astype(jnp.bfloat16)
    projected = jnp.dot(normed_low, wq_full, preferred_element_type=jnp.float32)
    query_flat = projected[:, :model_width].astype(jnp.bfloat16)
    key_flat = projected[:, model_width : 2 * model_width].astype(jnp.bfloat16)
    value_flat = projected[:, 2 * model_width :].astype(jnp.bfloat16)
    query_heads = query_flat.reshape(shard_rows, HEADS, HEAD_WIDTH_SIZE)
    gate_open = jax.nn.sigmoid(jnp.dot(normed_low, wg_full, preferred_element_type=jnp.float32))
    local_rows = jnp.arange(shard_rows, dtype=jnp.int32)
    query_pos = place_rows(device * shard_rows + local_rows, shard_rows, dev_count)
    segment_all = segments[0]
    query_seg = jnp.take(segment_all, query_pos)
    context = (query_heads, query_pos, query_seg, segment_all, shard_rows, dev_count)
    all_keys, all_values = (
        lax.all_gather(key_flat, "ctx", axis=0, tiled=True),
        lax.all_gather(value_flat, "ctx", axis=0, tiled=True),
    )
    persist_scores = head_scores(query_heads, pkeys_heads)
    start_state = (
        jnp.full((HEADS, shard_rows), masked_score, jnp.float32),
        jnp.zeros((HEADS, shard_rows), jnp.float32),
        jnp.zeros((shard_rows, HEADS, HEAD_WIDTH_SIZE), jnp.float32),
    )
    running = online_step(start_state, persist_scores, pvalues_heads)
    running = fold_keys(running, all_keys, all_values, context)
    run_max, run_total, accumulated = running
    attended = accumulated / jnp.transpose(run_total)[:, :, None]
    log_total = run_max + jnp.log(run_total)
    group_count = half_rows // GROUP
    alpha_all = 0.6 * jnp.exp2(-decay_index[0].astype(jnp.float32))
    theta_all = 0.1 * jnp.exp2(-step_index[0].astype(jnp.float32))
    early_first = device * group_count
    late_first = (2 * dev_count - 1 - device) * group_count
    alpha_early = lax.dynamic_slice_in_dim(alpha_all, early_first, group_count, 0)
    theta_early = lax.dynamic_slice_in_dim(theta_all, early_first, group_count, 0)
    alpha_late = lax.dynamic_slice_in_dim(alpha_all, late_first, group_count, 0)
    theta_late = lax.dynamic_slice_in_dim(theta_all, late_first, group_count, 0)
    query_f = query_heads.astype(jnp.float32)
    key_f = key_flat.astype(jnp.float32).reshape(shard_rows, HEADS, HEAD_WIDTH_SIZE)
    value_f = value_flat.astype(jnp.float32).reshape(shard_rows, HEADS, HEAD_WIDTH_SIZE)
    early_parts = (query_f[:half_rows], key_f[:half_rows], value_f[:half_rows])
    late_parts = (query_f[half_rows:], key_f[half_rows:], value_f[half_rows:])

    def early_run(stacked_rows, query_part, key_part, value_part):
        return run_block(stacked_rows, query_part, key_part, value_part, alpha_early, theta_early)

    def late_run(stacked_rows, query_part, key_part, value_part):
        return run_block(stacked_rows, query_part, key_part, value_part, alpha_late, theta_late)

    into_early, into_late = states_before(
        position_order(all_keys, dev_count),
        position_order(all_values, dev_count),
        alpha_all,
        theta_all,
        early_first,
        late_first,
    )
    recall_early, _ = early_run(into_early, early_parts[0], early_parts[1], early_parts[2])
    recall_late, _ = late_run(into_late, late_parts[0], late_parts[1], late_parts[2])
    recall = jnp.concatenate([recall_early, recall_late], axis=0).reshape(shard_rows, model_width)
    mixed_low = (attended.reshape(shard_rows, model_width) + gate_open * recall).astype(
        jnp.bfloat16
    )
    residual = inputs32 + jnp.dot(mixed_low, wo_full, preferred_element_type=jnp.float32)
    inv_rms_two = rms_scale(residual)
    normed_two = (residual * inv_rms_two * gain_ffn32).astype(jnp.bfloat16)
    gate_up = jnp.dot(normed_two, wgu_full, preferred_element_type=jnp.float32)
    gate_part = gate_up[:, :FF]
    up_part = gate_up[:, FF:]
    active = (jax.nn.silu(gate_part) * up_part).astype(jnp.bfloat16)
    result = residual + jnp.dot(active, wd_full, preferred_element_type=jnp.float32)
    cot_low = cotangent[0]
    grad_w_down = jnp.einsum("tf,td->fd", active, cot_low, preferred_element_type=jnp.float32)
    grad_active = jnp.einsum("td,fd->tf", cot_low, wd_full, preferred_element_type=jnp.float32)
    sigma_gate = jax.nn.sigmoid(gate_part)
    grad_gate_part = grad_active * up_part * sigma_gate * (1.0 + gate_part * (1.0 - sigma_gate))
    grad_up_part = grad_active * gate_part * sigma_gate
    grad_gu_low = jnp.concatenate([grad_gate_part, grad_up_part], axis=1).astype(jnp.bfloat16)
    grad_w_gu = jnp.einsum("td,tf->df", normed_two, grad_gu_low, preferred_element_type=jnp.float32)
    grad_normed_two = jnp.einsum(
        "tf,df->td", grad_gu_low, wgu_full, preferred_element_type=jnp.float32
    )
    grad_res_norm, grad_ffn_gain = norm_back(residual, inv_rms_two, gain_ffn32, grad_normed_two)
    grad_residual = cot_low.astype(jnp.float32) + grad_res_norm
    grad_branch = grad_residual.astype(jnp.bfloat16)
    grad_w_out = jnp.einsum("td,te->de", mixed_low, grad_branch, preferred_element_type=jnp.float32)
    grad_mixed_low = jnp.einsum(
        "te,de->td", grad_branch, wo_full, preferred_element_type=jnp.float32
    ).astype(jnp.bfloat16)
    grad_mixed32 = grad_mixed_low.astype(jnp.float32)
    grad_gate_low = (grad_mixed32 * recall * gate_open * (1.0 - gate_open)).astype(jnp.bfloat16)
    grad_w_gate = jnp.einsum(
        "td,tf->df", normed_low, grad_gate_low, preferred_element_type=jnp.float32
    )
    recall_grad_low = (grad_mixed32 * gate_open).astype(jnp.bfloat16)
    grad_recall = recall_grad_low.astype(jnp.float32).reshape(shard_rows, HEADS, HEAD_WIDTH_SIZE)
    grad_heads = grad_mixed_low.reshape(shard_rows, HEADS, HEAD_WIDTH_SIZE)
    row_delta = jnp.transpose(jnp.sum(grad_heads.astype(jnp.float32) * attended, axis=-1))
    memory_queries, all_recall_grads = (
        lax.all_gather(query_flat, "ctx", axis=0, tiled=True),
        lax.all_gather(recall_grad_low, "ctx", axis=0, tiled=True),
    )
    out_early, out_late = adjoints_after(
        position_order(memory_queries, dev_count),
        position_order(all_keys, dev_count),
        position_order(all_recall_grads, dev_count),
        alpha_all,
        theta_all,
        early_first + group_count,
        late_first + group_count,
    )
    _, pull_early = jax.vjp(early_run, into_early, early_parts[0], early_parts[1], early_parts[2])
    _, grad_qe, grad_ke, grad_ve = pull_early((grad_recall[:half_rows], out_early))
    _, pull_late = jax.vjp(late_run, into_late, late_parts[0], late_parts[1], late_parts[2])
    _, grad_ql, grad_kl, grad_vl = pull_late((grad_recall[half_rows:], out_late))
    grad_q_mem = jnp.concatenate([grad_qe, grad_ql], axis=0).reshape(shard_rows, model_width)
    grad_k_mem = jnp.concatenate([grad_ke, grad_kl], axis=0).reshape(shard_rows, model_width)
    grad_v_mem = jnp.concatenate([grad_ve, grad_vl], axis=0).reshape(shard_rows, model_width)
    persist_probs = jnp.exp(persist_scores - log_total[:, :, None])
    persist_grad_prob = jnp.einsum(
        "qhd,phd->hqp", grad_heads, pvalues_heads, preferred_element_type=jnp.float32
    )
    persist_ds = (persist_probs * (persist_grad_prob - row_delta[:, :, None])).astype(jnp.bfloat16)
    grad_query_att = (
        jnp.einsum("hqp,phd->qhd", persist_ds, pkeys_heads, preferred_element_type=jnp.float32)
        * scale_factor
    )
    grad_pkeys = (
        jnp.einsum("hqp,qhd->phd", persist_ds, query_heads, preferred_element_type=jnp.float32)
        * scale_factor
    )
    grad_pvalues = jnp.einsum(
        "hqp,qhd->phd",
        persist_probs.astype(jnp.bfloat16),
        grad_heads,
        preferred_element_type=jnp.float32,
    )
    grad_query_att, key_grads_all, value_grads_all = back_every_key(
        grad_query_att, all_keys, all_values, context, grad_heads, log_total, row_delta
    )
    key_grad_att, value_grad_att = (
        lax.psum_scatter(key_grads_all, "ctx", scatter_dimension=0, tiled=True),
        lax.psum_scatter(value_grads_all, "ctx", scatter_dimension=0, tiled=True),
    )
    grad_query = grad_query_att.reshape(shard_rows, model_width) + grad_q_mem
    grad_key = key_grad_att.reshape(shard_rows, model_width) + grad_k_mem
    grad_value = value_grad_att.reshape(shard_rows, model_width) + grad_v_mem
    grad_qkv_low = jnp.concatenate([grad_query, grad_key, grad_value], axis=1).astype(jnp.bfloat16)
    grad_w_qkv = jnp.einsum(
        "td,tf->df", normed_low, grad_qkv_low, preferred_element_type=jnp.float32
    )
    grad_normed = jnp.einsum(
        "tf,df->td", grad_qkv_low, wq_full, preferred_element_type=jnp.float32
    ) + jnp.einsum("tf,df->td", grad_gate_low, wg_full, preferred_element_type=jnp.float32)
    grad_in_norm, grad_norm_gain = norm_back(inputs32, inv_rms_one, gain_attn32, grad_normed)
    grad_inputs = grad_residual + grad_in_norm
    local_grads = (
        grad_w_qkv,
        grad_w_gate,
        grad_w_out,
        grad_w_gu,
        grad_w_down,
        grad_pkeys.reshape(-1, model_width),
        grad_pvalues.reshape(-1, model_width),
        grad_norm_gain,
        grad_ffn_gain,
    )
    shares = (
        lax.psum_scatter(
            local_grads[0].astype(jnp.bfloat16), "fsdp", scatter_dimension=0, tiled=True
        ).astype(jnp.float32),
        lax.psum_scatter(
            local_grads[1].astype(jnp.bfloat16), "fsdp", scatter_dimension=0, tiled=True
        ).astype(jnp.float32),
        lax.psum_scatter(
            local_grads[2].astype(jnp.bfloat16), "fsdp", scatter_dimension=0, tiled=True
        ).astype(jnp.float32),
        lax.psum_scatter(
            local_grads[3].astype(jnp.bfloat16), "fsdp", scatter_dimension=0, tiled=True
        ).astype(jnp.float32),
        lax.psum_scatter(
            local_grads[4].astype(jnp.bfloat16), "fsdp", scatter_dimension=0, tiled=True
        ).astype(jnp.float32),
        lax.psum_scatter(
            local_grads[5].astype(jnp.bfloat16), "fsdp", scatter_dimension=0, tiled=True
        ).astype(jnp.float32),
        lax.psum_scatter(
            local_grads[6].astype(jnp.bfloat16), "fsdp", scatter_dimension=0, tiled=True
        ).astype(jnp.float32),
        lax.psum_scatter(
            local_grads[7].astype(jnp.bfloat16), "fsdp", scatter_dimension=0, tiled=True
        ).astype(jnp.float32),
        lax.psum_scatter(
            local_grads[8].astype(jnp.bfloat16), "fsdp", scatter_dimension=0, tiled=True
        ).astype(jnp.float32),
    )
    totals = lax.psum(
        (
            shares[0],
            shares[1],
            shares[2],
            shares[3],
            shares[4],
            shares[5],
            shares[6],
            shares[7],
            shares[8],
        ),
        "ctx",
    )
    return (
        result.astype(jnp.bfloat16)[None],
        grad_inputs[None],
        totals[0],
        totals[1],
        totals[2],
        totals[3],
        totals[4],
        totals[5],
        totals[6],
        totals[7],
        totals[8],
    )


PERSIST = 16
PLANES = 4
HIDDEN_PAD = 384
Z_HIDDEN = HIDDEN_PAD // PLANES
EXTRA = 16


def head_of(x, f, k):
    return 2 * (f ^ (k & 3)) + (x ^ (k >> 2))


def linear(z, x, f):
    return (2 * z + x) * 4 + f


def shift(value, move):
    pairs = []
    for z in range(4):
        for x in range(2):
            for f in range(4):
                pairs.append((linear(z, x, f), linear(*move(z, x, f))))
    return lax.ppermute(value, ("ctx", "fsdp"), pairs)


def to_plane(value):
    return shift(value, lambda z, x, f: (f, x, z))


def flip(value, dx, df):
    return shift(value, lambda z, x, f: (z, x ^ dx, f ^ df))


def flip_z(value, dz):
    return shift(value, lambda z, x, f: (z ^ dz, x, f))


def gather_chips(block, last=None):
    last = block if last is None else last
    return [block, flip(block, 0, 2), flip(block, 1, 0), flip(last, 1, 2)]


def gather_cores(near):
    far = [flip(b, 0, 1) for b in near]
    return [near[0], far[0], near[1], far[1], near[2], far[2], near[3], far[3]]


def dot_nn(a, b):
    return lax.dot_general(a, b, (((1,), (0,)), ((), ())), preferred_element_type=jnp.float32)


def dot_nt(a, b):
    return lax.dot_general(a, b, (((1,), (1,)), ((), ())), preferred_element_type=jnp.float32)


def dot_tn(a, b):
    return lax.dot_general(a, b, (((0,), (0,)), ((), ())), preferred_element_type=jnp.float32)


def split_two(value):
    high = value.astype(jnp.bfloat16)
    return high, (value - high.astype(jnp.float32)).astype(jnp.bfloat16)


def product_three(a, b_high, b_low):
    a_high, a_low = split_two(a)
    return dot_nn(a_high, b_high) + dot_nn(a_low, b_high) + dot_nn(a_high, b_low)


def vspec():
    return pl.BlockSpec(memory_space=pltpu.VMEM)


def sspec():
    return pl.BlockSpec(memory_space=pltpu.SMEM)


def padded_bytes(shape, dtype):
    size = jnp.dtype(dtype).itemsize
    lanes = -(-shape[-1] // 128) * 128
    rows = -(-shape[-2] // (32 // size)) * (32 // size)
    return int(np.prod(shape[:-2])) * rows * lanes * size


def call(kernel, smem, operands, outs, scratch=(), name=None, spare=6, us=0.5):
    held = [(o.shape, o.dtype) for o in operands] + list(outs) + list(scratch)
    limit = sum(padded_bytes(shape, dtype) for shape, dtype in held) + spare * 1024 * 1024
    return pl.pallas_call(
        kernel,
        out_shape=[jax.ShapeDtypeStruct(shape, dtype) for shape, dtype in outs],
        in_specs=[sspec()] * len(smem) + [vspec()] * len(operands),
        out_specs=[vspec()] * len(outs),
        scratch_shapes=[pltpu.VMEM(shape, dtype) for shape, dtype in scratch],
        compiler_params=pltpu.CompilerParams(vmem_limit_bytes=limit),
        cost_estimate=pl.CostEstimate(
            flops=int(us * 1.1e9), bytes_accessed=1000, transcendentals=0
        ),
        name=name,
    )(*smem, *operands)


def after(value, *others):
    return lax.optimization_barrier((value, *others))[0]


def pack_qkvg_kernel(idx, wq, wg, pk, pv, gain_one, gain_two, o0, o1, o2, o3, sems):
    x, f = idx[1], idx[2]
    copies = []
    for j, out in enumerate((o0, o1, o2, o3)):
        start = pl.multiple_of((2 * (f ^ j) + x) * 128, 128)
        for part in range(4):
            first = start if part == 3 else pl.multiple_of(part * 1024 + start, 128)
            source = wg if part == 3 else wq
            copies.append(
                pltpu.make_async_copy(
                    source.at[:, pl.ds(first, 128)],
                    out.at[pl.ds(0, 256), pl.ds(part * 128, 128)],
                    sems.at[4 * j + part],
                )
            )
    for copy in copies:
        copy.start()
    for j, out in enumerate((o0, o1, o2, o3)):
        start = pl.multiple_of((2 * (f ^ j) + x) * 128, 128)
        tail = [
            jnp.concatenate([pk[:, pl.ds(start, 128)], pv[:, pl.ds(start, 128)]], axis=1),
            gain_one[...],
            gain_two[...],
            jnp.zeros((EXTRA - 6, 256), jnp.bfloat16),
        ]
        tail = jnp.concatenate([t.astype(jnp.float32) for t in tail], axis=0)
        tail = jnp.concatenate([tail, jnp.zeros((EXTRA, 256), jnp.float32)], axis=1)
        out[256 : 256 + EXTRA, :] = tail.astype(jnp.bfloat16)
    for copy in copies:
        copy.wait()


def pack_gu_kernel(idx, wgu, o0, o1, o2, o3):
    z, x, f = idx[0], idx[1], idx[2]
    width = FF // 8
    for j, out in enumerate((o0, o1, o2, o3)):
        head = 2 * (f ^ j) + x
        count = 256 if j < 2 else 128
        rows = pl.ds(0 if j < 2 else pl.multiple_of((z & 1) * 128, 128), count)
        pad = jnp.zeros((count, HIDDEN_PAD - width), jnp.bfloat16)
        for h in range(8):

            @pl.when(head == h)
            def _():
                for part in range(2):
                    first = part * FF + h * width
                    at = part * HIDDEN_PAD
                    out[:, at : at + HIDDEN_PAD] = jnp.concatenate(
                        [wgu[rows, first : first + width], pad], axis=1
                    )


def lay_weights(z, f, parts, w_full):
    for j in range(2):
        w_full[pl.ds(pl.multiple_of((f ^ j) * 256, 256), 256), :] = parts[j][0:256, :]
    for j in (2, 3):
        for side in range(2):
            rows = pl.multiple_of((f ^ j) * 256 + ((z ^ side) & 1) * 128, 128)
            w_full[pl.ds(rows, 128), :] = parts[j + 2 * side][0:128, :]


def mixer_forward_kernel(idx, rates, ints, *refs):
    blocks = refs[0:8]
    parts = refs[8:12]
    w_out = refs[12]
    send, keep, normed, w_full, qkv, gate, att, rec, probs, pprobs, states, mixed = refs[13:25]
    gain_one, gain_two, pk, pv = refs[25:29]
    x, f = idx[1], idx[2]
    head = 2 * f + x
    scale = HEAD_WIDTH_SIZE ** (-0.5)
    wo = w_out[pl.ds(pl.multiple_of(x * 128, 128), 128), :]
    tails = []
    for j in range(4):
        rows = pl.multiple_of((f ^ j) * 256, 256)
        w_full[pl.ds(rows, 256), :] = parts[j][0:256, :]
        tail = parts[j][256 : 256 + EXTRA, 0:256].astype(jnp.float32)
        tails.append(tail)
        gain_one[:, pl.ds(rows, 256)] = tail[4:5]
        gain_two[:, pl.ds(rows, 256)] = tail[5:6]
    tails = jnp.concatenate([tail[0:4] for tail in tails], axis=0).astype(jnp.bfloat16)
    pk[...] = tails[:, 0:128]
    pv[...] = tails[:, 128:256]
    gain_row = gain_one[...]
    for k in range(8):
        values = blocks[k][...].astype(jnp.float32)
        normed_block = (values * rms_scale(values) * gain_row).astype(jnp.bfloat16)
        hk = head_of(x, f, k)
        normed[pl.ds(pl.multiple_of(hk * 64, 64), 64), :] = normed_block[:64]
        normed[pl.ds(pl.multiple_of((15 - hk) * 64, 64), 64), :] = normed_block[64:]
    for t in range(4):
        rows = slice(t * 256, t * 256 + 256)
        product = dot_nn(normed[rows, :], w_full[...])
        qkv[rows, :] = product[:, :384].astype(jnp.bfloat16)
        gate[rows, :] = jax.nn.sigmoid(product[:, 384:])
    state = jnp.zeros((128, 128), jnp.float32)
    moment = jnp.zeros((128, 128), jnp.float32)
    for t in range(8):
        rows = slice(t * 128, t * 128 + 128)
        width = (t + 1) * 128
        query = qkv[rows, 0:128]
        scores = dot_nt(query, qkv[0:width, 128:256]) * scale
        row_seg = jnp.transpose(jnp.broadcast_to(ints[t : t + 1, :], (128, 128)))[:, 0:1]
        col_seg = jnp.concatenate([ints[u : u + 1, :] for u in range(t + 1)], axis=1)
        row_pos = lax.broadcasted_iota(jnp.int32, (128, width), 0) + t * 128
        col_pos = lax.broadcasted_iota(jnp.int32, (128, width), 1)
        allowed = (row_seg == col_seg) & (col_pos <= row_pos)
        scores = jnp.where(allowed, scores, masked_score)
        pscores = dot_nt(query, pk[...]) * scale
        top = jnp.maximum(
            jnp.max(scores, axis=-1, keepdims=True), jnp.max(pscores, axis=-1, keepdims=True)
        )
        weights = jnp.exp(scores - top)
        pweights = jnp.exp(pscores - top)
        inverse = 1.0 / (
            jnp.sum(weights, axis=-1, keepdims=True) + jnp.sum(pweights, axis=-1, keepdims=True)
        )
        weights = (weights * inverse).astype(jnp.bfloat16)
        pweights = (pweights * inverse).astype(jnp.bfloat16)
        probs[rows, 0:width] = weights
        pprobs[rows, :] = pweights
        att[rows, :] = dot_nn(weights, qkv[0:width, 256:384]) + dot_nn(pweights, pv[...])
        for c in (2 * t, 2 * t + 1):
            grows = slice(c * 64, c * 64 + 64)
            alpha = rates[0, c * 8 + head]
            theta = rates[1, c * 8 + head]
            high, low = split_two(state)
            states[c] = high
            recalled = dot_nt(qkv[grows, 0:128], high) + dot_nt(qkv[grows, 0:128], low)
            rec[grows, :] = recalled * scale
            both = dot_tn(qkv[grows, 128:384], qkv[grows, 128:256])
            gram_high, gram_low = split_two(both[:128] * (theta / HEAD_WIDTH_SIZE))
            change = (
                dot_nn(high, gram_high) + dot_nn(low, gram_high) + dot_nn(high, gram_low)
            ) - both[128:] * (theta * scale)
            moment = momentum * moment - change
            state = (1.0 - alpha) * state + moment
        mixed[rows, :] = (att[rows, :] + gate[rows, :] * rec[rows, :]).astype(jnp.bfloat16)
    for k in range(8):
        hk = head_of(x, f, k)
        piece = jnp.concatenate(
            [
                mixed[pl.ds(pl.multiple_of(hk * 64, 64), 64), :],
                mixed[pl.ds(pl.multiple_of((15 - hk) * 64, 64), 64), :],
            ],
            axis=0,
        )
        out = send if k & 1 else keep
        out[k >> 1] = dot_nn(piece, wo).astype(jnp.bfloat16)


def mixer_backward_kernel(idx, rates, *refs):
    blocks = refs[0:8]
    w_out, w_full, qkv, gate, att, rec, probs, pprobs, states, pk, pv = refs[8:19]
    send, keep, dqkvg, branch = refs[19:23]
    gm, dy, delta, ds, dk, dv, dsp = refs[23:30]
    x, f = idx[1], idx[2]
    head = 2 * f + x
    scale = HEAD_WIDTH_SIZE ** (-0.5)
    wo = w_out[pl.ds(pl.multiple_of(x * 128, 128), 128), :]
    for k in range(8):
        hk = head_of(x, f, k)
        early = pl.ds(pl.multiple_of(hk * 64, 64), 64)
        late = pl.ds(pl.multiple_of((15 - hk) * 64, 64), 64)
        block = blocks[k][...]
        grad = dot_nt(block, wo).astype(jnp.bfloat16)
        gm[early, :] = grad[:64]
        gm[late, :] = grad[64:]
        branch[early, :] = block[:64]
        branch[late, :] = block[64:]
    for t in range(8):
        rows = slice(t * 128, t * 128 + 128)
        width = (t + 1) * 128
        grad_low = gm[rows, :]
        grad = grad_low.astype(jnp.float32)
        opened = gate[rows, :]
        dqkvg[rows, 384:512] = (grad * rec[rows, :] * opened * (1.0 - opened)).astype(jnp.bfloat16)
        dy[rows, :] = (grad * opened).astype(jnp.bfloat16)
        row_delta = jnp.sum(grad * att[rows, :], axis=-1, keepdims=True)
        grad_probs = dot_nt(grad_low, qkv[0:width, 256:384])
        ds_tile = (probs[rows, 0:width].astype(jnp.float32) * (grad_probs - row_delta)).astype(
            jnp.bfloat16
        )
        ds[rows, 0:width] = ds_tile
        grad_pprobs = dot_nt(grad_low, pv[...])
        dsp_tile = (pprobs[rows, :].astype(jnp.float32) * (grad_pprobs - row_delta)).astype(
            jnp.bfloat16
        )
        dsp[rows, :] = dsp_tile
        delta[rows, :] = (
            dot_nn(ds_tile, qkv[0:width, 128:256]) + dot_nn(dsp_tile, pk[...])
        ) * scale
    grad_pk = dot_tn(dsp[...], qkv[:, 0:128]) * scale
    grad_pv = dot_tn(pprobs[...], gm[...])
    grad_state = jnp.zeros((128, 128), jnp.float32)
    grad_moment = jnp.zeros((128, 128), jnp.float32)
    for t in range(7, -1, -1):
        rows = slice(t * 128, t * 128 + 128)
        rest = slice(t * 128, 1024)
        dk[rows, :] = dot_tn(ds[rest, rows], qkv[rest, 0:128]) * scale
        dv[rows, :] = dot_tn(probs[rest, rows], gm[rest, :])
        for c in (2 * t + 1, 2 * t):
            grows = slice(c * 64, c * 64 + 64)
            alpha = rates[0, c * 8 + head]
            theta = rates[1, c * 8 + head]
            query, key, value = qkv[grows, 0:128], qkv[grows, 128:256], qkv[grows, 256:384]
            dy_rows = dy[grows, :]
            state = states[c]
            summed = grad_state + grad_moment
            high, low = split_two(summed)
            key_summed = dot_nt(key, high) * scale
            error = value.astype(jnp.float32) - dot_nt(key, state) * scale
            grad_value = dv[grows, :] + theta * key_summed
            grad_key = dk[grows, :] + (theta * scale) * (
                dot_nn(error.astype(jnp.bfloat16), high)
                - dot_nn(key_summed.astype(jnp.bfloat16), state)
            )
            grad_query = delta[grows, :] + dot_nn(dy_rows, state) * scale
            dqkvg[grows, 0:128] = grad_query.astype(jnp.bfloat16)
            dqkvg[grows, 128:256] = grad_key.astype(jnp.bfloat16)
            dqkvg[grows, 256:384] = grad_value.astype(jnp.bfloat16)
            gram_high, gram_low = split_two(dot_tn(key, key) * (theta / HEAD_WIDTH_SIZE))
            product = dot_nn(high, gram_high) + dot_nn(low, gram_high) + dot_nn(high, gram_low)
            grad_state = (
                dot_tn(dy_rows, query) * scale + (1.0 - alpha) * grad_state - product
            )
            grad_moment = momentum * summed
    for k in range(8):
        hk = head_of(x, f, k)
        piece = jnp.concatenate(
            [
                dqkvg[pl.ds(pl.multiple_of(hk * 64, 64), 64), :],
                dqkvg[pl.ds(pl.multiple_of((15 - hk) * 64, 64), 64), :],
            ],
            axis=0,
        )
        out = send if k & 1 else keep
        out[k >> 1, 0:128, :] = dot_nt(piece, w_full[...]).astype(jnp.bfloat16)
        j = k & 3
        extra = jnp.concatenate(
            [
                grad_pk[4 * j : 4 * j + 4],
                grad_pv[4 * j : 4 * j + 4],
                jnp.zeros((EXTRA - 8, 128), jnp.float32),
            ],
            axis=0,
        )
        out[k >> 1, 128 : 128 + EXTRA, :] = jnp.zeros((EXTRA, 1024), jnp.bfloat16)
        out[k >> 1, 128 : 128 + EXTRA, pl.ds(pl.multiple_of(head * 128, 128), 128)] = extra.astype(
            jnp.bfloat16
        )


def lay_chunk(out, rows, count, width):
    out[256 : 256 + count, :] = rows[:, 0:width]
    left = 1024 - width
    part = count * left // width
    for i in range(count // part):
        out[256 + count : 256 + count + part, i * left : (i + 1) * left] = rows[
            i * part : (i + 1) * part, width:1024
        ]


def lay_chunks(z, outs, total_rows, count, width):
    for j in range(4):
        first = pl.multiple_of((z ^ j) * count, 32)
        rows = total_rows[pl.ds(first, count), :].astype(jnp.bfloat16)
        lay_chunk(outs[j & 1].at[j >> 1], rows, count, width)


def mixer_weights_kernel(idx, normed, dqkvg, mixed, branch, keep, send, total, total_o):
    z, f = idx[0], idx[2]
    outs = (keep, send)
    for t in range(4):
        total[...] = dot_tn(normed[:, t * 256 : t * 256 + 256], dqkvg[...])
        spot = pl.ds(pl.multiple_of((t ^ f) * 64, 64), 64)
        for j in range(4):
            outs[j & 1][j >> 1, spot, :] = total[
                pl.ds(pl.multiple_of((z ^ j) * 64, 64), 64), :
            ].astype(jnp.bfloat16)
    total_o[...] = dot_tn(mixed[...], branch[...])
    lay_chunks(z, outs, total_o, 32, 512)


def feed_kernel(idx, *refs):
    blocks, cots, parts = refs[0:8], refs[8:16], refs[16:22]
    w_down = refs[22]
    send_g, keep_g, send_d, keep_d, active, dgu = refs[23:29]
    w_full, wd = refs[29:31]
    z, x, f = idx[0], idx[1], idx[2]
    lay_weights(z, f, parts, w_full)
    wd[0:352, :] = w_down[pl.ds(pl.multiple_of(x * 352, 32), 352), :]
    wd[352:HIDDEN_PAD, :] = jnp.zeros((HIDDEN_PAD - 352, 1024), jnp.bfloat16)
    for k in range(4):
        rows = slice(k * 256, k * 256 + 256)
        feed = jnp.concatenate([blocks[2 * k][...], blocks[2 * k + 1][...]], axis=0)
        cot = jnp.concatenate([cots[2 * k][...], cots[2 * k + 1][...]], axis=0)
        gate_up = dot_nn(feed, w_full[...])
        g, u = gate_up[:, :HIDDEN_PAD], gate_up[:, HIDDEN_PAD:]
        sigma = jax.nn.sigmoid(g)
        active_low = (g * sigma * u).astype(jnp.bfloat16)
        active[rows, :] = active_low
        grad_active = dot_nt(cot, wd[...])
        grad_g = (grad_active * u * sigma * (1.0 + g * (1.0 - sigma))).astype(jnp.bfloat16)
        grad_u = (grad_active * g * sigma).astype(jnp.bfloat16)
        grad_low = jnp.concatenate([grad_g, grad_u], axis=1)
        dgu[rows, :] = grad_low
        grad_feed = dot_nt(grad_low, w_full[...]).astype(jnp.bfloat16)
        keep_g[k] = grad_feed[:128]
        send_g[k] = grad_feed[128:]
        down = dot_nn(active_low, wd[...]).astype(jnp.bfloat16)
        keep_d[k] = down[:128]
        send_d[k] = down[128:]


def feed_weights_kernel(idx, dgu, active, *refs):
    blocks, cot_blocks = refs[0:8], refs[8:16]
    keeps, sends = refs[16:18], refs[18:20]
    total, total_d, feeds, cots, laid = refs[20:25]
    z, f = idx[0], idx[2]
    for k in range(8):
        feeds[k * 128 : k * 128 + 128, :] = blocks[k][...]
        cots[k * 128 : k * 128 + 128, :] = cot_blocks[k][...]
    half = HIDDEN_PAD
    for t in range(4):
        total[...] = dot_tn(feeds[:, t * 256 : t * 256 + 256], dgu[...])
        spot = pl.ds(pl.multiple_of((t ^ f) * 64, 64), 64)
        for j in range(4):
            rows = total[pl.ds(pl.multiple_of((z ^ j) * 64, 64), 64), :].astype(jnp.bfloat16)
            outs = sends if j & 1 else keeps
            outs[0][j >> 1, spot, :] = rows[:, 0:half]
            outs[1][j >> 1, spot, :] = rows[:, half:]
    total_d[...] = dot_tn(active[...], cots[...])
    for j in range(4):
        first = pl.multiple_of((z ^ j) * Z_HIDDEN, 32)
        lay_chunk(laid, total_d[pl.ds(first, Z_HIDDEN), :].astype(jnp.bfloat16), Z_HIDDEN, 768)
        outs = sends if j & 1 else keeps
        outs[0][j >> 1, 256:, :] = laid[256:, 0:half]
        outs[1][j >> 1, 256:, :] = laid[256:, half:]


def add_kernel(keep, received, s0, s1, s2, s3):
    s0[...] = keep[0].astype(jnp.float32) + received[0].astype(jnp.float32)
    for k, out in ((1, s1), (2, s2), (3, s3)):
        out[...] = (keep[k].astype(jnp.float32) + received[k].astype(jnp.float32)).astype(
            jnp.bfloat16
        )


def total_of(refs):
    return (
        refs[0][...]
        + refs[1][...].astype(jnp.float32)
        + refs[2][...].astype(jnp.float32)
        + refs[3][...].astype(jnp.float32)
    )


def residual_kernel(x, gain, s0, r1, r2, r3, residual, feed):
    values = x[...].astype(jnp.float32) + total_of((s0, r1, r2, r3))
    residual[...] = values
    feed[...] = (values * rms_scale(values) * gain[...]).astype(jnp.bfloat16)


def norm_grad(values, gain, grad):
    inv = rms_scale(values)
    scaled = grad * gain
    return inv * scaled - values * (inv * inv * inv) * jnp.mean(
        scaled * values, axis=-1, keepdims=True
    )


def branch_kernel(residual, gain, cot, s0, r1, r2, r3, grad_residual, branch):
    grad = total_of((s0, r1, r2, r3))
    total = cot[...].astype(jnp.float32) + norm_grad(residual[...], gain[...], grad)
    grad_residual[...] = total
    branch[...] = total.astype(jnp.bfloat16)


def tokens_sum_kernel(keep, received, keep_far, keep_near, send_far):
    keep_far[...] = keep[0].astype(jnp.float32) + received[0].astype(jnp.float32)
    keep_near[...] = keep[1].astype(jnp.float32) + received[1].astype(jnp.float32)
    for k in range(2):
        send_far[k] = (keep[2 + k].astype(jnp.float32) + received[2 + k].astype(jnp.float32)).astype(
            jnp.bfloat16
        )


def far_kernel(own, passed, received, out_own, out_passed):
    out_own[...] = own[...] + received[0].astype(jnp.float32)
    out_passed[...] = (passed[...] + received[1].astype(jnp.float32)).astype(jnp.bfloat16)


def tokens_kernel(x, gain, grad_residual, own_sum, received, out, persist):
    total = own_sum[...] + received[...].astype(jnp.float32)
    grad = total[0:128]
    persist[...] = total[128:136]
    values = x[...].astype(jnp.float32)
    out[...] = (grad_residual[...] + norm_grad(values, gain[...], grad)).astype(jnp.bfloat16)


def output_kernel(residual, s0, r1, r2, r3, out):
    out[...] = (residual[...] + total_of((s0, r1, r2, r3))).astype(jnp.bfloat16)


def half_kernel(keep, received, own, passed):
    own[...] = keep[0].astype(jnp.float32) + received[0].astype(jnp.float32)
    passed[...] = (keep[1].astype(jnp.float32) + received[1].astype(jnp.float32)).astype(
        jnp.bfloat16
    )


def whole_kernel(pieces, *refs):
    own, received, outs = refs[:pieces], refs[pieces : 2 * pieces], refs[2 * pieces :]
    total = [
        (a[...] + b[...].astype(jnp.float32)).astype(jnp.bfloat16) for a, b in zip(own, received)
    ]
    total = jnp.concatenate(total, axis=1)
    for j in range(4):
        outs[j][...] = total[j * 64 : j * 64 + 64]
    outs[4][...] = total[256:]


def join_kernel(*refs):
    parts, rest, out = refs[0:4], refs[4], refs[5]
    for j in range(4):
        out[j * 64 : j * 64 + 64, :] = parts[j][...]
    out[256:, :] = rest[...]


def row_sums(products, out):
    out[...] = jnp.sum(jnp.transpose(products), axis=0, keepdims=True)


def feed_unpack_kernel(idx, *refs):
    parts = refs[0:8]
    wgu, gain = refs[8:10]
    out_gu, out_down, out_gain = refs[10:13]
    laid = refs[13]
    z, x, f = idx[0], idx[1], idx[2]
    width = FF // 8
    for j in range(4):
        for dx in range(2):
            part = parts[2 * j + dx]
            zj, xj = z ^ j, x ^ dx
            for jf in range(4):
                head = 2 * (f ^ jf) + xj
                laid[zj, head] = part[jf * 64 : jf * 64 + 64, :]

            lower = part[256:352, :].astype(jnp.float32)
            upper = part[352:384, :].astype(jnp.float32)
            valid = 64
            base = pl.multiple_of(xj * 352 + zj * Z_HIDDEN, 32)

            def put(first, count):
                at = pl.ds(pl.multiple_of(base + first, 32), count)
                out_down[at, 0:768] = lower[first : first + count]
                for i in range(first // 32, (first + count) // 32):
                    spot = pl.ds(pl.multiple_of(base + 32 * i, 32), 32)
                    out_down[spot, 768:1024] = upper[:, i * 256 : (i + 1) * 256]

            put(0, valid)

            @pl.when(zj < 3)
            def _():
                put(64, 32)

    for zj in range(4):
        for side in range(2):
            rows = jnp.concatenate(
                [
                    laid[zj, head][:, side * HIDDEN_PAD : side * HIDDEN_PAD + width]
                    for head in range(8)
                ],
                axis=1,
            )
            out_gu[zj * 64 : zj * 64 + 64, side * FF : side * FF + FF] = rows.astype(jnp.float32)
    sums = jnp.zeros((256, 128), jnp.float32)
    for t in range(2 * FF // 128):
        cols = slice(t * 128, t * 128 + 128)
        sums = sums + out_gu[:, cols] * wgu[:, cols].astype(jnp.float32)
    row_sums(sums, out_gain)
    out_gain[...] = out_gain[...] / gain[...].astype(jnp.float32)


def mixer_unpack_kernel(idx, *refs):
    parts = refs[0:8]
    wq, wg, gain = refs[8:11]
    out_qkv, out_gate, out_out, out_gain = refs[11:15]
    z, x, f = idx[0], idx[1], idx[2]
    for j in range(4):
        for dx in range(2):
            part = parts[2 * j + dx]
            zj, xj = z ^ j, x ^ dx
            rows = pl.ds(pl.multiple_of(zj * 64, 64), 64)
            for jf in range(4):
                head = 2 * (f ^ jf) + xj
                start = pl.multiple_of(head * 128, 128)
                for side in range(3):
                    out_qkv[rows, pl.ds(pl.multiple_of(side * 1024 + start, 128), 128)] = part[
                        jf * 64 : jf * 64 + 64, side * 128 : side * 128 + 128
                    ].astype(jnp.float32)
                out_gate[rows, pl.ds(start, 128)] = part[jf * 64 : jf * 64 + 64, 384:512].astype(
                    jnp.float32
                )
            spot = pl.ds(pl.multiple_of(xj * 128 + zj * 32, 32), 32)
            out_out[spot, 0:512] = part[256:288, :].astype(jnp.float32)
            out_out[spot, 512:1024] = part[288:320, :].astype(jnp.float32)
    sums = jnp.zeros((256, 128), jnp.float32)
    for t in range(24):
        cols = slice(t * 128, t * 128 + 128)
        sums = sums + out_qkv[:, cols] * wq[:, cols].astype(jnp.float32)
    for t in range(8):
        cols = slice(t * 128, t * 128 + 128)
        sums = sums + out_gate[:, cols] * wg[:, cols].astype(jnp.float32)
    row_sums(sums, out_gain)
    out_gain[...] = out_gain[...] / gain[...].astype(jnp.float32)


def sum_cores(keep, send):
    block = keep.shape[1:]
    return call(
        add_kernel,
        (),
        (keep, flip(send, 0, 1)),
        [(block, jnp.float32)] + [(block, jnp.bfloat16)] * 3,
        name="core_sum",
    )


def cross_chips(s0, s1, s2, s3):
    return s0, flip(s1, 0, 2), flip(s2, 1, 0), flip(s3, 1, 2)


def half_sum(keep, received, name):
    _, rows, width = keep.shape
    return call(
        half_kernel,
        (),
        (keep, received),
        [((rows, width), jnp.float32), ((rows, width), jnp.bfloat16)],
        name=name + "_half",
    )


def whole_sum(own, moved, name):
    rows = own[0].shape[0]
    width = sum(piece.shape[1] for piece in own)
    return call(
        functools.partial(whole_kernel, len(own)),
        (),
        (*own, *moved),
        [((64, width), jnp.bfloat16)] * 4 + [((rows - 256, width), jnp.bfloat16)],
        name=name + "_whole",
    )


def hand_rows(parts):
    return [parts[0]] + [flip(parts[j], 0, j) for j in range(1, 4)]


def join(parts, rest, name):
    rows, width = 256 + rest.shape[0], rest.shape[1]
    (joined,) = call(
        join_kernel, (), (*parts, rest), [((rows, width), jnp.bfloat16)], name=name + "_join"
    )
    return joined


def spread_far(joined):
    return flip_z(joined, 2), flip_z(joined, 1)


def halves_from_next_plane(parts):
    return list(parts) + [flip_z(parts[2], 1), flip_z(parts[3], 1)]


def in_planes(
    tokens,
    cotangent,
    segments,
    decay_index,
    step_index,
    w_qkv,
    w_gate,
    w_out,
    w_gu,
    w_down,
    persist_keys,
    persist_values,
    norm_gain,
    ffn_gain,
):
    bf16, f32 = jnp.bfloat16, jnp.float32
    ctx = lax.axis_index("ctx")
    f = lax.axis_index("fsdp")
    z, x = ctx // 2, ctx % 2
    head = 2 * f + x
    idx = jnp.stack([z, x, f, head]).astype(jnp.int32)

    own = to_plane(tokens[0])
    ints = to_plane(
        jnp.concatenate([segments[0], decay_index[0].reshape(-1), step_index[0].reshape(-1)]).reshape(
            10, 128
        )
    )
    anywhere = pl.BlockSpec(memory_space=pl.ANY)
    wq_parts = pl.pallas_call(
        pack_qkvg_kernel,
        out_shape=[jax.ShapeDtypeStruct((256 + EXTRA, 512), bf16)] * 4,
        in_specs=[sspec(), anywhere, anywhere] + [vspec()] * 4,
        out_specs=[vspec()] * 4,
        scratch_shapes=[pltpu.SemaphoreType.DMA((16,))],
        compiler_params=pltpu.CompilerParams(vmem_limit_bytes=60 * 1024 * 1024),
        cost_estimate=pl.CostEstimate(flops=1000, bytes_accessed=1000, transcendentals=0),
        name="pack_qkvg",
    )(
        idx,
        w_qkv,
        w_gate,
        persist_keys,
        persist_values,
        norm_gain.reshape(1, 256),
        ffn_gain.reshape(1, 256),
    )
    gu_parts = call(
        pack_gu_kernel,
        (idx,),
        (w_gu,),
        [((256, 768), bf16)] * 2 + [((128, 768), bf16)] * 2,
        name="pack_gu",
    )
    rates = jnp.stack(
        [0.6 * jnp.exp2(-ints[8].astype(f32)), 0.1 * jnp.exp2(-ints[9].astype(f32))]
    )
    wq_parts = hand_rows(wq_parts)
    own = after(own, wq_parts[0], gu_parts[0], rates)
    near = gather_chips(own)
    own_cot = to_plane(after(cotangent[0], own))
    gu_parts = [after(w, own) for w in gu_parts]
    gu_parts = [gu_parts[0], gu_parts[1], flip(gu_parts[2], 0, 2), flip(gu_parts[3], 0, 3)]
    blocks = gather_cores(near)
    rates = after(rates, own_cot)
    cot_near = gather_chips(after(own_cot, near[2]))

    block = (128, 1024)
    quad = ((4, 128, 1024), bf16)
    (
        send,
        keep,
        normed,
        w_full,
        qkv,
        gate,
        att,
        rec,
        probs,
        pprobs,
        states,
        mixed,
        gain_one,
        gain_two,
        pk,
        pv,
    ) = call(
        mixer_forward_kernel,
        (idx, rates),
        (ints, *blocks, *wq_parts, w_out),
        [
            quad,
            quad,
            ((1024, 1024), bf16),
            ((1024, 512), bf16),
            ((1024, 384), bf16),
            ((1024, 128), f32),
            ((1024, 128), f32),
            ((1024, 128), f32),
            ((1024, 1024), bf16),
            ((1024, 16), bf16),
            ((16, 128, 128), bf16),
            ((1024, 128), bf16),
            ((1, 1024), f32),
            ((1, 1024), f32),
            ((16, 128), bf16),
            ((16, 128), bf16),
        ],
        name="mixer_forward",
        spare=10,
        us=10.0,
    )
    send = after(send, *cot_near[1:], gu_parts[2], gu_parts[3])
    sums = sum_cores(keep, send)
    shares = cross_chips(*sums)
    gu_parts[1] = flip(gu_parts[1], 0, 1)
    gu_parts = halves_from_next_plane(gu_parts)
    cots = gather_cores(cot_near)
    residual, feed = call(
        residual_kernel,
        (),
        (after(own, *gu_parts), gain_two, *shares),
        [(block, f32), (block, bf16)],
        name="residual",
    )
    feeds = gather_cores(gather_chips(feed))
    send_g, keep_g, send_d, keep_d, active, dgu = call(
        feed_kernel,
        (idx,),
        (*feeds, *cots, *gu_parts, w_down),
        [
            quad,
            quad,
            quad,
            quad,
            ((1024, HIDDEN_PAD), bf16),
            ((1024, 2 * HIDDEN_PAD), bf16),
        ],
        scratch=[((1024, 2 * HIDDEN_PAD), bf16), ((HIDDEN_PAD, 1024), bf16)],
        name="feed",
        spare=10,
        us=7.5,
    )
    feed_keep, feed_later_keep, feed_send, feed_later_send = call(
        feed_weights_kernel,
        (idx,),
        (dgu, active, *feeds, *cots),
        [((2, 256 + 4 * Z_HIDDEN // 3, HIDDEN_PAD), bf16)] * 4,
        scratch=[
            ((256, 768), f32),
            ((HIDDEN_PAD, 1024), f32),
            ((1024, 1024), bf16),
            ((1024, 1024), bf16),
            ((256 + 4 * Z_HIDDEN // 3, 768), bf16),
        ],
        name="feed_weights",
        spare=10,
        us=3.5,
    )
    sums = sum_cores(after(keep_g, feed_send), send_g)
    send_d = after(send_d, sums[0])
    shares = cross_chips(*sums)
    feed_received = flip_z(feed_send, 1)
    feed_later_received = flip_z(after(feed_later_send, sums[0]), 1)
    grad_residual, branch = call(
        branch_kernel,
        (),
        (residual, gain_two, own_cot, *shares),
        [(block, f32), (block, bf16)],
        name="branch",
    )
    feed_own, feed_passed = half_sum(after(feed_keep, branch), feed_received, "feed")
    branch_near = gather_chips(branch, after(branch, feed_passed))
    keep_d = after(keep_d, feed_passed)
    out_sums = sum_cores(keep_d, send_d)
    feed_moved = flip_z(feed_passed, 2)
    branches = gather_cores([after(piece, feed_moved) for piece in branch_near])
    feed_later, feed_later_passed = half_sum(
        after(feed_later_keep, out_sums[0]), feed_later_received, "feed_later"
    )
    rates = after(rates, feed_later_passed)
    feed_later_moved = flip_z(feed_later_passed, 2)
    out_sums = lax.optimization_barrier((*out_sums, branches[6]))[:4]
    out_shares = cross_chips(*out_sums)

    send, keep, dqkvg, branch_all = call(
        mixer_backward_kernel,
        (idx, rates),
        (*branches, w_out, w_full, qkv, gate, att, rec, probs, pprobs, states, pk, pv),
        [
            ((4, 128 + EXTRA, 1024), bf16),
            ((4, 128 + EXTRA, 1024), bf16),
            ((1024, 512), bf16),
            ((1024, 1024), bf16),
        ],
        scratch=[
            ((1024, 128), bf16),
            ((1024, 128), bf16),
            ((1024, 128), f32),
            ((1024, 1024), bf16),
            ((1024, 128), f32),
            ((1024, 128), f32),
            ((1024, 16), bf16),
        ],
        name="mixer_backward",
        spare=10,
        us=13.0,
    )
    send, dqkvg = lax.optimization_barrier(
        (send, dqkvg, feed_later_moved, *out_shares[1:])
    )[:2]
    *feed_parts, feed_rest = whole_sum(
        (after(feed_own, send), feed_later), (feed_moved, feed_later_moved), "feed"
    )
    feed_parts = hand_rows(feed_parts)
    dqkvg = after(dqkvg, feed_rest)
    mixer_keep, mixer_send = call(
        mixer_weights_kernel,
        (idx,),
        (normed, dqkvg, mixed, branch_all),
        [((2, 320, 512), bf16)] * 2,
        scratch=[((256, 512), f32), ((128, 1024), f32)],
        name="mixer_weights",
        spare=10,
        us=2.2,
    )
    (result,) = call(output_kernel, (), (residual, *out_shares), [(block, bf16)], name="output")
    result = to_plane(after(result, mixer_send))
    feed_joined = join(feed_parts, after(feed_rest, mixer_send), "feed")
    feed_second, feed_first = spread_far(feed_joined)
    feed_beside = flip(feed_joined, 1, 0)
    rows = (128 + EXTRA, 1024)
    keep_far, keep_near, send_far = call(
        tokens_sum_kernel,
        (),
        (after(keep, feed_joined), flip(send, 0, 1)),
        [(rows, f32), (rows, f32), ((2, *rows), bf16)],
        name="tokens_sum",
    )
    mixer_own, mixer_passed = half_sum(
        after(mixer_keep, keep_near, result), flip_z(mixer_send, 1), "mixer"
    )
    mixer_moved = flip_z(mixer_passed, 2)
    tokens_far = flip(after(send_far, mixer_passed), 1, 0)
    feed_first_beside = flip(after(feed_first, feed_beside), 1, 0)
    mixer_own = after(mixer_own, feed_second, feed_first_beside, tokens_far)
    *mixer_parts, mixer_rest = whole_sum((mixer_own,), (mixer_moved,), "mixer")
    feed_third = flip_z(after(feed_second, mixer_rest), 1)
    feed_second_beside = flip(after(feed_second, mixer_rest), 1, 0)
    mixer_joined = join(hand_rows(mixer_parts), mixer_rest, "mixer")
    mixer_second, mixer_first = spread_far(mixer_joined)
    mixer_beside = flip(mixer_joined, 1, 0)
    feed_third_beside = flip(after(feed_third, mixer_joined), 1, 0)
    tokens_own, tokens_passed = call(
        far_kernel,
        (),
        (after(keep_far, mixer_joined), keep_near, tokens_far),
        [((128 + EXTRA, 1024), f32), ((128 + EXTRA, 1024), bf16)],
        name="tokens_far",
    )
    tokens_near = flip(tokens_passed, 0, 2)
    mixer_second = after(
        mixer_second,
        mixer_first,
        mixer_beside,
        feed_second_beside,
        feed_third_beside,
        tokens_near,
    )
    mixer_third = flip_z(mixer_second, 1)
    mixer_first_beside = flip(after(mixer_first, mixer_second), 1, 0)
    mixer_second_beside = flip(mixer_second, 1, 0)
    grad_tokens, persist = call(
        tokens_kernel,
        (),
        (after(own, mixer_second), gain_one, grad_residual, tokens_own, tokens_near),
        [(block, bf16), ((8, 1024), f32)],
        name="tokens",
    )
    grad_tokens = to_plane(grad_tokens)
    persist = persist + flip_z(persist, 1)
    feed_pieces = (
        feed_joined,
        feed_beside,
        feed_first,
        feed_first_beside,
        feed_second,
        feed_second_beside,
        feed_third,
        feed_third_beside,
    )

    grad_gu, grad_down, grad_ffn = call(
        feed_unpack_kernel,
        (idx,),
        (*feed_pieces, w_gu, after(ffn_gain.reshape(1, 256), mixer_second)),
        [((256, 2 * FF), f32), ((FF // 4, 1024), f32), ((1, 256), f32)],
        scratch=[((4, 8, 64, 768), bf16)],
        name="feed_unpack",
        spare=10,
        us=5.5,
    )
    mixer_third_beside = flip(
        after(mixer_third, grad_ffn, mixer_first_beside, mixer_second_beside, persist), 1, 0
    )
    persist = persist + flip_z(persist, 2)
    mixer_pieces = (
        mixer_joined,
        mixer_beside,
        mixer_first,
        mixer_first_beside,
        mixer_second,
        mixer_second_beside,
        mixer_third,
        mixer_third_beside,
    )
    grad_qkv, grad_gate, grad_out, grad_norm = call(
        mixer_unpack_kernel,
        (idx,),
        (*mixer_pieces, w_qkv, w_gate, norm_gain.reshape(1, 256)),
        [
            ((256, 3072), f32),
            ((256, 1024), f32),
            ((256, 1024), f32),
            ((1, 256), f32),
        ],
        name="mixer_unpack",
    )
    return (
        result[None],
        grad_tokens.astype(f32)[None],
        grad_qkv,
        grad_gate,
        grad_out,
        grad_gu,
        grad_down,
        persist[0:4],
        persist[4:8],
        grad_norm.reshape(256),
        grad_ffn.reshape(256),
    )


def solution(mesh):
    in_specs = (
        P("fsdp", "ctx", None),
        P("fsdp", "ctx", None),
        P("fsdp", None),
        P("fsdp", None, None),
        P("fsdp", None, None),
        P("fsdp", None),
        P("fsdp", None),
        P("fsdp", None),
        P("fsdp", None),
        P("fsdp", None),
        P("fsdp", None),
        P("fsdp", None),
        P("fsdp"),
        P("fsdp"),
    )
    out_specs = (
        P("fsdp", "ctx", None),
        P("fsdp", "ctx", None),
        P("fsdp", None),
        P("fsdp", None),
        P("fsdp", None),
        P("fsdp", None),
        P("fsdp", None),
        P("fsdp", None),
        P("fsdp", None),
        P("fsdp"),
        P("fsdp"),
    )
    planes = dict(mesh.shape) == {"ctx": HEADS, "fsdp": PLANES}
    return jax.shard_map(
        in_planes if planes else on_device, mesh=mesh, in_specs=in_specs, out_specs=out_specs, check_vma=False
    )
```

```python
import functools

import jax
import jax.numpy as jnp
import numpy as np
from jax import lax
from jax.experimental import pallas as pl
from jax.experimental.pallas import tpu as pltpu
from jax.sharding import PartitionSpec as P

HEADS = 8
HEAD_WIDTH_SIZE = 128
FF = 2816
GROUP = 64


epsilon = 1e-06
momentum = 0.9
masked_score = -1e30
highest_precision = lax.Precision.HIGHEST


def rms_scale(values):
    return lax.rsqrt(jnp.mean(values * values, axis=-1, keepdims=True) + epsilon)


def norm_back(values, inv_rms, gain_vec, grad_normed):
    scaled_grad = grad_normed * gain_vec
    grad_gain = jnp.sum(grad_normed * values * inv_rms, axis=0)
    grad_values = inv_rms * scaled_grad - values * inv_rms * inv_rms * inv_rms * jnp.mean(
        scaled_grad * values, axis=-1, keepdims=True
    )
    return (grad_values, grad_gain)


def place_rows(row_index, shard_rows, dev_count):
    half_rows = shard_rows // 2
    owner_dev = row_index // shard_rows
    inner_row = row_index % shard_rows
    block_id = jnp.where(inner_row < half_rows, owner_dev, 2 * dev_count - 1 - owner_dev)
    return block_id * half_rows + inner_row % half_rows


def position_order(stored, dev_count):
    rows = stored.shape[0]
    rest = stored.shape[1:]
    split = stored.reshape((dev_count, 2, rows // (2 * dev_count)) + rest)
    early = split[:, 0].reshape((-1,) + rest)
    late = split[::-1, 1].reshape((-1,) + rest)
    return jnp.concatenate([early, late], axis=0)


def key_mask(query_pos, query_seg, key_pos, key_seg):
    return (key_seg[None, :] == query_seg[:, None]) & (key_pos[None, :] <= query_pos[:, None])


def head_scores(queries, key_block):
    return jnp.einsum(
        "qhd,khd->hqk", queries, key_block, preferred_element_type=jnp.float32
    ) * HEAD_WIDTH_SIZE ** (-0.5)


def online_step(running, scores, value_block):
    run_max, run_total, accumulated = running
    new_max = jnp.maximum(run_max, jnp.max(scores, axis=-1))
    rescale = jnp.exp(run_max - new_max)
    weights = jnp.exp(scores - new_max[:, :, None])
    run_total = run_total * rescale + jnp.sum(weights, axis=-1)
    update = jnp.einsum(
        "hqk,khd->qhd",
        weights.astype(jnp.bfloat16),
        value_block,
        preferred_element_type=jnp.float32,
    )
    accumulated = accumulated * jnp.transpose(rescale)[:, :, None] + update
    return (new_max, run_total, accumulated)


def fold_keys(running, all_keys, all_values, context):
    queries, query_pos, query_seg, segment_all, shard_rows, dev_count = context
    total_rows = all_keys.shape[0]
    block_rows = min(512, total_rows)

    def fold_one_block(carried, block_index):
        offset_row = block_index * block_rows
        key_block = lax.dynamic_slice_in_dim(all_keys, offset_row, block_rows, 0).reshape(
            block_rows, HEADS, HEAD_WIDTH_SIZE
        )
        value_block = lax.dynamic_slice_in_dim(all_values, offset_row, block_rows, 0).reshape(
            block_rows, HEADS, HEAD_WIDTH_SIZE
        )
        key_pos = place_rows(
            offset_row + jnp.arange(block_rows, dtype=jnp.int32), shard_rows, dev_count
        )
        key_seg = jnp.take(segment_all, key_pos)
        allowed = key_mask(query_pos, query_seg, key_pos, key_seg)
        scores = jnp.where(allowed[None], head_scores(queries, key_block), masked_score)
        carried = online_step(carried, scores, value_block)
        return (carried, None)

    running, _ = lax.scan(
        fold_one_block, running, jnp.arange(total_rows // block_rows, dtype=jnp.int32)
    )
    return running


def back_every_key(grad_query, all_keys, all_values, context, grad_heads, log_total, row_delta):
    queries, query_pos, query_seg, segment_all, shard_rows, dev_count = context
    total_rows = all_keys.shape[0]
    block_rows = min(512, total_rows)
    scale_factor = HEAD_WIDTH_SIZE ** (-0.5)

    def back_one_block(carried, block_index):
        offset_row = block_index * block_rows
        key_block = lax.dynamic_slice_in_dim(all_keys, offset_row, block_rows, 0).reshape(
            block_rows, HEADS, HEAD_WIDTH_SIZE
        )
        value_block = lax.dynamic_slice_in_dim(all_values, offset_row, block_rows, 0).reshape(
            block_rows, HEADS, HEAD_WIDTH_SIZE
        )
        key_pos = place_rows(
            offset_row + jnp.arange(block_rows, dtype=jnp.int32), shard_rows, dev_count
        )
        key_seg = jnp.take(segment_all, key_pos)
        allowed = key_mask(query_pos, query_seg, key_pos, key_seg)
        scores = jnp.where(allowed[None], head_scores(queries, key_block), masked_score)
        prob_block = jnp.exp(scores - log_total[:, :, None])
        grad_prob = jnp.einsum(
            "qhd,khd->hqk", grad_heads, value_block, preferred_element_type=jnp.float32
        )
        grad_scores = (prob_block * (grad_prob - row_delta[:, :, None])).astype(jnp.bfloat16)
        query_grad = (
            carried
            + jnp.einsum("hqk,khd->qhd", grad_scores, key_block, preferred_element_type=jnp.float32)
            * scale_factor
        )
        key_grad = (
            jnp.einsum("hqk,qhd->khd", grad_scores, queries, preferred_element_type=jnp.float32)
            * scale_factor
        )
        value_grad = jnp.einsum(
            "hqk,qhd->khd",
            prob_block.astype(jnp.bfloat16),
            grad_heads,
            preferred_element_type=jnp.float32,
        )
        return (query_grad, (key_grad, value_grad))

    grad_query, (key_grads, value_grads) = lax.scan(
        back_one_block, grad_query, jnp.arange(total_rows // block_rows, dtype=jnp.int32)
    )
    return (
        grad_query,
        key_grads.reshape(total_rows, HEADS, HEAD_WIDTH_SIZE),
        value_grads.reshape(total_rows, HEADS, HEAD_WIDTH_SIZE),
    )


def group_step(stacked_rows, group_key_rows, group_value_rows, alpha_row, learning_rate_row):
    current_memory = stacked_rows[:, :HEAD_WIDTH_SIZE]
    moment_now = stacked_rows[:, HEAD_WIDTH_SIZE:]
    gram_matrix = (
        jnp.einsum("thk,thj->hkj", group_key_rows, group_key_rows, precision=highest_precision)
        * learning_rate_row[:, None, None]
    )
    mixed_product = (
        jnp.einsum("qgw,qgc->gwc", group_key_rows, group_value_rows, precision=highest_precision)
        * learning_rate_row[:, None, None]
    )
    memory_gradient = (
        jnp.einsum("fld,fdi->fli", gram_matrix, current_memory, precision=highest_precision)
        - mixed_product
    )
    moment_next = momentum * moment_now - memory_gradient
    memory_next = (1.0 - alpha_row)[:, None, None] * current_memory + moment_next
    return jnp.concatenate([memory_next, moment_next], axis=1)


def run_block(stacked_rows, query_part, key_part, value_part, alphas, thetas):
    scale_factor = HEAD_WIDTH_SIZE ** (-0.5)
    group_query_rows = query_part * scale_factor
    recalled_rows = [
        jnp.einsum(
            "ipb,pbx->ipx",
            group_query_rows,
            stacked_rows[:, :HEAD_WIDTH_SIZE],
            precision=highest_precision,
        )
    ]
    stacked_rows = group_step(
        stacked_rows, key_part * scale_factor, value_part, alphas[0], thetas[0]
    )
    return (jnp.concatenate(recalled_rows, axis=0), stacked_rows)


def states_before(key_order, value_order, alpha_all, theta_all, early_index, late_index):
    groups = alpha_all.shape[0]
    scale_factor = HEAD_WIDTH_SIZE ** (-0.5)
    key_groups = key_order.reshape(groups, GROUP, HEADS, HEAD_WIDTH_SIZE)
    value_groups = value_order.reshape(groups, GROUP, HEADS, HEAD_WIDTH_SIZE)
    zero_state = jnp.zeros((HEADS, 2 * HEAD_WIDTH_SIZE, HEAD_WIDTH_SIZE), jnp.float32)

    def states_one_group(carried, inputs):
        stacked_rows, into_early, into_late = carried
        group_key_rows, group_value_rows, alpha_row, learning_rate_row, group_index = inputs
        into_early = jnp.where(group_index == early_index, stacked_rows, into_early)
        into_late = jnp.where(group_index == late_index, stacked_rows, into_late)
        current_memory = stacked_rows[:, :HEAD_WIDTH_SIZE]
        moment_now = stacked_rows[:, HEAD_WIDTH_SIZE:]
        gram_matrix = (
            jnp.einsum(
                "thk,thj->hkj", group_key_rows, group_key_rows, preferred_element_type=jnp.float32
            )
            * (learning_rate_row / HEAD_WIDTH_SIZE)[:, None, None]
        )
        mixed_product = (
            jnp.einsum(
                "qgw,qgc->gwc", group_key_rows, group_value_rows, preferred_element_type=jnp.float32
            )
            * (learning_rate_row * scale_factor)[:, None, None]
        )
        memory_gradient = (
            jnp.einsum("fld,fdi->fli", gram_matrix, current_memory, precision=highest_precision)
            - mixed_product
        )
        moment_next = momentum * moment_now - memory_gradient
        memory_next = (1.0 - alpha_row)[:, None, None] * current_memory + moment_next
        stacked_rows = jnp.concatenate([memory_next, moment_next], axis=1)
        return ((stacked_rows, into_early, into_late), None)

    (_, into_early, into_late), _ = lax.scan(
        states_one_group,
        (zero_state, zero_state, zero_state),
        (key_groups, value_groups, alpha_all, theta_all, jnp.arange(groups, dtype=jnp.int32)),
    )
    return (into_early, into_late)


def adjoints_after(
    query_order, key_order, recall_grad_order, alpha_all, theta_all, early_end, late_end
):
    groups = alpha_all.shape[0]
    scale_factor = HEAD_WIDTH_SIZE ** (-0.5)
    query_groups = query_order.reshape(groups, GROUP, HEADS, HEAD_WIDTH_SIZE)
    key_groups = key_order.reshape(groups, GROUP, HEADS, HEAD_WIDTH_SIZE)
    grad_groups = recall_grad_order.reshape(groups, GROUP, HEADS, HEAD_WIDTH_SIZE)
    zero_state = jnp.zeros((HEADS, 2 * HEAD_WIDTH_SIZE, HEAD_WIDTH_SIZE), jnp.float32)

    def adjoints_one_group(carried, inputs):
        adjoint, out_early, out_late = carried
        (
            group_query_rows,
            group_key_rows,
            gradient_group_rows,
            alpha_row,
            learning_rate_row,
            group_index,
        ) = inputs
        out_early = jnp.where(group_index + 1 == early_end, adjoint, out_early)
        out_late = jnp.where(group_index + 1 == late_end, adjoint, out_late)
        gram_matrix = (
            jnp.einsum(
                "thk,thj->hkj", group_key_rows, group_key_rows, preferred_element_type=jnp.float32
            )
            * (learning_rate_row / HEAD_WIDTH_SIZE)[:, None, None]
        )
        query_term = (
            jnp.einsum(
                "qgw,qgc->gwc",
                group_query_rows,
                gradient_group_rows,
                preferred_element_type=jnp.float32,
            )
            * scale_factor
        )
        grad_m = adjoint[:, :HEAD_WIDTH_SIZE]
        summed_rows = grad_m + adjoint[:, HEAD_WIDTH_SIZE:]
        new_m = (
            (1.0 - alpha_row)[:, None, None] * grad_m
            + query_term
            - jnp.einsum("fld,fdi->fli", gram_matrix, summed_rows, precision=highest_precision)
        )
        adjoint = jnp.concatenate([new_m, momentum * summed_rows], axis=1)
        return ((adjoint, out_early, out_late), None)

    (_, out_early, out_late), _ = lax.scan(
        adjoints_one_group,
        (zero_state, zero_state, zero_state),
        (
            query_groups,
            key_groups,
            grad_groups,
            alpha_all,
            theta_all,
            jnp.arange(groups, dtype=jnp.int32),
        ),
        reverse=True,
    )
    return (out_early, out_late)


def on_device(
    tokens,
    cotangent,
    segments,
    decay_index,
    step_index,
    w_qkv,
    w_gate,
    w_out,
    w_gu,
    w_down,
    persist_keys,
    persist_values,
    norm_gain,
    ffn_gain,
):
    shard_rows = tokens.shape[1]
    model_width = tokens.shape[2]
    half_rows = shard_rows // 2
    dev_count = lax.axis_size("ctx")
    device = lax.axis_index("ctx")
    scale_factor = HEAD_WIDTH_SIZE ** (-0.5)
    full_weights = (
        lax.all_gather(w_qkv, "fsdp", axis=0, tiled=True),
        lax.all_gather(w_gate, "fsdp", axis=0, tiled=True),
        lax.all_gather(w_out, "fsdp", axis=0, tiled=True),
        lax.all_gather(w_gu, "fsdp", axis=0, tiled=True),
        lax.all_gather(w_down, "fsdp", axis=0, tiled=True),
        lax.all_gather(persist_keys, "fsdp", axis=0, tiled=True),
        lax.all_gather(persist_values, "fsdp", axis=0, tiled=True),
        lax.all_gather(norm_gain, "fsdp", axis=0, tiled=True),
        lax.all_gather(ffn_gain, "fsdp", axis=0, tiled=True),
    )
    wq_full, wg_full, wo_full, wgu_full, wd_full, pkeys_full, pvalues_full, gain_attn, gain_ffn = (
        full_weights
    )
    gain_attn32 = gain_attn.astype(jnp.float32)
    gain_ffn32 = gain_ffn.astype(jnp.float32)
    pkeys_heads = pkeys_full.reshape(-1, HEADS, HEAD_WIDTH_SIZE)
    pvalues_heads = pvalues_full.reshape(-1, HEADS, HEAD_WIDTH_SIZE)
    inputs32 = tokens[0].astype(jnp.float32)
    inv_rms_one = rms_scale(inputs32)
    normed_low = (inputs32 * inv_rms_one * gain_attn32).astype(jnp.bfloat16)
    projected = jnp.dot(normed_low, wq_full, preferred_element_type=jnp.float32)
    query_flat = projected[:, :model_width].astype(jnp.bfloat16)
    key_flat = projected[:, model_width : 2 * model_width].astype(jnp.bfloat16)
    value_flat = projected[:, 2 * model_width :].astype(jnp.bfloat16)
    query_heads = query_flat.reshape(shard_rows, HEADS, HEAD_WIDTH_SIZE)
    gate_open = jax.nn.sigmoid(jnp.dot(normed_low, wg_full, preferred_element_type=jnp.float32))
    local_rows = jnp.arange(shard_rows, dtype=jnp.int32)
    query_pos = place_rows(device * shard_rows + local_rows, shard_rows, dev_count)
    segment_all = segments[0]
    query_seg = jnp.take(segment_all, query_pos)
    context = (query_heads, query_pos, query_seg, segment_all, shard_rows, dev_count)
    all_keys, all_values = (
        lax.all_gather(key_flat, "ctx", axis=0, tiled=True),
        lax.all_gather(value_flat, "ctx", axis=0, tiled=True),
    )
    persist_scores = head_scores(query_heads, pkeys_heads)
    start_state = (
        jnp.full((HEADS, shard_rows), masked_score, jnp.float32),
        jnp.zeros((HEADS, shard_rows), jnp.float32),
        jnp.zeros((shard_rows, HEADS, HEAD_WIDTH_SIZE), jnp.float32),
    )
    running = online_step(start_state, persist_scores, pvalues_heads)
    running = fold_keys(running, all_keys, all_values, context)
    run_max, run_total, accumulated = running
    attended = accumulated / jnp.transpose(run_total)[:, :, None]
    log_total = run_max + jnp.log(run_total)
    group_count = half_rows // GROUP
    alpha_all = 0.6 * jnp.exp2(-decay_index[0].astype(jnp.float32))
    theta_all = 0.1 * jnp.exp2(-step_index[0].astype(jnp.float32))
    early_first = device * group_count
    late_first = (2 * dev_count - 1 - device) * group_count
    alpha_early = lax.dynamic_slice_in_dim(alpha_all, early_first, group_count, 0)
    theta_early = lax.dynamic_slice_in_dim(theta_all, early_first, group_count, 0)
    alpha_late = lax.dynamic_slice_in_dim(alpha_all, late_first, group_count, 0)
    theta_late = lax.dynamic_slice_in_dim(theta_all, late_first, group_count, 0)
    query_f = query_heads.astype(jnp.float32)
    key_f = key_flat.astype(jnp.float32).reshape(shard_rows, HEADS, HEAD_WIDTH_SIZE)
    value_f = value_flat.astype(jnp.float32).reshape(shard_rows, HEADS, HEAD_WIDTH_SIZE)
    early_parts = (query_f[:half_rows], key_f[:half_rows], value_f[:half_rows])
    late_parts = (query_f[half_rows:], key_f[half_rows:], value_f[half_rows:])

    def early_run(stacked_rows, query_part, key_part, value_part):
        return run_block(stacked_rows, query_part, key_part, value_part, alpha_early, theta_early)

    def late_run(stacked_rows, query_part, key_part, value_part):
        return run_block(stacked_rows, query_part, key_part, value_part, alpha_late, theta_late)

    into_early, into_late = states_before(
        position_order(all_keys, dev_count),
        position_order(all_values, dev_count),
        alpha_all,
        theta_all,
        early_first,
        late_first,
    )
    recall_early, _ = early_run(into_early, early_parts[0], early_parts[1], early_parts[2])
    recall_late, _ = late_run(into_late, late_parts[0], late_parts[1], late_parts[2])
    recall = jnp.concatenate([recall_early, recall_late], axis=0).reshape(shard_rows, model_width)
    mixed_low = (attended.reshape(shard_rows, model_width) + gate_open * recall).astype(
        jnp.bfloat16
    )
    residual = inputs32 + jnp.dot(mixed_low, wo_full, preferred_element_type=jnp.float32)
    inv_rms_two = rms_scale(residual)
    normed_two = (residual * inv_rms_two * gain_ffn32).astype(jnp.bfloat16)
    gate_up = jnp.dot(normed_two, wgu_full, preferred_element_type=jnp.float32)
    gate_part = gate_up[:, :FF]
    up_part = gate_up[:, FF:]
    active = (jax.nn.silu(gate_part) * up_part).astype(jnp.bfloat16)
    result = residual + jnp.dot(active, wd_full, preferred_element_type=jnp.float32)
    cot_low = cotangent[0]
    grad_w_down = jnp.einsum("tf,td->fd", active, cot_low, preferred_element_type=jnp.float32)
    grad_active = jnp.einsum("td,fd->tf", cot_low, wd_full, preferred_element_type=jnp.float32)
    sigma_gate = jax.nn.sigmoid(gate_part)
    grad_gate_part = grad_active * up_part * sigma_gate * (1.0 + gate_part * (1.0 - sigma_gate))
    grad_up_part = grad_active * gate_part * sigma_gate
    grad_gu_low = jnp.concatenate([grad_gate_part, grad_up_part], axis=1).astype(jnp.bfloat16)
    grad_w_gu = jnp.einsum("td,tf->df", normed_two, grad_gu_low, preferred_element_type=jnp.float32)
    grad_normed_two = jnp.einsum(
        "tf,df->td", grad_gu_low, wgu_full, preferred_element_type=jnp.float32
    )
    grad_res_norm, grad_ffn_gain = norm_back(residual, inv_rms_two, gain_ffn32, grad_normed_two)
    grad_residual = cot_low.astype(jnp.float32) + grad_res_norm
    grad_branch = grad_residual.astype(jnp.bfloat16)
    grad_w_out = jnp.einsum("td,te->de", mixed_low, grad_branch, preferred_element_type=jnp.float32)
    grad_mixed_low = jnp.einsum(
        "te,de->td", grad_branch, wo_full, preferred_element_type=jnp.float32
    ).astype(jnp.bfloat16)
    grad_mixed32 = grad_mixed_low.astype(jnp.float32)
    grad_gate_low = (grad_mixed32 * recall * gate_open * (1.0 - gate_open)).astype(jnp.bfloat16)
    grad_w_gate = jnp.einsum(
        "td,tf->df", normed_low, grad_gate_low, preferred_element_type=jnp.float32
    )
    recall_grad_low = (grad_mixed32 * gate_open).astype(jnp.bfloat16)
    grad_recall = recall_grad_low.astype(jnp.float32).reshape(shard_rows, HEADS, HEAD_WIDTH_SIZE)
    grad_heads = grad_mixed_low.reshape(shard_rows, HEADS, HEAD_WIDTH_SIZE)
    row_delta = jnp.transpose(jnp.sum(grad_heads.astype(jnp.float32) * attended, axis=-1))
    memory_queries, all_recall_grads = (
        lax.all_gather(query_flat, "ctx", axis=0, tiled=True),
        lax.all_gather(recall_grad_low, "ctx", axis=0, tiled=True),
    )
    out_early, out_late = adjoints_after(
        position_order(memory_queries, dev_count),
        position_order(all_keys, dev_count),
        position_order(all_recall_grads, dev_count),
        alpha_all,
        theta_all,
        early_first + group_count,
        late_first + group_count,
    )
    _, pull_early = jax.vjp(early_run, into_early, early_parts[0], early_parts[1], early_parts[2])
    _, grad_qe, grad_ke, grad_ve = pull_early((grad_recall[:half_rows], out_early))
    _, pull_late = jax.vjp(late_run, into_late, late_parts[0], late_parts[1], late_parts[2])
    _, grad_ql, grad_kl, grad_vl = pull_late((grad_recall[half_rows:], out_late))
    grad_q_mem = jnp.concatenate([grad_qe, grad_ql], axis=0).reshape(shard_rows, model_width)
    grad_k_mem = jnp.concatenate([grad_ke, grad_kl], axis=0).reshape(shard_rows, model_width)
    grad_v_mem = jnp.concatenate([grad_ve, grad_vl], axis=0).reshape(shard_rows, model_width)
    persist_probs = jnp.exp(persist_scores - log_total[:, :, None])
    persist_grad_prob = jnp.einsum(
        "qhd,phd->hqp", grad_heads, pvalues_heads, preferred_element_type=jnp.float32
    )
    persist_ds = (persist_probs * (persist_grad_prob - row_delta[:, :, None])).astype(jnp.bfloat16)
    grad_query_att = (
        jnp.einsum("hqp,phd->qhd", persist_ds, pkeys_heads, preferred_element_type=jnp.float32)
        * scale_factor
    )
    grad_pkeys = (
        jnp.einsum("hqp,qhd->phd", persist_ds, query_heads, preferred_element_type=jnp.float32)
        * scale_factor
    )
    grad_pvalues = jnp.einsum(
        "hqp,qhd->phd",
        persist_probs.astype(jnp.bfloat16),
        grad_heads,
        preferred_element_type=jnp.float32,
    )
    grad_query_att, key_grads_all, value_grads_all = back_every_key(
        grad_query_att, all_keys, all_values, context, grad_heads, log_total, row_delta
    )
    key_grad_att, value_grad_att = (
        lax.psum_scatter(key_grads_all, "ctx", scatter_dimension=0, tiled=True),
        lax.psum_scatter(value_grads_all, "ctx", scatter_dimension=0, tiled=True),
    )
    grad_query = grad_query_att.reshape(shard_rows, model_width) + grad_q_mem
    grad_key = key_grad_att.reshape(shard_rows, model_width) + grad_k_mem
    grad_value = value_grad_att.reshape(shard_rows, model_width) + grad_v_mem
    grad_qkv_low = jnp.concatenate([grad_query, grad_key, grad_value], axis=1).astype(jnp.bfloat16)
    grad_w_qkv = jnp.einsum(
        "td,tf->df", normed_low, grad_qkv_low, preferred_element_type=jnp.float32
    )
    grad_normed = jnp.einsum(
        "tf,df->td", grad_qkv_low, wq_full, preferred_element_type=jnp.float32
    ) + jnp.einsum("tf,df->td", grad_gate_low, wg_full, preferred_element_type=jnp.float32)
    grad_in_norm, grad_norm_gain = norm_back(inputs32, inv_rms_one, gain_attn32, grad_normed)
    grad_inputs = grad_residual + grad_in_norm
    local_grads = (
        grad_w_qkv,
        grad_w_gate,
        grad_w_out,
        grad_w_gu,
        grad_w_down,
        grad_pkeys.reshape(-1, model_width),
        grad_pvalues.reshape(-1, model_width),
        grad_norm_gain,
        grad_ffn_gain,
    )
    shares = (
        lax.psum_scatter(
            local_grads[0].astype(jnp.bfloat16), "fsdp", scatter_dimension=0, tiled=True
        ).astype(jnp.float32),
        lax.psum_scatter(
            local_grads[1].astype(jnp.bfloat16), "fsdp", scatter_dimension=0, tiled=True
        ).astype(jnp.float32),
        lax.psum_scatter(
            local_grads[2].astype(jnp.bfloat16), "fsdp", scatter_dimension=0, tiled=True
        ).astype(jnp.float32),
        lax.psum_scatter(
            local_grads[3].astype(jnp.bfloat16), "fsdp", scatter_dimension=0, tiled=True
        ).astype(jnp.float32),
        lax.psum_scatter(
            local_grads[4].astype(jnp.bfloat16), "fsdp", scatter_dimension=0, tiled=True
        ).astype(jnp.float32),
        lax.psum_scatter(
            local_grads[5].astype(jnp.bfloat16), "fsdp", scatter_dimension=0, tiled=True
        ).astype(jnp.float32),
        lax.psum_scatter(
            local_grads[6].astype(jnp.bfloat16), "fsdp", scatter_dimension=0, tiled=True
        ).astype(jnp.float32),
        lax.psum_scatter(
            local_grads[7].astype(jnp.bfloat16), "fsdp", scatter_dimension=0, tiled=True
        ).astype(jnp.float32),
        lax.psum_scatter(
            local_grads[8].astype(jnp.bfloat16), "fsdp", scatter_dimension=0, tiled=True
        ).astype(jnp.float32),
    )
    totals = lax.psum(
        (
            shares[0],
            shares[1],
            shares[2],
            shares[3],
            shares[4],
            shares[5],
            shares[6],
            shares[7],
            shares[8],
        ),
        "ctx",
    )
    return (
        result.astype(jnp.bfloat16)[None],
        grad_inputs[None],
        totals[0],
        totals[1],
        totals[2],
        totals[3],
        totals[4],
        totals[5],
        totals[6],
        totals[7],
        totals[8],
    )


PERSIST = 16
PLANES = 4
HIDDEN_PAD = 384
Z_HIDDEN = HIDDEN_PAD // PLANES
EXTRA = 16


def head_of(x, f, k):
    return 2 * (f ^ (k & 3)) + (x ^ (k >> 2))


def linear(z, x, f):
    return (2 * z + x) * 4 + f


def shift(value, move):
    pairs = []
    for z in range(4):
        for x in range(2):
            for f in range(4):
                pairs.append((linear(z, x, f), linear(*move(z, x, f))))
    return lax.ppermute(value, ("ctx", "fsdp"), pairs)


def to_plane(value):
    return shift(value, lambda z, x, f: (f, x, z))


def flip(value, dx, df):
    return shift(value, lambda z, x, f: (z, x ^ dx, f ^ df))


def flip_z(value, dz):
    return shift(value, lambda z, x, f: (z ^ dz, x, f))


def gather_chips(block, last=None):
    last = block if last is None else last
    return [block, flip(block, 0, 2), flip(block, 1, 0), flip(last, 1, 2)]


def gather_cores(near):
    far = [flip(b, 0, 1) for b in near]
    return [near[0], far[0], near[1], far[1], near[2], far[2], near[3], far[3]]


def dot_nn(a, b):
    return lax.dot_general(a, b, (((1,), (0,)), ((), ())), preferred_element_type=jnp.float32)


def dot_nt(a, b):
    return lax.dot_general(a, b, (((1,), (1,)), ((), ())), preferred_element_type=jnp.float32)


def dot_tn(a, b):
    return lax.dot_general(a, b, (((0,), (0,)), ((), ())), preferred_element_type=jnp.float32)


def split_two(value):
    high = value.astype(jnp.bfloat16)
    return high, (value - high.astype(jnp.float32)).astype(jnp.bfloat16)


def product_three(a, b_high, b_low):
    a_high, a_low = split_two(a)
    return dot_nn(a_high, b_high) + dot_nn(a_low, b_high) + dot_nn(a_high, b_low)


def vspec():
    return pl.BlockSpec(memory_space=pltpu.VMEM)


def sspec():
    return pl.BlockSpec(memory_space=pltpu.SMEM)


def padded_bytes(shape, dtype):
    size = jnp.dtype(dtype).itemsize
    lanes = -(-shape[-1] // 128) * 128
    rows = -(-shape[-2] // (32 // size)) * (32 // size)
    return int(np.prod(shape[:-2])) * rows * lanes * size


def call(kernel, smem, operands, outs, scratch=(), name=None, spare=6, us=0.5):
    held = [(o.shape, o.dtype) for o in operands] + list(outs) + list(scratch)
    limit = sum(padded_bytes(shape, dtype) for shape, dtype in held) + spare * 1024 * 1024
    return pl.pallas_call(
        kernel,
        out_shape=[jax.ShapeDtypeStruct(shape, dtype) for shape, dtype in outs],
        in_specs=[sspec()] * len(smem) + [vspec()] * len(operands),
        out_specs=[vspec()] * len(outs),
        scratch_shapes=[pltpu.VMEM(shape, dtype) for shape, dtype in scratch],
        compiler_params=pltpu.CompilerParams(vmem_limit_bytes=limit),
        cost_estimate=pl.CostEstimate(
            flops=int(us * 1.1e9), bytes_accessed=1000, transcendentals=0
        ),
        name=name,
    )(*smem, *operands)


def after(value, *others):
    return lax.optimization_barrier((value, *others))[0]


def pack_qkvg_kernel(idx, wq, wg, pk, pv, gains, o0, o1, o23, sems):
    x, f = idx[1], idx[2]
    copies = []
    for j, out in enumerate((o0, o1, o23.at[0], o23.at[1])):
        start = pl.multiple_of((2 * (f ^ j) + x) * 128, 128)
        for part in range(4):
            first = start if part == 3 else pl.multiple_of(part * 1024 + start, 128)
            source = wg if part == 3 else wq
            copies.append(
                pltpu.make_async_copy(
                    source.at[:, pl.ds(first, 128)],
                    out.at[pl.ds(0, 256), pl.ds(part * 128, 128)],
                    sems.at[4 * j + part],
                )
            )
    for copy in copies:
        copy.start()
    for j, out in enumerate((o0, o1, o23.at[0], o23.at[1])):
        start = pl.multiple_of((2 * (f ^ j) + x) * 128, 128)
        tail = [
            jnp.concatenate([pk[:, pl.ds(start, 128)], pv[:, pl.ds(start, 128)]], axis=1),
            gains[:, 0:256],
            gains[:, 256:512],
            jnp.zeros((EXTRA - 6, 256), jnp.bfloat16),
        ]
        tail = jnp.concatenate([t.astype(jnp.float32) for t in tail], axis=0)
        tail = jnp.concatenate([tail, jnp.zeros((EXTRA, 256), jnp.float32)], axis=1)
        out[256 : 256 + EXTRA, :] = tail.astype(jnp.bfloat16)
    for copy in copies:
        copy.wait()


def pack_gu_kernel(idx, wgu, o0, o1, o23):
    z, x, f = idx[0], idx[1], idx[2]
    width = FF // 8
    for j, out in enumerate((o0, o1, o23.at[0], o23.at[1])):
        head = 2 * (f ^ j) + x
        count = 256 if j < 2 else 128
        rows = pl.ds(0 if j < 2 else pl.multiple_of((z & 1) * 128, 128), count)
        pad = jnp.zeros((count, HIDDEN_PAD - width), jnp.bfloat16)
        for h in range(8):

            @pl.when(head == h)
            def _():
                for part in range(2):
                    first = part * FF + h * width
                    at = part * HIDDEN_PAD
                    out[:, at : at + HIDDEN_PAD] = jnp.concatenate(
                        [wgu[rows, first : first + width], pad], axis=1
                    )


def lay_weights(z, f, parts, w_full):
    own, beside, far, far_beside, next_far, next_beside = parts
    w_full[pl.ds(pl.multiple_of(f * 256, 256), 256), :] = own[...]
    w_full[pl.ds(pl.multiple_of((f ^ 1) * 256, 256), 256), :] = beside[...]
    halves = ((2, 0, far, 0), (3, 0, far_beside, 1), (2, 1, next_far, 0), (3, 1, next_beside, 1))
    for j, side, part, which in halves:
        rows = pl.multiple_of((f ^ j) * 256 + ((z ^ side) & 1) * 128, 128)
        w_full[pl.ds(rows, 128), :] = part[which]


def mixer_forward_kernel(idx, rates, ints, *refs):
    blocks = refs[0:8]
    parts = refs[8:12]
    w_out = refs[12]
    send, keep, normed, w_full, qkv, gate, att, rec, probs, pprobs, states, mixed = refs[13:25]
    gain_one, gain_two, pk, pv = refs[25:29]
    x, f = idx[1], idx[2]
    head = 2 * f + x
    scale = HEAD_WIDTH_SIZE ** (-0.5)
    wo = w_out[pl.ds(pl.multiple_of(x * 128, 128), 128), :]
    tails = []
    for j, part in enumerate((parts[0], parts[1], parts[2].at[0], parts[3].at[1])):
        rows = pl.multiple_of((f ^ j) * 256, 256)
        w_full[pl.ds(rows, 256), :] = part[0:256, :]
        tail = part[256 : 256 + EXTRA, 0:256].astype(jnp.float32)
        tails.append(tail)
        gain_one[:, pl.ds(rows, 256)] = tail[4:5]
        gain_two[:, pl.ds(rows, 256)] = tail[5:6]
    tails = jnp.concatenate([tail[0:4] for tail in tails], axis=0).astype(jnp.bfloat16)
    pk[...] = tails[:, 0:128]
    pv[...] = tails[:, 128:256]
    gain_row = gain_one[...]
    for k in range(8):
        values = blocks[k][...].astype(jnp.float32)
        normed_block = (values * rms_scale(values) * gain_row).astype(jnp.bfloat16)
        hk = head_of(x, f, k)
        normed[pl.ds(pl.multiple_of(hk * 64, 64), 64), :] = normed_block[:64]
        normed[pl.ds(pl.multiple_of((15 - hk) * 64, 64), 64), :] = normed_block[64:]
    for t in range(4):
        rows = slice(t * 256, t * 256 + 256)
        product = dot_nn(normed[rows, :], w_full[...])
        qkv[rows, :] = product[:, :384].astype(jnp.bfloat16)
        gate[rows, :] = jax.nn.sigmoid(product[:, 384:])
    state = jnp.zeros((128, 128), jnp.float32)
    moment = jnp.zeros((128, 128), jnp.float32)
    for t in range(8):
        rows = slice(t * 128, t * 128 + 128)
        width = (t + 1) * 128
        query = qkv[rows, 0:128]
        scores = dot_nt(query, qkv[0:width, 128:256]) * scale
        row_seg = jnp.transpose(jnp.broadcast_to(ints[t : t + 1, :], (128, 128)))[:, 0:1]
        col_seg = jnp.concatenate([ints[u : u + 1, :] for u in range(t + 1)], axis=1)
        row_pos = lax.broadcasted_iota(jnp.int32, (128, width), 0) + t * 128
        col_pos = lax.broadcasted_iota(jnp.int32, (128, width), 1)
        allowed = (row_seg == col_seg) & (col_pos <= row_pos)
        scores = jnp.where(allowed, scores, masked_score)
        pscores = dot_nt(query, pk[...]) * scale
        top = jnp.maximum(
            jnp.max(scores, axis=-1, keepdims=True), jnp.max(pscores, axis=-1, keepdims=True)
        )
        weights = jnp.exp(scores - top)
        pweights = jnp.exp(pscores - top)
        inverse = 1.0 / (
            jnp.sum(weights, axis=-1, keepdims=True) + jnp.sum(pweights, axis=-1, keepdims=True)
        )
        weights = (weights * inverse).astype(jnp.bfloat16)
        pweights = (pweights * inverse).astype(jnp.bfloat16)
        probs[rows, 0:width] = weights
        pprobs[rows, :] = pweights
        att[rows, :] = dot_nn(weights, qkv[0:width, 256:384]) + dot_nn(pweights, pv[...])
        for c in (2 * t, 2 * t + 1):
            grows = slice(c * 64, c * 64 + 64)
            alpha = rates[0, c * 8 + head]
            theta = rates[1, c * 8 + head]
            high, low = split_two(state)
            states[c] = high
            recalled = dot_nt(qkv[grows, 0:128], high) + dot_nt(qkv[grows, 0:128], low)
            rec[grows, :] = recalled * scale
            both = dot_tn(qkv[grows, 128:384], qkv[grows, 128:256])
            gram_high, gram_low = split_two(both[:128] * (theta / HEAD_WIDTH_SIZE))
            change = (
                dot_nn(high, gram_high) + dot_nn(low, gram_high) + dot_nn(high, gram_low)
            ) - both[128:] * (theta * scale)
            moment = momentum * moment - change
            state = (1.0 - alpha) * state + moment
        mixed[rows, :] = (att[rows, :] + gate[rows, :] * rec[rows, :]).astype(jnp.bfloat16)
    for k in range(8):
        hk = head_of(x, f, k)
        piece = jnp.concatenate(
            [
                mixed[pl.ds(pl.multiple_of(hk * 64, 64), 64), :],
                mixed[pl.ds(pl.multiple_of((15 - hk) * 64, 64), 64), :],
            ],
            axis=0,
        )
        out = send if k & 1 else keep
        out[k >> 1] = dot_nn(piece, wo).astype(jnp.bfloat16)


def mixer_backward_kernel(idx, rates, *refs):
    blocks = refs[0:8]
    w_out, w_full, qkv, gate, att, rec, probs, pprobs, states, pk, pv = refs[8:19]
    send, keep, dqkvg, branch = refs[19:23]
    gm, dy, delta, ds, dk, dv, dsp = refs[23:30]
    x, f = idx[1], idx[2]
    head = 2 * f + x
    scale = HEAD_WIDTH_SIZE ** (-0.5)
    wo = w_out[pl.ds(pl.multiple_of(x * 128, 128), 128), :]
    for k in range(8):
        hk = head_of(x, f, k)
        early = pl.ds(pl.multiple_of(hk * 64, 64), 64)
        late = pl.ds(pl.multiple_of((15 - hk) * 64, 64), 64)
        block = blocks[k][...]
        grad = dot_nt(block, wo).astype(jnp.bfloat16)
        gm[early, :] = grad[:64]
        gm[late, :] = grad[64:]
        branch[early, :] = block[:64]
        branch[late, :] = block[64:]
    for t in range(8):
        rows = slice(t * 128, t * 128 + 128)
        width = (t + 1) * 128
        grad_low = gm[rows, :]
        grad = grad_low.astype(jnp.float32)
        opened = gate[rows, :]
        dqkvg[rows, 384:512] = (grad * rec[rows, :] * opened * (1.0 - opened)).astype(jnp.bfloat16)
        dy[rows, :] = (grad * opened).astype(jnp.bfloat16)
        row_delta = jnp.sum(grad * att[rows, :], axis=-1, keepdims=True)
        grad_probs = dot_nt(grad_low, qkv[0:width, 256:384])
        ds_tile = (probs[rows, 0:width].astype(jnp.float32) * (grad_probs - row_delta)).astype(
            jnp.bfloat16
        )
        ds[rows, 0:width] = ds_tile
        grad_pprobs = dot_nt(grad_low, pv[...])
        dsp_tile = (pprobs[rows, :].astype(jnp.float32) * (grad_pprobs - row_delta)).astype(
            jnp.bfloat16
        )
        dsp[rows, :] = dsp_tile
        delta[rows, :] = (
            dot_nn(ds_tile, qkv[0:width, 128:256]) + dot_nn(dsp_tile, pk[...])
        ) * scale
    grad_pk = dot_tn(dsp[...], qkv[:, 0:128]) * scale
    grad_pv = dot_tn(pprobs[...], gm[...])
    grad_state = jnp.zeros((128, 128), jnp.float32)
    grad_moment = jnp.zeros((128, 128), jnp.float32)
    for t in range(7, -1, -1):
        rows = slice(t * 128, t * 128 + 128)
        rest = slice(t * 128, 1024)
        dk[rows, :] = dot_tn(ds[rest, rows], qkv[rest, 0:128]) * scale
        dv[rows, :] = dot_tn(probs[rest, rows], gm[rest, :])
        for c in (2 * t + 1, 2 * t):
            grows = slice(c * 64, c * 64 + 64)
            alpha = rates[0, c * 8 + head]
            theta = rates[1, c * 8 + head]
            query, key, value = qkv[grows, 0:128], qkv[grows, 128:256], qkv[grows, 256:384]
            dy_rows = dy[grows, :]
            state = states[c]
            summed = grad_state + grad_moment
            high, low = split_two(summed)
            key_summed = dot_nt(key, high) * scale
            error = value.astype(jnp.float32) - dot_nt(key, state) * scale
            grad_value = dv[grows, :] + theta * key_summed
            grad_key = dk[grows, :] + (theta * scale) * (
                dot_nn(error.astype(jnp.bfloat16), high)
                - dot_nn(key_summed.astype(jnp.bfloat16), state)
            )
            grad_query = delta[grows, :] + dot_nn(dy_rows, state) * scale
            dqkvg[grows, 0:128] = grad_query.astype(jnp.bfloat16)
            dqkvg[grows, 128:256] = grad_key.astype(jnp.bfloat16)
            dqkvg[grows, 256:384] = grad_value.astype(jnp.bfloat16)
            gram_high, gram_low = split_two(dot_tn(key, key) * (theta / HEAD_WIDTH_SIZE))
            product = dot_nn(high, gram_high) + dot_nn(low, gram_high) + dot_nn(high, gram_low)
            grad_state = (
                dot_tn(dy_rows, query) * scale + (1.0 - alpha) * grad_state - product
            )
            grad_moment = momentum * summed
    for k in range(8):
        hk = head_of(x, f, k)
        piece = jnp.concatenate(
            [
                dqkvg[pl.ds(pl.multiple_of(hk * 64, 64), 64), :],
                dqkvg[pl.ds(pl.multiple_of((15 - hk) * 64, 64), 64), :],
            ],
            axis=0,
        )
        out = send if k & 1 else keep
        out[k >> 1, 0:128, :] = dot_nt(piece, w_full[...]).astype(jnp.bfloat16)
        j = k & 3
        extra = jnp.concatenate(
            [
                grad_pk[4 * j : 4 * j + 4],
                grad_pv[4 * j : 4 * j + 4],
                jnp.zeros((EXTRA - 8, 128), jnp.float32),
            ],
            axis=0,
        )
        out[k >> 1, 128 : 128 + EXTRA, :] = jnp.zeros((EXTRA, 1024), jnp.bfloat16)
        out[k >> 1, 128 : 128 + EXTRA, pl.ds(pl.multiple_of(head * 128, 128), 128)] = extra.astype(
            jnp.bfloat16
        )


def lay_chunk(out, rows, count, width):
    out[256 : 256 + count, :] = rows[:, 0:width]
    left = 1024 - width
    part = count * left // width
    for i in range(count // part):
        out[256 + count : 256 + count + part, i * left : (i + 1) * left] = rows[
            i * part : (i + 1) * part, width:1024
        ]


def lay_chunks(z, outs, total_rows, count, width):
    for j in range(4):
        first = pl.multiple_of((z ^ j) * count, 32)
        rows = total_rows[pl.ds(first, count), :].astype(jnp.bfloat16)
        lay_chunk(outs[j & 1].at[j >> 1], rows, count, width)


def mixer_weights_kernel(idx, normed, dqkvg, mixed, branch, keep, send, total, total_o):
    z, f = idx[0], idx[2]
    outs = (keep, send)
    for t in range(4):
        total[...] = dot_tn(normed[:, t * 256 : t * 256 + 256], dqkvg[...])
        spot = pl.ds(pl.multiple_of((t ^ f) * 64, 64), 64)
        for j in range(4):
            outs[j & 1][j >> 1, spot, :] = total[
                pl.ds(pl.multiple_of((z ^ j) * 64, 64), 64), :
            ].astype(jnp.bfloat16)
    total_o[...] = dot_tn(mixed[...], branch[...])
    lay_chunks(z, outs, total_o, 32, 512)


def feed_kernel(idx, *refs):
    blocks, cots, parts = refs[0:8], refs[8:16], refs[16:22]
    w_down = refs[22]
    send_g, keep_g, send_d, keep_d, active, dgu = refs[23:29]
    w_full, wd = refs[29:31]
    z, x, f = idx[0], idx[1], idx[2]
    lay_weights(z, f, parts, w_full)
    wd[0:352, :] = w_down[pl.ds(pl.multiple_of(x * 352, 32), 352), :]
    wd[352:HIDDEN_PAD, :] = jnp.zeros((HIDDEN_PAD - 352, 1024), jnp.bfloat16)
    for k in range(4):
        rows = slice(k * 256, k * 256 + 256)
        feed = jnp.concatenate([blocks[2 * k][...], blocks[2 * k + 1][...]], axis=0)
        cot = jnp.concatenate([cots[2 * k][...], cots[2 * k + 1][...]], axis=0)
        gate_up = dot_nn(feed, w_full[...])
        g, u = gate_up[:, :HIDDEN_PAD], gate_up[:, HIDDEN_PAD:]
        sigma = jax.nn.sigmoid(g)
        active_low = (g * sigma * u).astype(jnp.bfloat16)
        active[rows, :] = active_low
        grad_active = dot_nt(cot, wd[...])
        grad_g = (grad_active * u * sigma * (1.0 + g * (1.0 - sigma))).astype(jnp.bfloat16)
        grad_u = (grad_active * g * sigma).astype(jnp.bfloat16)
        grad_low = jnp.concatenate([grad_g, grad_u], axis=1)
        dgu[rows, :] = grad_low
        grad_feed = dot_nt(grad_low, w_full[...]).astype(jnp.bfloat16)
        keep_g[k] = grad_feed[:128]
        send_g[k] = grad_feed[128:]
        down = dot_nn(active_low, wd[...]).astype(jnp.bfloat16)
        keep_d[k] = down[:128]
        send_d[k] = down[128:]


def feed_weights_kernel(idx, dgu, active, *refs):
    blocks, cot_blocks = refs[0:8], refs[8:16]
    keeps, sends = refs[16:18], refs[18:20]
    total, total_d, feeds, cots, laid = refs[20:25]
    z, f = idx[0], idx[2]
    for k in range(8):
        feeds[k * 128 : k * 128 + 128, :] = blocks[k][...]
        cots[k * 128 : k * 128 + 128, :] = cot_blocks[k][...]
    half = HIDDEN_PAD
    for t in range(4):
        total[...] = dot_tn(feeds[:, t * 256 : t * 256 + 256], dgu[...])
        spot = pl.ds(pl.multiple_of((t ^ f) * 64, 64), 64)
        for j in range(4):
            rows = total[pl.ds(pl.multiple_of((z ^ j) * 64, 64), 64), :].astype(jnp.bfloat16)
            outs = sends if j & 1 else keeps
            outs[0][j >> 1, spot, :] = rows[:, 0:half]
            outs[1][j >> 1, spot, :] = rows[:, half:]
    total_d[...] = dot_tn(active[...], cots[...])
    for j in range(4):
        first = pl.multiple_of((z ^ j) * Z_HIDDEN, 32)
        lay_chunk(laid, total_d[pl.ds(first, Z_HIDDEN), :].astype(jnp.bfloat16), Z_HIDDEN, 768)
        outs = sends if j & 1 else keeps
        outs[0][j >> 1, 256:, :] = laid[256:, 0:half]
        outs[1][j >> 1, 256:, :] = laid[256:, half:]


def add_kernel(keep, received, s0, s1, s2, s3):
    s0[...] = keep[0].astype(jnp.float32) + received[0].astype(jnp.float32)
    for k, out in ((1, s1), (2, s2), (3, s3)):
        out[...] = (keep[k].astype(jnp.float32) + received[k].astype(jnp.float32)).astype(
            jnp.bfloat16
        )


def total_of(refs):
    return (
        refs[0][...]
        + refs[1][...].astype(jnp.float32)
        + refs[2][...].astype(jnp.float32)
        + refs[3][...].astype(jnp.float32)
    )


def residual_kernel(x, gain, s0, r1, r2, r3, residual, feed):
    values = x[...].astype(jnp.float32) + total_of((s0, r1, r2, r3))
    residual[...] = values
    feed[...] = (values * rms_scale(values) * gain[...]).astype(jnp.bfloat16)


def norm_grad(values, gain, grad):
    inv = rms_scale(values)
    scaled = grad * gain
    return inv * scaled - values * (inv * inv * inv) * jnp.mean(
        scaled * values, axis=-1, keepdims=True
    )


def branch_kernel(residual, gain, cot, s0, r1, r2, r3, grad_residual, branch):
    grad = total_of((s0, r1, r2, r3))
    total = cot[...].astype(jnp.float32) + norm_grad(residual[...], gain[...], grad)
    grad_residual[...] = total
    branch[...] = total.astype(jnp.bfloat16)


def tokens_sum_kernel(keep, received, keep_far, keep_near, send_far):
    keep_far[...] = keep[0].astype(jnp.float32) + received[0].astype(jnp.float32)
    keep_near[...] = keep[1].astype(jnp.float32) + received[1].astype(jnp.float32)
    for k in range(2):
        send_far[k] = (keep[2 + k].astype(jnp.float32) + received[2 + k].astype(jnp.float32)).astype(
            jnp.bfloat16
        )


def far_kernel(own, passed, received, out_own, out_passed):
    out_own[...] = own[...] + received[0].astype(jnp.float32)
    out_passed[...] = (passed[...] + received[1].astype(jnp.float32)).astype(jnp.bfloat16)


def tokens_kernel(x, gain, grad_residual, own_sum, received, out, persist):
    total = own_sum[...] + received[...].astype(jnp.float32)
    grad = total[0:128]
    persist[...] = total[128:136]
    values = x[...].astype(jnp.float32)
    out[...] = (grad_residual[...] + norm_grad(values, gain[...], grad)).astype(jnp.bfloat16)


def output_kernel(residual, s0, r1, r2, r3, out):
    out[...] = (residual[...] + total_of((s0, r1, r2, r3))).astype(jnp.bfloat16)


def half_kernel(keep, received, own, passed):
    own[...] = keep[0].astype(jnp.float32) + received[0].astype(jnp.float32)
    passed[...] = (keep[1].astype(jnp.float32) + received[1].astype(jnp.float32)).astype(
        jnp.bfloat16
    )


def whole_kernel(pieces, *refs):
    own, received, outs = refs[:pieces], refs[pieces : 2 * pieces], refs[2 * pieces :]
    total = [
        (a[...] + b[...].astype(jnp.float32)).astype(jnp.bfloat16) for a, b in zip(own, received)
    ]
    total = jnp.concatenate(total, axis=1)
    for j in range(4):
        outs[j][...] = total[j * 64 : j * 64 + 64]
    outs[4][...] = total[256:]


def join_kernel(*refs):
    parts, rest, out = refs[0:4], refs[4], refs[5]
    for j in range(4):
        out[j * 64 : j * 64 + 64, :] = parts[j][...]
    out[256:, :] = rest[...]


def row_sums(products, out):
    out[...] = jnp.sum(jnp.transpose(products), axis=0, keepdims=True)


def feed_unpack_kernel(idx, *refs):
    parts = refs[0:8]
    wgu, gain = refs[8:10]
    out_gu, out_down, out_gain = refs[10:13]
    laid = refs[13]
    z, x, f = idx[0], idx[1], idx[2]
    width = FF // 8
    for j in range(4):
        for dx in range(2):
            part = parts[2 * j + dx]
            zj, xj = z ^ j, x ^ dx
            for jf in range(4):
                head = 2 * (f ^ jf) + xj
                laid[zj, head] = part[jf * 64 : jf * 64 + 64, :]

            lower = part[256:352, :].astype(jnp.float32)
            upper = part[352:384, :].astype(jnp.float32)
            valid = 64
            base = pl.multiple_of(xj * 352 + zj * Z_HIDDEN, 32)

            def put(first, count):
                at = pl.ds(pl.multiple_of(base + first, 32), count)
                out_down[at, 0:768] = lower[first : first + count]
                for i in range(first // 32, (first + count) // 32):
                    spot = pl.ds(pl.multiple_of(base + 32 * i, 32), 32)
                    out_down[spot, 768:1024] = upper[:, i * 256 : (i + 1) * 256]

            put(0, valid)

            @pl.when(zj < 3)
            def _():
                put(64, 32)

    for zj in range(4):
        for side in range(2):
            rows = jnp.concatenate(
                [
                    laid[zj, head][:, side * HIDDEN_PAD : side * HIDDEN_PAD + width]
                    for head in range(8)
                ],
                axis=1,
            )
            out_gu[zj * 64 : zj * 64 + 64, side * FF : side * FF + FF] = rows.astype(jnp.float32)
    sums = jnp.zeros((256, 128), jnp.float32)
    for t in range(2 * FF // 128):
        cols = slice(t * 128, t * 128 + 128)
        sums = sums + out_gu[:, cols] * wgu[:, cols].astype(jnp.float32)
    row_sums(sums, out_gain)
    out_gain[...] = out_gain[...] / gain[...].astype(jnp.float32)


def mixer_unpack_kernel(idx, *refs):
    parts = refs[0:8]
    wq, wg, gain = refs[8:11]
    out_qkv, out_gate, out_out, out_gain = refs[11:15]
    z, x, f = idx[0], idx[1], idx[2]
    for j in range(4):
        for dx in range(2):
            part = parts[2 * j + dx]
            zj, xj = z ^ j, x ^ dx
            rows = pl.ds(pl.multiple_of(zj * 64, 64), 64)
            for jf in range(4):
                head = 2 * (f ^ jf) + xj
                start = pl.multiple_of(head * 128, 128)
                for side in range(3):
                    out_qkv[rows, pl.ds(pl.multiple_of(side * 1024 + start, 128), 128)] = part[
                        jf * 64 : jf * 64 + 64, side * 128 : side * 128 + 128
                    ].astype(jnp.float32)
                out_gate[rows, pl.ds(start, 128)] = part[jf * 64 : jf * 64 + 64, 384:512].astype(
                    jnp.float32
                )
            spot = pl.ds(pl.multiple_of(xj * 128 + zj * 32, 32), 32)
            out_out[spot, 0:512] = part[256:288, :].astype(jnp.float32)
            out_out[spot, 512:1024] = part[288:320, :].astype(jnp.float32)
    sums = jnp.zeros((256, 128), jnp.float32)
    for t in range(24):
        cols = slice(t * 128, t * 128 + 128)
        sums = sums + out_qkv[:, cols] * wq[:, cols].astype(jnp.float32)
    for t in range(8):
        cols = slice(t * 128, t * 128 + 128)
        sums = sums + out_gate[:, cols] * wg[:, cols].astype(jnp.float32)
    row_sums(sums, out_gain)
    out_gain[...] = out_gain[...] / gain[...].astype(jnp.float32)


def sum_cores(keep, send):
    block = keep.shape[1:]
    return call(
        add_kernel,
        (),
        (keep, flip(send, 0, 1)),
        [(block, jnp.float32)] + [(block, jnp.bfloat16)] * 3,
        name="core_sum",
    )


def cross_chips(s0, s1, s2, s3):
    return s0, flip(s1, 0, 2), flip(s2, 1, 0), flip(s3, 1, 2)


def half_sum(keep, received, name):
    _, rows, width = keep.shape
    return call(
        half_kernel,
        (),
        (keep, received),
        [((rows, width), jnp.float32), ((rows, width), jnp.bfloat16)],
        name=name + "_half",
    )


def whole_sum(own, moved, name):
    rows = own[0].shape[0]
    width = sum(piece.shape[1] for piece in own)
    return call(
        functools.partial(whole_kernel, len(own)),
        (),
        (*own, *moved),
        [((64, width), jnp.bfloat16)] * 4 + [((rows - 256, width), jnp.bfloat16)],
        name=name + "_whole",
    )


def hand_rows(parts):
    return [parts[0]] + [flip(parts[j], 0, j) for j in range(1, 4)]


def join(parts, rest, name):
    rows, width = 256 + rest.shape[0], rest.shape[1]
    (joined,) = call(
        join_kernel, (), (*parts, rest), [((rows, width), jnp.bfloat16)], name=name + "_join"
    )
    return joined


def spread_far(joined):
    return flip_z(joined, 2), flip_z(joined, 1)


def in_planes(
    tokens,
    cotangent,
    segments,
    decay_index,
    step_index,
    w_qkv,
    w_gate,
    w_out,
    w_gu,
    w_down,
    persist_keys,
    persist_values,
    norm_gain,
    ffn_gain,
):
    bf16, f32 = jnp.bfloat16, jnp.float32
    ctx = lax.axis_index("ctx")
    f = lax.axis_index("fsdp")
    z, x = ctx // 2, ctx % 2
    head = 2 * f + x
    idx = jnp.stack([z, x, f, head]).astype(jnp.int32)

    own = to_plane(tokens[0])
    anywhere = pl.BlockSpec(memory_space=pl.ANY)
    wq_parts = pl.pallas_call(
        pack_qkvg_kernel,
        out_shape=[jax.ShapeDtypeStruct((256 + EXTRA, 512), bf16)] * 2
        + [jax.ShapeDtypeStruct((2, 256 + EXTRA, 512), bf16)],
        in_specs=[sspec(), anywhere, anywhere] + [vspec()] * 3,
        out_specs=[vspec()] * 3,
        scratch_shapes=[pltpu.SemaphoreType.DMA((16,))],
        compiler_params=pltpu.CompilerParams(vmem_limit_bytes=60 * 1024 * 1024),
        cost_estimate=pl.CostEstimate(flops=1000, bytes_accessed=1000, transcendentals=0),
        name="pack_qkvg",
    )(
        idx,
        w_qkv,
        w_gate,
        persist_keys,
        persist_values,
        jnp.concatenate([norm_gain, ffn_gain]).reshape(1, 512),
    )
    gu_parts = call(
        pack_gu_kernel,
        (idx,),
        (w_gu,),
        [((256, 768), bf16)] * 2 + [((2, 128, 768), bf16)],
        name="pack_gu",
    )
    ints = jnp.concatenate([segments[0], decay_index[0].reshape(-1), step_index[0].reshape(-1)])
    ints = to_plane(after(ints.reshape(10, 128), wq_parts[0]))
    rates = jnp.stack(
        [0.6 * jnp.exp2(-ints[8].astype(f32)), 0.1 * jnp.exp2(-ints[9].astype(f32))]
    )
    far = flip(wq_parts[2], 0, 2)
    wq_parts = [wq_parts[0], flip(wq_parts[1], 0, 1), far, flip(far, 0, 1)]
    own = after(own, wq_parts[0])
    near = gather_chips(own)
    own_cot = to_plane(after(cotangent[0], own))
    gu_far = flip(after(gu_parts[2], own), 0, 2)
    blocks = gather_cores(near)
    rates = after(rates, own_cot)
    cot_near = gather_chips(after(own_cot, near[2]))

    block = (128, 1024)
    quad = ((4, 128, 1024), bf16)
    (
        send,
        keep,
        normed,
        w_full,
        qkv,
        gate,
        att,
        rec,
        probs,
        pprobs,
        states,
        mixed,
        gain_one,
        gain_two,
        pk,
        pv,
    ) = call(
        mixer_forward_kernel,
        (idx, rates),
        (ints, *blocks, *wq_parts, w_out),
        [
            quad,
            quad,
            ((1024, 1024), bf16),
            ((1024, 512), bf16),
            ((1024, 384), bf16),
            ((1024, 128), f32),
            ((1024, 128), f32),
            ((1024, 128), f32),
            ((1024, 1024), bf16),
            ((1024, 16), bf16),
            ((16, 128, 128), bf16),
            ((1024, 128), bf16),
            ((1, 1024), f32),
            ((1, 1024), f32),
            ((16, 128), bf16),
            ((16, 128), bf16),
        ],
        name="mixer_forward",
        spare=10,
        us=10.0,
    )
    send = after(send, *cot_near[1:], gu_far)
    sums = sum_cores(keep, send)
    shares = cross_chips(*sums)
    gu_next = flip_z(gu_far, 1)
    gu_parts = [gu_parts[0], flip(gu_parts[1], 0, 1), gu_far, flip(gu_far, 0, 1)]
    gu_parts += [gu_next, flip(after(gu_next, shares[3]), 0, 1)]
    cots = gather_cores(cot_near)
    residual, feed = call(
        residual_kernel,
        (),
        (own, gain_two, *shares),
        [(block, f32), (block, bf16)],
        name="residual",
    )
    feeds = gather_cores(gather_chips(feed))
    send_g, keep_g, send_d, keep_d, active, dgu = call(
        feed_kernel,
        (idx,),
        (*feeds, *cots, *gu_parts, w_down),
        [
            quad,
            quad,
            quad,
            quad,
            ((1024, HIDDEN_PAD), bf16),
            ((1024, 2 * HIDDEN_PAD), bf16),
        ],
        scratch=[((1024, 2 * HIDDEN_PAD), bf16), ((HIDDEN_PAD, 1024), bf16)],
        name="feed",
        spare=10,
        us=7.5,
    )
    feed_keep, feed_later_keep, feed_send, feed_later_send = call(
        feed_weights_kernel,
        (idx,),
        (dgu, active, *feeds, *cots),
        [((2, 256 + 4 * Z_HIDDEN // 3, HIDDEN_PAD), bf16)] * 4,
        scratch=[
            ((256, 768), f32),
            ((HIDDEN_PAD, 1024), f32),
            ((1024, 1024), bf16),
            ((1024, 1024), bf16),
            ((256 + 4 * Z_HIDDEN // 3, 768), bf16),
        ],
        name="feed_weights",
        spare=10,
        us=3.5,
    )
    sums = sum_cores(after(keep_g, feed_send), send_g)
    send_d = after(send_d, sums[0])
    shares = cross_chips(*sums)
    feed_received = flip_z(feed_send, 1)
    feed_later_received = flip_z(after(feed_later_send, sums[0]), 1)
    out_sums = sum_cores(keep_d, send_d)
    grad_residual, branch = call(
        branch_kernel,
        (),
        (residual, gain_two, after(own_cot, out_sums[0]), *shares),
        [(block, f32), (block, bf16)],
        name="branch",
    )
    feed_own, feed_passed = half_sum(after(feed_keep, branch), feed_received, "feed")
    branch_near = gather_chips(branch, after(branch, feed_passed))
    feed_moved = flip_z(feed_passed, 2)
    branches = gather_cores(branch_near)
    feed_later, feed_later_passed = half_sum(
        after(feed_later_keep, branch_near[3]), feed_later_received, "feed_later"
    )
    rates = after(rates, feed_later_passed, feed_moved)
    feed_later_moved = flip_z(feed_later_passed, 2)
    out_sums = lax.optimization_barrier((*out_sums, branches[6]))[:4]
    out_shares = cross_chips(*out_sums)

    send, keep, dqkvg, branch_all = call(
        mixer_backward_kernel,
        (idx, rates),
        (*branches, w_out, w_full, qkv, gate, att, rec, probs, pprobs, states, pk, pv),
        [
            ((4, 128 + EXTRA, 1024), bf16),
            ((4, 128 + EXTRA, 1024), bf16),
            ((1024, 512), bf16),
            ((1024, 1024), bf16),
        ],
        scratch=[
            ((1024, 128), bf16),
            ((1024, 128), bf16),
            ((1024, 128), f32),
            ((1024, 1024), bf16),
            ((1024, 128), f32),
            ((1024, 128), f32),
            ((1024, 16), bf16),
        ],
        name="mixer_backward",
        spare=10,
        us=13.0,
    )
    send, dqkvg = lax.optimization_barrier(
        (send, dqkvg, feed_moved, feed_later_moved, *out_shares[1:])
    )[:2]
    *feed_parts, feed_rest = whole_sum(
        (after(feed_own, send), feed_later), (feed_moved, feed_later_moved), "feed"
    )
    feed_parts = hand_rows(feed_parts)
    dqkvg = after(dqkvg, feed_rest)
    mixer_keep, mixer_send = call(
        mixer_weights_kernel,
        (idx,),
        (normed, dqkvg, mixed, branch_all),
        [((2, 320, 512), bf16)] * 2,
        scratch=[((256, 512), f32), ((128, 1024), f32)],
        name="mixer_weights",
        spare=10,
        us=2.2,
    )
    (result,) = call(output_kernel, (), (residual, *out_shares), [(block, bf16)], name="output")
    rows = (128 + EXTRA, 1024)
    keep_far, keep_near, send_far = call(
        tokens_sum_kernel,
        (),
        (after(keep, feed_rest), flip(send, 0, 1)),
        [(rows, f32), (rows, f32), ((2, *rows), bf16)],
        name="tokens_sum",
    )
    feed_joined = join(feed_parts, after(feed_rest, mixer_send, keep_near), "feed")
    feed_second = flip_z(feed_joined, 2)
    feed_beside = flip(feed_joined, 1, 0)
    mixer_own, mixer_passed = half_sum(
        after(mixer_keep, feed_joined), flip_z(mixer_send, 1), "mixer"
    )
    mixer_moved = flip_z(mixer_passed, 2)
    feed_first = flip_z(feed_joined, 1)
    tokens_far = flip(after(send_far, mixer_passed), 1, 0)
    feed_first_beside = flip(after(feed_first, mixer_passed), 1, 0)
    mixer_own = after(mixer_own, feed_beside)
    *mixer_parts, mixer_rest = whole_sum((mixer_own,), (mixer_moved,), "mixer")
    result = to_plane(after(result, mixer_passed))
    feed_third = flip_z(after(feed_second, mixer_rest), 1)
    feed_second_beside = flip(after(feed_second, mixer_rest), 1, 0)
    mixer_joined = join(
        hand_rows(mixer_parts), after(mixer_rest, tokens_far, feed_first_beside), "mixer"
    )
    mixer_second, mixer_first = spread_far(mixer_joined)
    mixer_beside = flip(mixer_joined, 1, 0)
    feed_third_beside = flip(
        after(
            feed_third,
            mixer_joined,


        ),
        1,
        0,
    )
    tokens_own, tokens_passed = call(
        far_kernel,
        (),
        (after(keep_far, mixer_joined), keep_near, tokens_far),
        [((128 + EXTRA, 1024), f32), ((128 + EXTRA, 1024), bf16)],
        name="tokens_far",
    )
    tokens_near = flip(tokens_passed, 0, 2)
    mixer_second = after(
        mixer_second,
        mixer_first,
        mixer_beside,
        feed_second_beside,
        tokens_near,
    )
    mixer_third = flip_z(mixer_second, 1)
    mixer_first_beside = flip(after(mixer_first, mixer_second), 1, 0)
    mixer_second_beside = flip(mixer_second, 1, 0)
    grad_tokens, persist = call(
        tokens_kernel,
        (),
        (after(own, mixer_second), gain_one, grad_residual, tokens_own, tokens_near),
        [(block, bf16), ((8, 1024), f32)],
        name="tokens",
    )
    grad_tokens = to_plane(grad_tokens)
    persist = persist + after(flip_z(persist, 1), mixer_third)
    feed_pieces = (
        feed_joined,
        feed_beside,
        feed_first,
        feed_first_beside,
        feed_second,
        feed_second_beside,
        feed_third,
        feed_third_beside,
    )

    grad_gu, grad_down, grad_ffn = call(
        feed_unpack_kernel,
        (idx,),
        (*feed_pieces, w_gu, after(ffn_gain.reshape(1, 256), mixer_second)),
        [((256, 2 * FF), f32), ((FF // 4, 1024), f32), ((1, 256), f32)],
        scratch=[((4, 8, 64, 768), bf16)],
        name="feed_unpack",
        spare=10,
        us=5.5,
    )
    mixer_third_beside = flip(
        after(mixer_third, grad_ffn, mixer_first_beside, mixer_second_beside), 1, 0
    )
    persist = persist + flip_z(persist, 2)
    mixer_pieces = (
        mixer_joined,
        mixer_beside,
        mixer_first,
        mixer_first_beside,
        mixer_second,
        mixer_second_beside,
        mixer_third,
        mixer_third_beside,
    )
    grad_qkv, grad_gate, grad_out, grad_norm = call(
        mixer_unpack_kernel,
        (idx,),
        (*mixer_pieces, w_qkv, w_gate, norm_gain.reshape(1, 256)),
        [
            ((256, 3072), f32),
            ((256, 1024), f32),
            ((256, 1024), f32),
            ((1, 256), f32),
        ],
        name="mixer_unpack",
    )
    return (
        result[None],
        grad_tokens.astype(f32)[None],
        grad_qkv,
        grad_gate,
        grad_out,
        grad_gu,
        grad_down,
        persist[0:4],
        persist[4:8],
        grad_norm.reshape(256),
        grad_ffn.reshape(256),
    )


def solution(mesh):
    in_specs = (
        P("fsdp", "ctx", None),
        P("fsdp", "ctx", None),
        P("fsdp", None),
        P("fsdp", None, None),
        P("fsdp", None, None),
        P("fsdp", None),
        P("fsdp", None),
        P("fsdp", None),
        P("fsdp", None),
        P("fsdp", None),
        P("fsdp", None),
        P("fsdp", None),
        P("fsdp"),
        P("fsdp"),
    )
    out_specs = (
        P("fsdp", "ctx", None),
        P("fsdp", "ctx", None),
        P("fsdp", None),
        P("fsdp", None),
        P("fsdp", None),
        P("fsdp", None),
        P("fsdp", None),
        P("fsdp", None),
        P("fsdp", None),
        P("fsdp"),
        P("fsdp"),
    )
    planes = dict(mesh.shape) == {"ctx": HEADS, "fsdp": PLANES}
    return jax.shard_map(
        in_planes if planes else on_device, mesh=mesh, in_specs=in_specs, out_specs=out_specs, check_vma=False
    )
```

```python
import functools

import jax
import jax.numpy as jnp
import numpy as np
from jax import lax
from jax.experimental import pallas as pl
from jax.experimental.pallas import tpu as pltpu
from jax.sharding import PartitionSpec as P

HEADS = 8
HEAD_WIDTH_SIZE = 128
FF = 2816
GROUP = 64


epsilon = 1e-06
momentum = 0.9
masked_score = -1e30
highest_precision = lax.Precision.HIGHEST


def rms_scale(values):
    return lax.rsqrt(jnp.mean(values * values, axis=-1, keepdims=True) + epsilon)


def norm_back(values, inv_rms, gain_vec, grad_normed):
    scaled_grad = grad_normed * gain_vec
    grad_gain = jnp.sum(grad_normed * values * inv_rms, axis=0)
    grad_values = inv_rms * scaled_grad - values * inv_rms * inv_rms * inv_rms * jnp.mean(
        scaled_grad * values, axis=-1, keepdims=True
    )
    return (grad_values, grad_gain)


def place_rows(row_index, shard_rows, dev_count):
    half_rows = shard_rows // 2
    owner_dev = row_index // shard_rows
    inner_row = row_index % shard_rows
    block_id = jnp.where(inner_row < half_rows, owner_dev, 2 * dev_count - 1 - owner_dev)
    return block_id * half_rows + inner_row % half_rows


def position_order(stored, dev_count):
    rows = stored.shape[0]
    rest = stored.shape[1:]
    split = stored.reshape((dev_count, 2, rows // (2 * dev_count)) + rest)
    early = split[:, 0].reshape((-1,) + rest)
    late = split[::-1, 1].reshape((-1,) + rest)
    return jnp.concatenate([early, late], axis=0)


def key_mask(query_pos, query_seg, key_pos, key_seg):
    return (key_seg[None, :] == query_seg[:, None]) & (key_pos[None, :] <= query_pos[:, None])


def head_scores(queries, key_block):
    return jnp.einsum(
        "qhd,khd->hqk", queries, key_block, preferred_element_type=jnp.float32
    ) * HEAD_WIDTH_SIZE ** (-0.5)


def online_step(running, scores, value_block):
    run_max, run_total, accumulated = running
    new_max = jnp.maximum(run_max, jnp.max(scores, axis=-1))
    rescale = jnp.exp(run_max - new_max)
    weights = jnp.exp(scores - new_max[:, :, None])
    run_total = run_total * rescale + jnp.sum(weights, axis=-1)
    update = jnp.einsum(
        "hqk,khd->qhd",
        weights.astype(jnp.bfloat16),
        value_block,
        preferred_element_type=jnp.float32,
    )
    accumulated = accumulated * jnp.transpose(rescale)[:, :, None] + update
    return (new_max, run_total, accumulated)


def fold_keys(running, all_keys, all_values, context):
    queries, query_pos, query_seg, segment_all, shard_rows, dev_count = context
    total_rows = all_keys.shape[0]
    block_rows = min(512, total_rows)

    def fold_one_block(carried, block_index):
        offset_row = block_index * block_rows
        key_block = lax.dynamic_slice_in_dim(all_keys, offset_row, block_rows, 0).reshape(
            block_rows, HEADS, HEAD_WIDTH_SIZE
        )
        value_block = lax.dynamic_slice_in_dim(all_values, offset_row, block_rows, 0).reshape(
            block_rows, HEADS, HEAD_WIDTH_SIZE
        )
        key_pos = place_rows(
            offset_row + jnp.arange(block_rows, dtype=jnp.int32), shard_rows, dev_count
        )
        key_seg = jnp.take(segment_all, key_pos)
        allowed = key_mask(query_pos, query_seg, key_pos, key_seg)
        scores = jnp.where(allowed[None], head_scores(queries, key_block), masked_score)
        carried = online_step(carried, scores, value_block)
        return (carried, None)

    running, _ = lax.scan(
        fold_one_block, running, jnp.arange(total_rows // block_rows, dtype=jnp.int32)
    )
    return running


def back_every_key(grad_query, all_keys, all_values, context, grad_heads, log_total, row_delta):
    queries, query_pos, query_seg, segment_all, shard_rows, dev_count = context
    total_rows = all_keys.shape[0]
    block_rows = min(512, total_rows)
    scale_factor = HEAD_WIDTH_SIZE ** (-0.5)

    def back_one_block(carried, block_index):
        offset_row = block_index * block_rows
        key_block = lax.dynamic_slice_in_dim(all_keys, offset_row, block_rows, 0).reshape(
            block_rows, HEADS, HEAD_WIDTH_SIZE
        )
        value_block = lax.dynamic_slice_in_dim(all_values, offset_row, block_rows, 0).reshape(
            block_rows, HEADS, HEAD_WIDTH_SIZE
        )
        key_pos = place_rows(
            offset_row + jnp.arange(block_rows, dtype=jnp.int32), shard_rows, dev_count
        )
        key_seg = jnp.take(segment_all, key_pos)
        allowed = key_mask(query_pos, query_seg, key_pos, key_seg)
        scores = jnp.where(allowed[None], head_scores(queries, key_block), masked_score)
        prob_block = jnp.exp(scores - log_total[:, :, None])
        grad_prob = jnp.einsum(
            "qhd,khd->hqk", grad_heads, value_block, preferred_element_type=jnp.float32
        )
        grad_scores = (prob_block * (grad_prob - row_delta[:, :, None])).astype(jnp.bfloat16)
        query_grad = (
            carried
            + jnp.einsum("hqk,khd->qhd", grad_scores, key_block, preferred_element_type=jnp.float32)
            * scale_factor
        )
        key_grad = (
            jnp.einsum("hqk,qhd->khd", grad_scores, queries, preferred_element_type=jnp.float32)
            * scale_factor
        )
        value_grad = jnp.einsum(
            "hqk,qhd->khd",
            prob_block.astype(jnp.bfloat16),
            grad_heads,
            preferred_element_type=jnp.float32,
        )
        return (query_grad, (key_grad, value_grad))

    grad_query, (key_grads, value_grads) = lax.scan(
        back_one_block, grad_query, jnp.arange(total_rows // block_rows, dtype=jnp.int32)
    )
    return (
        grad_query,
        key_grads.reshape(total_rows, HEADS, HEAD_WIDTH_SIZE),
        value_grads.reshape(total_rows, HEADS, HEAD_WIDTH_SIZE),
    )


def group_step(stacked_rows, group_key_rows, group_value_rows, alpha_row, learning_rate_row):
    current_memory = stacked_rows[:, :HEAD_WIDTH_SIZE]
    moment_now = stacked_rows[:, HEAD_WIDTH_SIZE:]
    gram_matrix = (
        jnp.einsum("thk,thj->hkj", group_key_rows, group_key_rows, precision=highest_precision)
        * learning_rate_row[:, None, None]
    )
    mixed_product = (
        jnp.einsum("qgw,qgc->gwc", group_key_rows, group_value_rows, precision=highest_precision)
        * learning_rate_row[:, None, None]
    )
    memory_gradient = (
        jnp.einsum("fld,fdi->fli", gram_matrix, current_memory, precision=highest_precision)
        - mixed_product
    )
    moment_next = momentum * moment_now - memory_gradient
    memory_next = (1.0 - alpha_row)[:, None, None] * current_memory + moment_next
    return jnp.concatenate([memory_next, moment_next], axis=1)


def run_block(stacked_rows, query_part, key_part, value_part, alphas, thetas):
    scale_factor = HEAD_WIDTH_SIZE ** (-0.5)
    group_query_rows = query_part * scale_factor
    recalled_rows = [
        jnp.einsum(
            "ipb,pbx->ipx",
            group_query_rows,
            stacked_rows[:, :HEAD_WIDTH_SIZE],
            precision=highest_precision,
        )
    ]
    stacked_rows = group_step(
        stacked_rows, key_part * scale_factor, value_part, alphas[0], thetas[0]
    )
    return (jnp.concatenate(recalled_rows, axis=0), stacked_rows)


def states_before(key_order, value_order, alpha_all, theta_all, early_index, late_index):
    groups = alpha_all.shape[0]
    scale_factor = HEAD_WIDTH_SIZE ** (-0.5)
    key_groups = key_order.reshape(groups, GROUP, HEADS, HEAD_WIDTH_SIZE)
    value_groups = value_order.reshape(groups, GROUP, HEADS, HEAD_WIDTH_SIZE)
    zero_state = jnp.zeros((HEADS, 2 * HEAD_WIDTH_SIZE, HEAD_WIDTH_SIZE), jnp.float32)

    def states_one_group(carried, inputs):
        stacked_rows, into_early, into_late = carried
        group_key_rows, group_value_rows, alpha_row, learning_rate_row, group_index = inputs
        into_early = jnp.where(group_index == early_index, stacked_rows, into_early)
        into_late = jnp.where(group_index == late_index, stacked_rows, into_late)
        current_memory = stacked_rows[:, :HEAD_WIDTH_SIZE]
        moment_now = stacked_rows[:, HEAD_WIDTH_SIZE:]
        gram_matrix = (
            jnp.einsum(
                "thk,thj->hkj", group_key_rows, group_key_rows, preferred_element_type=jnp.float32
            )
            * (learning_rate_row / HEAD_WIDTH_SIZE)[:, None, None]
        )
        mixed_product = (
            jnp.einsum(
                "qgw,qgc->gwc", group_key_rows, group_value_rows, preferred_element_type=jnp.float32
            )
            * (learning_rate_row * scale_factor)[:, None, None]
        )
        memory_gradient = (
            jnp.einsum("fld,fdi->fli", gram_matrix, current_memory, precision=highest_precision)
            - mixed_product
        )
        moment_next = momentum * moment_now - memory_gradient
        memory_next = (1.0 - alpha_row)[:, None, None] * current_memory + moment_next
        stacked_rows = jnp.concatenate([memory_next, moment_next], axis=1)
        return ((stacked_rows, into_early, into_late), None)

    (_, into_early, into_late), _ = lax.scan(
        states_one_group,
        (zero_state, zero_state, zero_state),
        (key_groups, value_groups, alpha_all, theta_all, jnp.arange(groups, dtype=jnp.int32)),
    )
    return (into_early, into_late)


def adjoints_after(
    query_order, key_order, recall_grad_order, alpha_all, theta_all, early_end, late_end
):
    groups = alpha_all.shape[0]
    scale_factor = HEAD_WIDTH_SIZE ** (-0.5)
    query_groups = query_order.reshape(groups, GROUP, HEADS, HEAD_WIDTH_SIZE)
    key_groups = key_order.reshape(groups, GROUP, HEADS, HEAD_WIDTH_SIZE)
    grad_groups = recall_grad_order.reshape(groups, GROUP, HEADS, HEAD_WIDTH_SIZE)
    zero_state = jnp.zeros((HEADS, 2 * HEAD_WIDTH_SIZE, HEAD_WIDTH_SIZE), jnp.float32)

    def adjoints_one_group(carried, inputs):
        adjoint, out_early, out_late = carried
        (
            group_query_rows,
            group_key_rows,
            gradient_group_rows,
            alpha_row,
            learning_rate_row,
            group_index,
        ) = inputs
        out_early = jnp.where(group_index + 1 == early_end, adjoint, out_early)
        out_late = jnp.where(group_index + 1 == late_end, adjoint, out_late)
        gram_matrix = (
            jnp.einsum(
                "thk,thj->hkj", group_key_rows, group_key_rows, preferred_element_type=jnp.float32
            )
            * (learning_rate_row / HEAD_WIDTH_SIZE)[:, None, None]
        )
        query_term = (
            jnp.einsum(
                "qgw,qgc->gwc",
                group_query_rows,
                gradient_group_rows,
                preferred_element_type=jnp.float32,
            )
            * scale_factor
        )
        grad_m = adjoint[:, :HEAD_WIDTH_SIZE]
        summed_rows = grad_m + adjoint[:, HEAD_WIDTH_SIZE:]
        new_m = (
            (1.0 - alpha_row)[:, None, None] * grad_m
            + query_term
            - jnp.einsum("fld,fdi->fli", gram_matrix, summed_rows, precision=highest_precision)
        )
        adjoint = jnp.concatenate([new_m, momentum * summed_rows], axis=1)
        return ((adjoint, out_early, out_late), None)

    (_, out_early, out_late), _ = lax.scan(
        adjoints_one_group,
        (zero_state, zero_state, zero_state),
        (
            query_groups,
            key_groups,
            grad_groups,
            alpha_all,
            theta_all,
            jnp.arange(groups, dtype=jnp.int32),
        ),
        reverse=True,
    )
    return (out_early, out_late)


def on_device(
    tokens,
    cotangent,
    segments,
    decay_index,
    step_index,
    w_qkv,
    w_gate,
    w_out,
    w_gu,
    w_down,
    persist_keys,
    persist_values,
    norm_gain,
    ffn_gain,
):
    shard_rows = tokens.shape[1]
    model_width = tokens.shape[2]
    half_rows = shard_rows // 2
    dev_count = lax.axis_size("ctx")
    device = lax.axis_index("ctx")
    scale_factor = HEAD_WIDTH_SIZE ** (-0.5)
    full_weights = (
        lax.all_gather(w_qkv, "fsdp", axis=0, tiled=True),
        lax.all_gather(w_gate, "fsdp", axis=0, tiled=True),
        lax.all_gather(w_out, "fsdp", axis=0, tiled=True),
        lax.all_gather(w_gu, "fsdp", axis=0, tiled=True),
        lax.all_gather(w_down, "fsdp", axis=0, tiled=True),
        lax.all_gather(persist_keys, "fsdp", axis=0, tiled=True),
        lax.all_gather(persist_values, "fsdp", axis=0, tiled=True),
        lax.all_gather(norm_gain, "fsdp", axis=0, tiled=True),
        lax.all_gather(ffn_gain, "fsdp", axis=0, tiled=True),
    )
    wq_full, wg_full, wo_full, wgu_full, wd_full, pkeys_full, pvalues_full, gain_attn, gain_ffn = (
        full_weights
    )
    gain_attn32 = gain_attn.astype(jnp.float32)
    gain_ffn32 = gain_ffn.astype(jnp.float32)
    pkeys_heads = pkeys_full.reshape(-1, HEADS, HEAD_WIDTH_SIZE)
    pvalues_heads = pvalues_full.reshape(-1, HEADS, HEAD_WIDTH_SIZE)
    inputs32 = tokens[0].astype(jnp.float32)
    inv_rms_one = rms_scale(inputs32)
    normed_low = (inputs32 * inv_rms_one * gain_attn32).astype(jnp.bfloat16)
    projected = jnp.dot(normed_low, wq_full, preferred_element_type=jnp.float32)
    query_flat = projected[:, :model_width].astype(jnp.bfloat16)
    key_flat = projected[:, model_width : 2 * model_width].astype(jnp.bfloat16)
    value_flat = projected[:, 2 * model_width :].astype(jnp.bfloat16)
    query_heads = query_flat.reshape(shard_rows, HEADS, HEAD_WIDTH_SIZE)
    gate_open = jax.nn.sigmoid(jnp.dot(normed_low, wg_full, preferred_element_type=jnp.float32))
    local_rows = jnp.arange(shard_rows, dtype=jnp.int32)
    query_pos = place_rows(device * shard_rows + local_rows, shard_rows, dev_count)
    segment_all = segments[0]
    query_seg = jnp.take(segment_all, query_pos)
    context = (query_heads, query_pos, query_seg, segment_all, shard_rows, dev_count)
    all_keys, all_values = (
        lax.all_gather(key_flat, "ctx", axis=0, tiled=True),
        lax.all_gather(value_flat, "ctx", axis=0, tiled=True),
    )
    persist_scores = head_scores(query_heads, pkeys_heads)
    start_state = (
        jnp.full((HEADS, shard_rows), masked_score, jnp.float32),
        jnp.zeros((HEADS, shard_rows), jnp.float32),
        jnp.zeros((shard_rows, HEADS, HEAD_WIDTH_SIZE), jnp.float32),
    )
    running = online_step(start_state, persist_scores, pvalues_heads)
    running = fold_keys(running, all_keys, all_values, context)
    run_max, run_total, accumulated = running
    attended = accumulated / jnp.transpose(run_total)[:, :, None]
    log_total = run_max + jnp.log(run_total)
    group_count = half_rows // GROUP
    alpha_all = 0.6 * jnp.exp2(-decay_index[0].astype(jnp.float32))
    theta_all = 0.1 * jnp.exp2(-step_index[0].astype(jnp.float32))
    early_first = device * group_count
    late_first = (2 * dev_count - 1 - device) * group_count
    alpha_early = lax.dynamic_slice_in_dim(alpha_all, early_first, group_count, 0)
    theta_early = lax.dynamic_slice_in_dim(theta_all, early_first, group_count, 0)
    alpha_late = lax.dynamic_slice_in_dim(alpha_all, late_first, group_count, 0)
    theta_late = lax.dynamic_slice_in_dim(theta_all, late_first, group_count, 0)
    query_f = query_heads.astype(jnp.float32)
    key_f = key_flat.astype(jnp.float32).reshape(shard_rows, HEADS, HEAD_WIDTH_SIZE)
    value_f = value_flat.astype(jnp.float32).reshape(shard_rows, HEADS, HEAD_WIDTH_SIZE)
    early_parts = (query_f[:half_rows], key_f[:half_rows], value_f[:half_rows])
    late_parts = (query_f[half_rows:], key_f[half_rows:], value_f[half_rows:])

    def early_run(stacked_rows, query_part, key_part, value_part):
        return run_block(stacked_rows, query_part, key_part, value_part, alpha_early, theta_early)

    def late_run(stacked_rows, query_part, key_part, value_part):
        return run_block(stacked_rows, query_part, key_part, value_part, alpha_late, theta_late)

    into_early, into_late = states_before(
        position_order(all_keys, dev_count),
        position_order(all_values, dev_count),
        alpha_all,
        theta_all,
        early_first,
        late_first,
    )
    recall_early, _ = early_run(into_early, early_parts[0], early_parts[1], early_parts[2])
    recall_late, _ = late_run(into_late, late_parts[0], late_parts[1], late_parts[2])
    recall = jnp.concatenate([recall_early, recall_late], axis=0).reshape(shard_rows, model_width)
    mixed_low = (attended.reshape(shard_rows, model_width) + gate_open * recall).astype(
        jnp.bfloat16
    )
    residual = inputs32 + jnp.dot(mixed_low, wo_full, preferred_element_type=jnp.float32)
    inv_rms_two = rms_scale(residual)
    normed_two = (residual * inv_rms_two * gain_ffn32).astype(jnp.bfloat16)
    gate_up = jnp.dot(normed_two, wgu_full, preferred_element_type=jnp.float32)
    gate_part = gate_up[:, :FF]
    up_part = gate_up[:, FF:]
    active = (jax.nn.silu(gate_part) * up_part).astype(jnp.bfloat16)
    result = residual + jnp.dot(active, wd_full, preferred_element_type=jnp.float32)
    cot_low = cotangent[0]
    grad_w_down = jnp.einsum("tf,td->fd", active, cot_low, preferred_element_type=jnp.float32)
    grad_active = jnp.einsum("td,fd->tf", cot_low, wd_full, preferred_element_type=jnp.float32)
    sigma_gate = jax.nn.sigmoid(gate_part)
    grad_gate_part = grad_active * up_part * sigma_gate * (1.0 + gate_part * (1.0 - sigma_gate))
    grad_up_part = grad_active * gate_part * sigma_gate
    grad_gu_low = jnp.concatenate([grad_gate_part, grad_up_part], axis=1).astype(jnp.bfloat16)
    grad_w_gu = jnp.einsum("td,tf->df", normed_two, grad_gu_low, preferred_element_type=jnp.float32)
    grad_normed_two = jnp.einsum(
        "tf,df->td", grad_gu_low, wgu_full, preferred_element_type=jnp.float32
    )
    grad_res_norm, grad_ffn_gain = norm_back(residual, inv_rms_two, gain_ffn32, grad_normed_two)
    grad_residual = cot_low.astype(jnp.float32) + grad_res_norm
    grad_branch = grad_residual.astype(jnp.bfloat16)
    grad_w_out = jnp.einsum("td,te->de", mixed_low, grad_branch, preferred_element_type=jnp.float32)
    grad_mixed_low = jnp.einsum(
        "te,de->td", grad_branch, wo_full, preferred_element_type=jnp.float32
    ).astype(jnp.bfloat16)
    grad_mixed32 = grad_mixed_low.astype(jnp.float32)
    grad_gate_low = (grad_mixed32 * recall * gate_open * (1.0 - gate_open)).astype(jnp.bfloat16)
    grad_w_gate = jnp.einsum(
        "td,tf->df", normed_low, grad_gate_low, preferred_element_type=jnp.float32
    )
    recall_grad_low = (grad_mixed32 * gate_open).astype(jnp.bfloat16)
    grad_recall = recall_grad_low.astype(jnp.float32).reshape(shard_rows, HEADS, HEAD_WIDTH_SIZE)
    grad_heads = grad_mixed_low.reshape(shard_rows, HEADS, HEAD_WIDTH_SIZE)
    row_delta = jnp.transpose(jnp.sum(grad_heads.astype(jnp.float32) * attended, axis=-1))
    memory_queries, all_recall_grads = (
        lax.all_gather(query_flat, "ctx", axis=0, tiled=True),
        lax.all_gather(recall_grad_low, "ctx", axis=0, tiled=True),
    )
    out_early, out_late = adjoints_after(
        position_order(memory_queries, dev_count),
        position_order(all_keys, dev_count),
        position_order(all_recall_grads, dev_count),
        alpha_all,
        theta_all,
        early_first + group_count,
        late_first + group_count,
    )
    _, pull_early = jax.vjp(early_run, into_early, early_parts[0], early_parts[1], early_parts[2])
    _, grad_qe, grad_ke, grad_ve = pull_early((grad_recall[:half_rows], out_early))
    _, pull_late = jax.vjp(late_run, into_late, late_parts[0], late_parts[1], late_parts[2])
    _, grad_ql, grad_kl, grad_vl = pull_late((grad_recall[half_rows:], out_late))
    grad_q_mem = jnp.concatenate([grad_qe, grad_ql], axis=0).reshape(shard_rows, model_width)
    grad_k_mem = jnp.concatenate([grad_ke, grad_kl], axis=0).reshape(shard_rows, model_width)
    grad_v_mem = jnp.concatenate([grad_ve, grad_vl], axis=0).reshape(shard_rows, model_width)
    persist_probs = jnp.exp(persist_scores - log_total[:, :, None])
    persist_grad_prob = jnp.einsum(
        "qhd,phd->hqp", grad_heads, pvalues_heads, preferred_element_type=jnp.float32
    )
    persist_ds = (persist_probs * (persist_grad_prob - row_delta[:, :, None])).astype(jnp.bfloat16)
    grad_query_att = (
        jnp.einsum("hqp,phd->qhd", persist_ds, pkeys_heads, preferred_element_type=jnp.float32)
        * scale_factor
    )
    grad_pkeys = (
        jnp.einsum("hqp,qhd->phd", persist_ds, query_heads, preferred_element_type=jnp.float32)
        * scale_factor
    )
    grad_pvalues = jnp.einsum(
        "hqp,qhd->phd",
        persist_probs.astype(jnp.bfloat16),
        grad_heads,
        preferred_element_type=jnp.float32,
    )
    grad_query_att, key_grads_all, value_grads_all = back_every_key(
        grad_query_att, all_keys, all_values, context, grad_heads, log_total, row_delta
    )
    key_grad_att, value_grad_att = (
        lax.psum_scatter(key_grads_all, "ctx", scatter_dimension=0, tiled=True),
        lax.psum_scatter(value_grads_all, "ctx", scatter_dimension=0, tiled=True),
    )
    grad_query = grad_query_att.reshape(shard_rows, model_width) + grad_q_mem
    grad_key = key_grad_att.reshape(shard_rows, model_width) + grad_k_mem
    grad_value = value_grad_att.reshape(shard_rows, model_width) + grad_v_mem
    grad_qkv_low = jnp.concatenate([grad_query, grad_key, grad_value], axis=1).astype(jnp.bfloat16)
    grad_w_qkv = jnp.einsum(
        "td,tf->df", normed_low, grad_qkv_low, preferred_element_type=jnp.float32
    )
    grad_normed = jnp.einsum(
        "tf,df->td", grad_qkv_low, wq_full, preferred_element_type=jnp.float32
    ) + jnp.einsum("tf,df->td", grad_gate_low, wg_full, preferred_element_type=jnp.float32)
    grad_in_norm, grad_norm_gain = norm_back(inputs32, inv_rms_one, gain_attn32, grad_normed)
    grad_inputs = grad_residual + grad_in_norm
    local_grads = (
        grad_w_qkv,
        grad_w_gate,
        grad_w_out,
        grad_w_gu,
        grad_w_down,
        grad_pkeys.reshape(-1, model_width),
        grad_pvalues.reshape(-1, model_width),
        grad_norm_gain,
        grad_ffn_gain,
    )
    shares = (
        lax.psum_scatter(
            local_grads[0].astype(jnp.bfloat16), "fsdp", scatter_dimension=0, tiled=True
        ).astype(jnp.float32),
        lax.psum_scatter(
            local_grads[1].astype(jnp.bfloat16), "fsdp", scatter_dimension=0, tiled=True
        ).astype(jnp.float32),
        lax.psum_scatter(
            local_grads[2].astype(jnp.bfloat16), "fsdp", scatter_dimension=0, tiled=True
        ).astype(jnp.float32),
        lax.psum_scatter(
            local_grads[3].astype(jnp.bfloat16), "fsdp", scatter_dimension=0, tiled=True
        ).astype(jnp.float32),
        lax.psum_scatter(
            local_grads[4].astype(jnp.bfloat16), "fsdp", scatter_dimension=0, tiled=True
        ).astype(jnp.float32),
        lax.psum_scatter(
            local_grads[5].astype(jnp.bfloat16), "fsdp", scatter_dimension=0, tiled=True
        ).astype(jnp.float32),
        lax.psum_scatter(
            local_grads[6].astype(jnp.bfloat16), "fsdp", scatter_dimension=0, tiled=True
        ).astype(jnp.float32),
        lax.psum_scatter(
            local_grads[7].astype(jnp.bfloat16), "fsdp", scatter_dimension=0, tiled=True
        ).astype(jnp.float32),
        lax.psum_scatter(
            local_grads[8].astype(jnp.bfloat16), "fsdp", scatter_dimension=0, tiled=True
        ).astype(jnp.float32),
    )
    totals = lax.psum(
        (
            shares[0],
            shares[1],
            shares[2],
            shares[3],
            shares[4],
            shares[5],
            shares[6],
            shares[7],
            shares[8],
        ),
        "ctx",
    )
    return (
        result.astype(jnp.bfloat16)[None],
        grad_inputs[None],
        totals[0],
        totals[1],
        totals[2],
        totals[3],
        totals[4],
        totals[5],
        totals[6],
        totals[7],
        totals[8],
    )


PERSIST = 16
PLANES = 4
HIDDEN_PAD = 384
Z_HIDDEN = HIDDEN_PAD // PLANES
EXTRA = 16


def head_of(x, f, k):
    return 2 * (f ^ (k & 3)) + (x ^ (k >> 2))


def linear(z, x, f):
    return (2 * z + x) * 4 + f


def shift(value, move):
    pairs = []
    for z in range(4):
        for x in range(2):
            for f in range(4):
                pairs.append((linear(z, x, f), linear(*move(z, x, f))))
    return lax.ppermute(value, ("ctx", "fsdp"), pairs)


def to_plane(value):
    return shift(value, lambda z, x, f: (f, x, z))


def flip(value, dx, df):
    return shift(value, lambda z, x, f: (z, x ^ dx, f ^ df))


def flip_z(value, dz):
    return shift(value, lambda z, x, f: (z ^ dz, x, f))


def gather_chips(block, last=None):
    last = block if last is None else last
    return [block, flip(block, 0, 2), flip(block, 1, 0), flip(last, 1, 2)]


def gather_cores(near):
    far = [flip(b, 0, 1) for b in near]
    return [near[0], far[0], near[1], far[1], near[2], far[2], near[3], far[3]]


def dot_nn(a, b):
    return lax.dot_general(a, b, (((1,), (0,)), ((), ())), preferred_element_type=jnp.float32)


def dot_nt(a, b):
    return lax.dot_general(a, b, (((1,), (1,)), ((), ())), preferred_element_type=jnp.float32)


def dot_tn(a, b):
    return lax.dot_general(a, b, (((0,), (0,)), ((), ())), preferred_element_type=jnp.float32)


def split_two(value):
    high = value.astype(jnp.bfloat16)
    return high, (value - high.astype(jnp.float32)).astype(jnp.bfloat16)


def product_three(a, b_high, b_low):
    a_high, a_low = split_two(a)
    return dot_nn(a_high, b_high) + dot_nn(a_low, b_high) + dot_nn(a_high, b_low)


def vspec():
    return pl.BlockSpec(memory_space=pltpu.VMEM)


def sspec():
    return pl.BlockSpec(memory_space=pltpu.SMEM)


def padded_bytes(shape, dtype):
    size = jnp.dtype(dtype).itemsize
    lanes = -(-shape[-1] // 128) * 128
    rows = -(-shape[-2] // (32 // size)) * (32 // size)
    return int(np.prod(shape[:-2])) * rows * lanes * size


def call(kernel, smem, operands, outs, scratch=(), name=None, spare=6, us=0.5):
    held = [(o.shape, o.dtype) for o in operands] + list(outs) + list(scratch)
    limit = sum(padded_bytes(shape, dtype) for shape, dtype in held) + spare * 1024 * 1024
    return pl.pallas_call(
        kernel,
        out_shape=[jax.ShapeDtypeStruct(shape, dtype) for shape, dtype in outs],
        in_specs=[sspec()] * len(smem) + [vspec()] * len(operands),
        out_specs=[vspec()] * len(outs),
        scratch_shapes=[pltpu.VMEM(shape, dtype) for shape, dtype in scratch],
        compiler_params=pltpu.CompilerParams(vmem_limit_bytes=limit),
        cost_estimate=pl.CostEstimate(
            flops=int(us * 1.1e9), bytes_accessed=1000, transcendentals=0
        ),
        name=name,
    )(*smem, *operands)


def after(value, *others):
    return lax.optimization_barrier((value, *others))[0]


def pack_qkvg_kernel(idx, wq, wg, pk, pv, gains, o0, o1, o23, sems):
    x, f = idx[1], idx[2]
    copies = []
    for j, out in enumerate((o0, o1, o23.at[0], o23.at[1])):
        start = pl.multiple_of((2 * (f ^ j) + x) * 128, 128)
        for part in range(4):
            first = start if part == 3 else pl.multiple_of(part * 1024 + start, 128)
            source = wg if part == 3 else wq
            copies.append(
                pltpu.make_async_copy(
                    source.at[:, pl.ds(first, 128)],
                    out.at[pl.ds(0, 256), pl.ds(part * 128, 128)],
                    sems.at[4 * j + part],
                )
            )
    for copy in copies:
        copy.start()
    for j, out in enumerate((o0, o1, o23.at[0], o23.at[1])):
        start = pl.multiple_of((2 * (f ^ j) + x) * 128, 128)
        tail = [
            jnp.concatenate([pk[:, pl.ds(start, 128)], pv[:, pl.ds(start, 128)]], axis=1),
            gains[:, 0:256],
            gains[:, 256:512],
            jnp.zeros((EXTRA - 6, 256), jnp.bfloat16),
        ]
        tail = jnp.concatenate([t.astype(jnp.float32) for t in tail], axis=0)
        tail = jnp.concatenate([tail, jnp.zeros((EXTRA, 256), jnp.float32)], axis=1)
        out[256 : 256 + EXTRA, :] = tail.astype(jnp.bfloat16)
    for copy in copies:
        copy.wait()


def pack_gu_kernel(idx, wgu, o0, o1, o23):
    z, x, f = idx[0], idx[1], idx[2]
    width = FF // 8
    for j, out in enumerate((o0, o1, o23.at[0], o23.at[1])):
        head = 2 * (f ^ j) + x
        count = 256 if j < 2 else 128
        rows = pl.ds(0 if j < 2 else pl.multiple_of((z & 1) * 128, 128), count)
        pad = jnp.zeros((count, HIDDEN_PAD - width), jnp.bfloat16)
        for h in range(8):

            @pl.when(head == h)
            def _():
                for part in range(2):
                    first = part * FF + h * width
                    at = part * HIDDEN_PAD
                    out[:, at : at + HIDDEN_PAD] = jnp.concatenate(
                        [wgu[rows, first : first + width], pad], axis=1
                    )


def lay_weights(z, f, parts, w_full):
    own, beside, far, far_beside, next_far, next_beside = parts
    w_full[pl.ds(pl.multiple_of(f * 256, 256), 256), :] = own[...]
    w_full[pl.ds(pl.multiple_of((f ^ 1) * 256, 256), 256), :] = beside[...]
    halves = ((2, 0, far, 0), (3, 0, far_beside, 1), (2, 1, next_far, 0), (3, 1, next_beside, 1))
    for j, side, part, which in halves:
        rows = pl.multiple_of((f ^ j) * 256 + ((z ^ side) & 1) * 128, 128)
        w_full[pl.ds(rows, 128), :] = part[which]


def mixer_forward_kernel(idx, rates, ints, *refs):
    blocks = refs[0:8]
    parts = refs[8:12]
    w_out = refs[12]
    send, keep, normed, w_full, qkv, gate, att, rec, probs, pprobs, states, mixed = refs[13:25]
    gain_one, gain_two, pk, pv = refs[25:29]
    x, f = idx[1], idx[2]
    head = 2 * f + x
    scale = HEAD_WIDTH_SIZE ** (-0.5)
    wo = w_out[pl.ds(pl.multiple_of(x * 128, 128), 128), :]
    tails = []
    for j, part in enumerate((parts[0], parts[1], parts[2].at[0], parts[3].at[1])):
        rows = pl.multiple_of((f ^ j) * 256, 256)
        w_full[pl.ds(rows, 256), :] = part[0:256, :]
        tail = part[256 : 256 + EXTRA, 0:256].astype(jnp.float32)
        tails.append(tail)
        gain_one[:, pl.ds(rows, 256)] = tail[4:5]
        gain_two[:, pl.ds(rows, 256)] = tail[5:6]
    tails = jnp.concatenate([tail[0:4] for tail in tails], axis=0).astype(jnp.bfloat16)
    pk[...] = tails[:, 0:128]
    pv[...] = tails[:, 128:256]
    gain_row = gain_one[...]
    for k in range(8):
        values = blocks[k][...].astype(jnp.float32)
        normed_block = (values * rms_scale(values) * gain_row).astype(jnp.bfloat16)
        hk = head_of(x, f, k)
        normed[pl.ds(pl.multiple_of(hk * 64, 64), 64), :] = normed_block[:64]
        normed[pl.ds(pl.multiple_of((15 - hk) * 64, 64), 64), :] = normed_block[64:]
    state = jnp.zeros((128, 128), jnp.float32)
    moment = jnp.zeros((128, 128), jnp.float32)
    for t in range(8):
        if t % 2 == 0:
            rows = slice(t * 128, t * 128 + 256)
            product = dot_nn(normed[rows, :], w_full[...])
            qkv[rows, :] = product[:, :384].astype(jnp.bfloat16)
            gate[rows, :] = jax.nn.sigmoid(product[:, 384:])
        rows = slice(t * 128, t * 128 + 128)
        width = (t + 1) * 128
        query = qkv[rows, 0:128]
        scores = dot_nt(query, qkv[0:width, 128:256]) * scale
        row_seg = jnp.transpose(jnp.broadcast_to(ints[t : t + 1, :], (128, 128)))[:, 0:1]
        col_seg = jnp.concatenate([ints[u : u + 1, :] for u in range(t + 1)], axis=1)
        row_pos = lax.broadcasted_iota(jnp.int32, (128, width), 0) + t * 128
        col_pos = lax.broadcasted_iota(jnp.int32, (128, width), 1)
        allowed = (row_seg == col_seg) & (col_pos <= row_pos)
        scores = jnp.where(allowed, scores, masked_score)
        pscores = dot_nt(query, pk[...]) * scale
        top = jnp.maximum(
            jnp.max(scores, axis=-1, keepdims=True), jnp.max(pscores, axis=-1, keepdims=True)
        )
        weights = jnp.exp(scores - top)
        pweights = jnp.exp(pscores - top)
        inverse = 1.0 / (
            jnp.sum(weights, axis=-1, keepdims=True) + jnp.sum(pweights, axis=-1, keepdims=True)
        )
        weights = (weights * inverse).astype(jnp.bfloat16)
        pweights = (pweights * inverse).astype(jnp.bfloat16)
        probs[rows, 0:width] = weights
        pprobs[rows, :] = pweights
        att[rows, :] = dot_nn(weights, qkv[0:width, 256:384]) + dot_nn(pweights, pv[...])
        for c in (2 * t, 2 * t + 1):
            grows = slice(c * 64, c * 64 + 64)
            alpha = rates[0, c * 8 + head]
            theta = rates[1, c * 8 + head]
            high, low = split_two(state)
            states[c] = high
            recalled = dot_nt(qkv[grows, 0:128], high) + dot_nt(qkv[grows, 0:128], low)
            rec[grows, :] = recalled * scale
            both = dot_tn(qkv[grows, 128:384], qkv[grows, 128:256])
            gram_high, gram_low = split_two(both[:128] * (theta / HEAD_WIDTH_SIZE))
            change = (
                dot_nn(high, gram_high) + dot_nn(low, gram_high) + dot_nn(high, gram_low)
            ) - both[128:] * (theta * scale)
            moment = momentum * moment - change
            state = (1.0 - alpha) * state + moment
        mixed[rows, :] = (att[rows, :] + gate[rows, :] * rec[rows, :]).astype(jnp.bfloat16)
    for k in range(8):
        hk = head_of(x, f, k)
        piece = jnp.concatenate(
            [
                mixed[pl.ds(pl.multiple_of(hk * 64, 64), 64), :],
                mixed[pl.ds(pl.multiple_of((15 - hk) * 64, 64), 64), :],
            ],
            axis=0,
        )
        out = send if k & 1 else keep
        out[k >> 1] = dot_nn(piece, wo).astype(jnp.bfloat16)


def mixer_backward_kernel(idx, rates, *refs):
    blocks = refs[0:8]
    w_out, w_full, qkv, gate, att, rec, probs, pprobs, states, pk, pv = refs[8:19]
    send, keep, dqkvg, branch = refs[19:23]
    gm, ds, dk, dv, dsp = refs[23:28]
    x, f = idx[1], idx[2]
    head = 2 * f + x
    scale = HEAD_WIDTH_SIZE ** (-0.5)
    wo = w_out[pl.ds(pl.multiple_of(x * 128, 128), 128), :]
    for k in range(8):
        hk = head_of(x, f, k)
        early = pl.ds(pl.multiple_of(hk * 64, 64), 64)
        late = pl.ds(pl.multiple_of((15 - hk) * 64, 64), 64)
        block = blocks[k][...]
        grad = dot_nt(block, wo).astype(jnp.bfloat16)
        gm[early, :] = grad[:64]
        gm[late, :] = grad[64:]
        branch[early, :] = block[:64]
        branch[late, :] = block[64:]
    grad_state = jnp.zeros((128, 128), jnp.float32)
    grad_moment = jnp.zeros((128, 128), jnp.float32)
    for t in range(7, -1, -1):
        rows = slice(t * 128, t * 128 + 128)
        width = (t + 1) * 128
        grad_low = gm[rows, :]
        grad = grad_low.astype(jnp.float32)
        opened = gate[rows, :]
        dqkvg[rows, 384:512] = (grad * rec[rows, :] * opened * (1.0 - opened)).astype(jnp.bfloat16)
        dy_tile = (grad * opened).astype(jnp.bfloat16)
        row_delta = jnp.sum(grad * att[rows, :], axis=-1, keepdims=True)
        grad_probs = dot_nt(grad_low, qkv[0:width, 256:384])
        ds_tile = (probs[rows, 0:width].astype(jnp.float32) * (grad_probs - row_delta)).astype(
            jnp.bfloat16
        )
        ds[rows, 0:width] = ds_tile
        grad_pprobs = dot_nt(grad_low, pv[...])
        dsp_tile = (pprobs[rows, :].astype(jnp.float32) * (grad_pprobs - row_delta)).astype(
            jnp.bfloat16
        )
        dsp[rows, :] = dsp_tile
        query_grad = (
            dot_nn(ds_tile, qkv[0:width, 128:256]) + dot_nn(dsp_tile, pk[...])
        ) * scale
        for c in (2 * t + 1, 2 * t):
            grows = slice(c * 64, c * 64 + 64)
            local = slice((c - 2 * t) * 64, (c - 2 * t) * 64 + 64)
            alpha = rates[0, c * 8 + head]
            theta = rates[1, c * 8 + head]
            query, key, value = qkv[grows, 0:128], qkv[grows, 128:256], qkv[grows, 256:384]
            dy_rows = dy_tile[local]
            state = states[c]
            summed = grad_state + grad_moment
            high, low = split_two(summed)
            gram_high, gram_low = split_two(dot_tn(key, key) * (theta / HEAD_WIDTH_SIZE))
            product = dot_nn(high, gram_high) + dot_nn(low, gram_high) + dot_nn(high, gram_low)
            grad_state = (
                dot_tn(dy_rows, query) * scale + (1.0 - alpha) * grad_state - product
            )
            grad_moment = momentum * summed
            key_summed = dot_nt(key, high) * scale
            error = value.astype(jnp.float32) - dot_nt(key, state) * scale
            dv[grows, :] = theta * key_summed
            dk[grows, :] = (theta * scale) * (
                dot_nn(error.astype(jnp.bfloat16), high)
                - dot_nn(key_summed.astype(jnp.bfloat16), state)
            )
            dqkvg[grows, 0:128] = (
                query_grad[local] + dot_nn(dy_rows, state) * scale
            ).astype(jnp.bfloat16)
    grad_pk = dot_tn(dsp[...], qkv[:, 0:128]) * scale
    grad_pv = dot_tn(pprobs[...], gm[...])
    for t in range(8):
        rows = slice(t * 128, t * 128 + 128)
        rest = slice(t * 128, 1024)
        key_grad = dk[rows, :] + dot_tn(ds[rest, rows], qkv[rest, 0:128]) * scale
        value_grad = dv[rows, :] + dot_tn(probs[rest, rows], gm[rest, :])
        dqkvg[rows, 128:256] = key_grad.astype(jnp.bfloat16)
        dqkvg[rows, 256:384] = value_grad.astype(jnp.bfloat16)
    for k in range(8):
        hk = head_of(x, f, k)
        piece = jnp.concatenate(
            [
                dqkvg[pl.ds(pl.multiple_of(hk * 64, 64), 64), :],
                dqkvg[pl.ds(pl.multiple_of((15 - hk) * 64, 64), 64), :],
            ],
            axis=0,
        )
        out = send if k & 1 else keep
        out[k >> 1, 0:128, :] = dot_nt(piece, w_full[...]).astype(jnp.bfloat16)
        j = k & 3
        extra = jnp.concatenate(
            [
                grad_pk[4 * j : 4 * j + 4],
                grad_pv[4 * j : 4 * j + 4],
                jnp.zeros((EXTRA - 8, 128), jnp.float32),
            ],
            axis=0,
        )
        out[k >> 1, 128 : 128 + EXTRA, :] = jnp.zeros((EXTRA, 1024), jnp.bfloat16)
        out[k >> 1, 128 : 128 + EXTRA, pl.ds(pl.multiple_of(head * 128, 128), 128)] = extra.astype(
            jnp.bfloat16
        )


def lay_chunk(out, rows, count, width):
    out[256 : 256 + count, :] = rows[:, 0:width]
    left = 1024 - width
    part = count * left // width
    for i in range(count // part):
        out[256 + count : 256 + count + part, i * left : (i + 1) * left] = rows[
            i * part : (i + 1) * part, width:1024
        ]


def lay_chunks(z, outs, total_rows, count, width):
    for j in range(4):
        first = pl.multiple_of((z ^ j) * count, 32)
        rows = total_rows[pl.ds(first, count), :].astype(jnp.bfloat16)
        lay_chunk(outs[j & 1].at[j >> 1], rows, count, width)


def mixer_weights_kernel(idx, normed, dqkvg, mixed, branch, keep, send, total, total_o):
    z, f = idx[0], idx[2]
    outs = (keep, send)
    for t in range(4):
        total[...] = dot_tn(normed[:, t * 256 : t * 256 + 256], dqkvg[...])
        spot = pl.ds(pl.multiple_of((t ^ f) * 64, 64), 64)
        for j in range(4):
            outs[j & 1][j >> 1, spot, :] = total[
                pl.ds(pl.multiple_of((z ^ j) * 64, 64), 64), :
            ].astype(jnp.bfloat16)
    total_o[...] = dot_tn(mixed[...], branch[...])
    lay_chunks(z, outs, total_o, 32, 512)


def feed_kernel(idx, *refs):
    blocks, cots, parts = refs[0:8], refs[8:16], refs[16:22]
    w_down = refs[22]
    send_g, keep_g, send_d, keep_d, active, dgu = refs[23:29]
    w_full, wd = refs[29:31]
    z, x, f = idx[0], idx[1], idx[2]
    lay_weights(z, f, parts, w_full)
    wd[0:352, :] = w_down[pl.ds(pl.multiple_of(x * 352, 32), 352), :]
    wd[352:HIDDEN_PAD, :] = jnp.zeros((HIDDEN_PAD - 352, 1024), jnp.bfloat16)
    for k in range(4):
        rows = slice(k * 256, k * 256 + 256)
        feed = jnp.concatenate([blocks[2 * k][...], blocks[2 * k + 1][...]], axis=0)
        cot = jnp.concatenate([cots[2 * k][...], cots[2 * k + 1][...]], axis=0)
        gate_up = dot_nn(feed, w_full[...])
        g, u = gate_up[:, :HIDDEN_PAD], gate_up[:, HIDDEN_PAD:]
        sigma = jax.nn.sigmoid(g)
        active_low = (g * sigma * u).astype(jnp.bfloat16)
        active[rows, :] = active_low
        grad_active = dot_nt(cot, wd[...])
        grad_g = (grad_active * u * sigma * (1.0 + g * (1.0 - sigma))).astype(jnp.bfloat16)
        grad_u = (grad_active * g * sigma).astype(jnp.bfloat16)
        grad_low = jnp.concatenate([grad_g, grad_u], axis=1)
        dgu[rows, :] = grad_low
        grad_feed = dot_nt(grad_low, w_full[...]).astype(jnp.bfloat16)
        keep_g[k] = grad_feed[:128]
        send_g[k] = grad_feed[128:]
        down = dot_nn(active_low, wd[...]).astype(jnp.bfloat16)
        keep_d[k] = down[:128]
        send_d[k] = down[128:]


def feed_weights_kernel(idx, dgu, active, *refs):
    blocks, cot_blocks = refs[0:8], refs[8:16]
    keeps, sends = refs[16:18], refs[18:20]
    total, total_d, feeds, cots, laid = refs[20:25]
    z, f = idx[0], idx[2]
    for k in range(8):
        feeds[k * 128 : k * 128 + 128, :] = blocks[k][...]
        cots[k * 128 : k * 128 + 128, :] = cot_blocks[k][...]
    half = HIDDEN_PAD
    for t in range(4):
        total[...] = dot_tn(feeds[:, t * 256 : t * 256 + 256], dgu[...])
        spot = pl.ds(pl.multiple_of((t ^ f) * 64, 64), 64)
        for j in range(4):
            rows = total[pl.ds(pl.multiple_of((z ^ j) * 64, 64), 64), :].astype(jnp.bfloat16)
            outs = sends if j & 1 else keeps
            outs[0][j >> 1, spot, :] = rows[:, 0:half]
            outs[1][j >> 1, spot, :] = rows[:, half:]
    total_d[...] = dot_tn(active[...], cots[...])
    for j in range(4):
        first = pl.multiple_of((z ^ j) * Z_HIDDEN, 32)
        lay_chunk(laid, total_d[pl.ds(first, Z_HIDDEN), :].astype(jnp.bfloat16), Z_HIDDEN, 768)
        outs = sends if j & 1 else keeps
        outs[0][j >> 1, 256:, :] = laid[256:, 0:half]
        outs[1][j >> 1, 256:, :] = laid[256:, half:]


def add_kernel(keep, received, s0, s1, s2, s3):
    s0[...] = keep[0].astype(jnp.float32) + received[0].astype(jnp.float32)
    for k, out in ((1, s1), (2, s2), (3, s3)):
        out[...] = (keep[k].astype(jnp.float32) + received[k].astype(jnp.float32)).astype(
            jnp.bfloat16
        )


def total_of(refs):
    return (
        refs[0][...]
        + refs[1][...].astype(jnp.float32)
        + refs[2][...].astype(jnp.float32)
        + refs[3][...].astype(jnp.float32)
    )


def residual_kernel(x, gain, s0, r1, r2, r3, residual, feed):
    values = x[...].astype(jnp.float32) + total_of((s0, r1, r2, r3))
    residual[...] = values
    feed[...] = (values * rms_scale(values) * gain[...]).astype(jnp.bfloat16)


def norm_grad(values, gain, grad):
    inv = rms_scale(values)
    scaled = grad * gain
    return inv * scaled - values * (inv * inv * inv) * jnp.mean(
        scaled * values, axis=-1, keepdims=True
    )


def branch_kernel(residual, gain, cot, s0, r1, r2, r3, grad_residual, branch):
    grad = total_of((s0, r1, r2, r3))
    total = cot[...].astype(jnp.float32) + norm_grad(residual[...], gain[...], grad)
    grad_residual[...] = total
    branch[...] = total.astype(jnp.bfloat16)


def split_kernel(order, keep, received, own, beside, crossing):
    def total(k):
        return keep[k].astype(jnp.float32) + received[k].astype(jnp.float32)

    own[...] = total(order[0])
    beside[...] = total(order[1])
    for i in range(2):
        crossing[i] = total(order[2 + i]).astype(jnp.bfloat16)


def far_kernel(own, passed, received, out_own, out_passed):
    out_own[...] = own[...] + received[0].astype(jnp.float32)
    out_passed[...] = (passed[...] + received[1].astype(jnp.float32)).astype(jnp.bfloat16)


def tokens_kernel(x, gain, grad_residual, own_sum, received, out, persist):
    total = own_sum[...] + received[...].astype(jnp.float32)
    grad = total[0:128]
    persist[...] = total[128:136]
    values = x[...].astype(jnp.float32)
    out[...] = (grad_residual[...] + norm_grad(values, gain[...], grad)).astype(jnp.bfloat16)


def output_kernel(residual, own_sum, *refs):
    received, out = refs[:-1], refs[-1]
    total = residual[...] + own_sum[...]
    for piece in received:
        total = total + piece[...].astype(jnp.float32)
    out[...] = total.astype(jnp.bfloat16)


def half_kernel(keep, received, own, passed):
    own[...] = keep[0].astype(jnp.float32) + received[0].astype(jnp.float32)
    passed[...] = (keep[1].astype(jnp.float32) + received[1].astype(jnp.float32)).astype(
        jnp.bfloat16
    )


def whole_kernel(pieces, *refs):
    own, received, outs = refs[:pieces], refs[pieces : 2 * pieces], refs[2 * pieces :]
    total = [
        (a[...] + b[...].astype(jnp.float32)).astype(jnp.bfloat16) for a, b in zip(own, received)
    ]
    total = jnp.concatenate(total, axis=1)
    for j in range(4):
        outs[j][...] = total[j * 64 : j * 64 + 64]
    outs[4][...] = total[256:]


def join_kernel(*refs):
    parts, rest, out = refs[0:4], refs[4], refs[5]
    for j in range(4):
        out[j * 64 : j * 64 + 64, :] = parts[j][...]
    out[256:, :] = rest[...]


def row_sums(products, out):
    out[...] = jnp.sum(jnp.transpose(products), axis=0, keepdims=True)


def feed_unpack_kernel(idx, *refs):
    parts = refs[0:8]
    wgu, gain = refs[8:10]
    out_gu, out_down, out_gain = refs[10:13]
    laid = refs[13]
    z, x, f = idx[0], idx[1], idx[2]
    width = FF // 8
    for j in range(4):
        for dx in range(2):
            part = parts[2 * j + dx]
            zj, xj = z ^ j, x ^ dx
            for jf in range(4):
                head = 2 * (f ^ jf) + xj
                laid[zj, head] = part[jf * 64 : jf * 64 + 64, :]

            lower = part[256:352, :].astype(jnp.float32)
            upper = part[352:384, :].astype(jnp.float32)
            valid = 64
            base = pl.multiple_of(xj * 352 + zj * Z_HIDDEN, 32)

            def put(first, count):
                at = pl.ds(pl.multiple_of(base + first, 32), count)
                out_down[at, 0:768] = lower[first : first + count]
                for i in range(first // 32, (first + count) // 32):
                    spot = pl.ds(pl.multiple_of(base + 32 * i, 32), 32)
                    out_down[spot, 768:1024] = upper[:, i * 256 : (i + 1) * 256]

            put(0, valid)

            @pl.when(zj < 3)
            def _():
                put(64, 32)

    for zj in range(4):
        for side in range(2):
            rows = jnp.concatenate(
                [
                    laid[zj, head][:, side * HIDDEN_PAD : side * HIDDEN_PAD + width]
                    for head in range(8)
                ],
                axis=1,
            )
            out_gu[zj * 64 : zj * 64 + 64, side * FF : side * FF + FF] = rows.astype(jnp.float32)
    sums = jnp.zeros((256, 128), jnp.float32)
    for t in range(2 * FF // 128):
        cols = slice(t * 128, t * 128 + 128)
        sums = sums + out_gu[:, cols] * wgu[:, cols].astype(jnp.float32)
    row_sums(sums, out_gain)
    out_gain[...] = out_gain[...] / gain[...].astype(jnp.float32)


def mixer_unpack_kernel(idx, *refs):
    parts = refs[0:8]
    wq, wg, gain = refs[8:11]
    out_qkv, out_gate, out_out, out_gain = refs[11:15]
    z, x, f = idx[0], idx[1], idx[2]
    for j in range(4):
        for dx in range(2):
            part = parts[2 * j + dx]
            zj, xj = z ^ j, x ^ dx
            rows = pl.ds(pl.multiple_of(zj * 64, 64), 64)
            for jf in range(4):
                head = 2 * (f ^ jf) + xj
                start = pl.multiple_of(head * 128, 128)
                for side in range(3):
                    out_qkv[rows, pl.ds(pl.multiple_of(side * 1024 + start, 128), 128)] = part[
                        jf * 64 : jf * 64 + 64, side * 128 : side * 128 + 128
                    ].astype(jnp.float32)
                out_gate[rows, pl.ds(start, 128)] = part[jf * 64 : jf * 64 + 64, 384:512].astype(
                    jnp.float32
                )
            spot = pl.ds(pl.multiple_of(xj * 128 + zj * 32, 32), 32)
            out_out[spot, 0:512] = part[256:288, :].astype(jnp.float32)
            out_out[spot, 512:1024] = part[288:320, :].astype(jnp.float32)
    sums = jnp.zeros((256, 128), jnp.float32)
    for t in range(24):
        cols = slice(t * 128, t * 128 + 128)
        sums = sums + out_qkv[:, cols] * wq[:, cols].astype(jnp.float32)
    for t in range(8):
        cols = slice(t * 128, t * 128 + 128)
        sums = sums + out_gate[:, cols] * wg[:, cols].astype(jnp.float32)
    row_sums(sums, out_gain)
    out_gain[...] = out_gain[...] / gain[...].astype(jnp.float32)


def sum_cores(keep, send):
    block = keep.shape[1:]
    return call(
        add_kernel,
        (),
        (keep, flip(send, 0, 1)),
        [(block, jnp.float32)] + [(block, jnp.bfloat16)] * 3,
        name="core_sum",
    )


def split_sums(keep, received, order, name):
    rows = keep.shape[1:]
    return call(
        functools.partial(split_kernel, order),
        (),
        (keep, received),
        [(rows, jnp.float32), (rows, jnp.float32), ((2, *rows), jnp.bfloat16)],
        name=name,
    )


def second_stage(own, beside, received, name):
    rows = own.shape
    return call(
        far_kernel,
        (),
        (own, beside, received),
        [(rows, jnp.float32), (rows, jnp.bfloat16)],
        name=name,
    )


def cross_chips(s0, s1, s2, s3):
    return s0, flip(s1, 0, 2), flip(s2, 1, 0), flip(s3, 1, 2)


def half_sum(keep, received, name):
    _, rows, width = keep.shape
    return call(
        half_kernel,
        (),
        (keep, received),
        [((rows, width), jnp.float32), ((rows, width), jnp.bfloat16)],
        name=name + "_half",
    )


def whole_sum(own, moved, name):
    rows = own[0].shape[0]
    width = sum(piece.shape[1] for piece in own)
    return call(
        functools.partial(whole_kernel, len(own)),
        (),
        (*own, *moved),
        [((64, width), jnp.bfloat16)] * 4 + [((rows - 256, width), jnp.bfloat16)],
        name=name + "_whole",
    )


def hand_rows(parts):
    return [parts[0]] + [flip(parts[j], 0, j) for j in range(1, 4)]


def join(parts, rest, name):
    rows, width = 256 + rest.shape[0], rest.shape[1]
    (joined,) = call(
        join_kernel, (), (*parts, rest), [((rows, width), jnp.bfloat16)], name=name + "_join"
    )
    return joined


def spread_far(joined):
    return flip_z(joined, 2), flip_z(joined, 1)


def in_planes(
    tokens,
    cotangent,
    segments,
    decay_index,
    step_index,
    w_qkv,
    w_gate,
    w_out,
    w_gu,
    w_down,
    persist_keys,
    persist_values,
    norm_gain,
    ffn_gain,
):
    bf16, f32 = jnp.bfloat16, jnp.float32
    ctx = lax.axis_index("ctx")
    f = lax.axis_index("fsdp")
    z, x = ctx // 2, ctx % 2
    head = 2 * f + x
    idx = jnp.stack([z, x, f, head]).astype(jnp.int32)

    own = to_plane(tokens[0])
    anywhere = pl.BlockSpec(memory_space=pl.ANY)
    wq_parts = pl.pallas_call(
        pack_qkvg_kernel,
        out_shape=[jax.ShapeDtypeStruct((256 + EXTRA, 512), bf16)] * 2
        + [jax.ShapeDtypeStruct((2, 256 + EXTRA, 512), bf16)],
        in_specs=[sspec(), anywhere, anywhere] + [vspec()] * 3,
        out_specs=[vspec()] * 3,
        scratch_shapes=[pltpu.SemaphoreType.DMA((16,))],
        compiler_params=pltpu.CompilerParams(vmem_limit_bytes=60 * 1024 * 1024),
        cost_estimate=pl.CostEstimate(flops=1000, bytes_accessed=1000, transcendentals=0),
        name="pack_qkvg",
    )(
        idx,
        w_qkv,
        w_gate,
        persist_keys,
        persist_values,
        jnp.concatenate([norm_gain, ffn_gain]).reshape(1, 512),
    )
    gu_parts = call(
        pack_gu_kernel,
        (idx,),
        (w_gu,),
        [((256, 768), bf16)] * 2 + [((2, 128, 768), bf16)],
        name="pack_gu",
    )
    ints = jnp.concatenate([segments[0], decay_index[0].reshape(-1), step_index[0].reshape(-1)])
    ints = to_plane(after(ints.reshape(10, 128), wq_parts[0]))
    rates = jnp.stack(
        [0.6 * jnp.exp2(-ints[8].astype(f32)), 0.1 * jnp.exp2(-ints[9].astype(f32))]
    )
    far = flip(wq_parts[2], 0, 2)
    wq_parts = [wq_parts[0], flip(wq_parts[1], 0, 1), far, flip(far, 0, 1)]
    own = after(own, wq_parts[0])
    near = gather_chips(own)
    own_cot = to_plane(after(cotangent[0], own))
    gu_far = flip(after(gu_parts[2], own), 0, 2)
    blocks = gather_cores(near)
    rates = after(rates, own_cot)
    ready = after(own_cot, near[2])
    cot_near = [own_cot, flip(ready, 0, 2), flip(ready, 1, 0)]
    cot_near += [flip(cot_near[1], 1, 0)]
    rates = rates
    block = (128, 1024)
    quad = ((4, 128, 1024), bf16)
    (
        send,
        keep,
        normed,
        w_full,
        qkv,
        gate,
        att,
        rec,
        probs,
        pprobs,
        states,
        mixed,
        gain_one,
        gain_two,
        pk,
        pv,
    ) = call(
        mixer_forward_kernel,
        (idx, rates),
        (ints, *blocks, *wq_parts, w_out),
        [
            quad,
            quad,
            ((1024, 1024), bf16),
            ((1024, 512), bf16),
            ((1024, 384), bf16),
            ((1024, 128), f32),
            ((1024, 128), f32),
            ((1024, 128), f32),
            ((1024, 1024), bf16),
            ((1024, 16), bf16),
            ((16, 128, 128), bf16),
            ((1024, 128), bf16),
            ((1, 1024), f32),
            ((1, 1024), f32),
            ((16, 128), bf16),
            ((16, 128), bf16),
        ],
        name="mixer_forward",
        spare=10,
        us=10.0,
    )
    send = after(send, *cot_near[1:], gu_far)
    sums = sum_cores(keep, send)
    shares = cross_chips(*sums)
    gu_next = flip_z(gu_far, 1)
    gu_parts = [gu_parts[0], flip(gu_parts[1], 0, 1), gu_far, flip(gu_far, 0, 1)]
    gu_parts += [gu_next, flip(after(gu_next, shares[3]), 0, 1)]
    cots = gather_cores(cot_near)
    residual, feed = call(
        residual_kernel,
        (),
        (own, gain_two, *shares),
        [(block, f32), (block, bf16)],
        name="residual",
    )
    feeds = gather_cores(gather_chips(feed))
    send_g, keep_g, send_d, keep_d, active, dgu = call(
        feed_kernel,
        (idx,),
        (*feeds, *cots, *gu_parts, w_down),
        [
            quad,
            quad,
            quad,
            quad,
            ((1024, HIDDEN_PAD), bf16),
            ((1024, 2 * HIDDEN_PAD), bf16),
        ],
        scratch=[((1024, 2 * HIDDEN_PAD), bf16), ((HIDDEN_PAD, 1024), bf16)],
        name="feed",
        spare=10,
        us=7.5,
    )
    feed_keep, feed_later_keep, feed_send, feed_later_send = call(
        feed_weights_kernel,
        (idx,),
        (dgu, active, *feeds, *cots),
        [((2, 256 + 4 * Z_HIDDEN // 3, HIDDEN_PAD), bf16)] * 4,
        scratch=[
            ((256, 768), f32),
            ((HIDDEN_PAD, 1024), f32),
            ((1024, 1024), bf16),
            ((1024, 1024), bf16),
            ((256 + 4 * Z_HIDDEN // 3, 768), bf16),
        ],
        name="feed_weights",
        spare=10,
        us=3.5,
    )
    sums = sum_cores(after(keep_g, feed_send), send_g)
    send_d = after(send_d, sums[0])
    shares = cross_chips(*sums)
    feed_received = flip_z(feed_send, 1)
    feed_later_received = flip_z(after(feed_later_send, sums[0]), 1)
    out_sums = split_sums(keep_d, flip(send_d, 0, 1), (0, 1, 2, 3), "output_cores")
    grad_residual, branch = call(
        branch_kernel,
        (),
        (residual, gain_two, after(own_cot, out_sums[0]), *shares),
        [(block, f32), (block, bf16)],
        name="branch",
    )
    feed_own, feed_passed = half_sum(after(feed_keep, branch), feed_received, "feed")
    branch_near = gather_chips(branch, after(branch, feed_passed))
    feed_moved = flip_z(feed_passed, 2)
    branches = gather_cores(branch_near)
    feed_later, feed_later_passed = half_sum(
        after(feed_later_keep, branch_near[3]), feed_later_received, "feed_later"
    )
    rates = after(rates, feed_later_passed, feed_moved)
    feed_later_moved = flip_z(feed_later_passed, 2)
    out_shares = (out_sums[0], flip(after(out_sums[2], branches[6]), 1, 0))
    send, keep, dqkvg, branch_all = call(
        mixer_backward_kernel,
        (idx, rates),
        (*branches, w_out, w_full, qkv, gate, att, rec, probs, pprobs, states, pk, pv),
        [
            ((4, 128 + EXTRA, 1024), bf16),
            ((4, 128 + EXTRA, 1024), bf16),
            ((1024, 512), bf16),
            ((1024, 1024), bf16),
        ],
        scratch=[
            ((1024, 128), bf16),
            ((1024, 1024), bf16),
            ((1024, 128), f32),
            ((1024, 128), f32),
            ((1024, 16), bf16),
        ],
        name="mixer_backward",
        spare=10,
        us=13.0,
    )
    send, dqkvg = lax.optimization_barrier(
        (send, dqkvg, feed_moved, feed_later_moved, *out_shares[1:])
    )[:2]
    *feed_parts, feed_rest = whole_sum(
        (after(feed_own, send), feed_later), (feed_moved, feed_later_moved), "feed"
    )
    feed_parts = hand_rows(feed_parts)
    dqkvg = after(dqkvg, feed_rest)
    mixer_keep, mixer_send = call(
        mixer_weights_kernel,
        (idx,),
        (normed, dqkvg, mixed, branch_all),
        [((2, 320, 512), bf16)] * 2,
        scratch=[((256, 512), f32), ((128, 1024), f32)],
        name="mixer_weights",
        spare=10,
        us=2.2,
    )
    out_own, out_passed = second_stage(
        after(out_sums[0], mixer_send), out_sums[1], out_shares[1], "output_far"
    )
    out_shares = (out_own, flip(out_passed, 0, 2))
    (result,) = call(output_kernel, (), (residual, *out_shares), [(block, bf16)], name="output")
    tokens_sums = split_sums(
        after(keep, feed_rest),
        flip(send, 0, 1),
        (0, 1, 2, 3),
        "tokens_cores",
    )
    feed_joined = join(feed_parts, after(feed_rest, mixer_send, tokens_sums[0]), "feed")
    feed_second = flip_z(feed_joined, 2)
    feed_beside = flip(feed_joined, 1, 0)
    mixer_own, mixer_passed = half_sum(
        after(mixer_keep, feed_joined, result), flip_z(mixer_send, 1), "mixer"
    )
    mixer_moved = flip_z(mixer_passed, 2)
    feed_first = flip_z(feed_joined, 1)
    tokens_far = flip(after(tokens_sums[2], mixer_passed), 1, 0)
    feed_first_beside = flip(after(feed_first, mixer_passed), 1, 0)
    mixer_own = after(mixer_own, feed_beside)
    *mixer_parts, mixer_rest = whole_sum((mixer_own,), (mixer_moved,), "mixer")
    feed_third = flip_z(after(feed_second, mixer_rest), 1)
    feed_second_beside = flip(after(feed_second, mixer_rest), 1, 0)
    mixer_joined = join(
        hand_rows(mixer_parts), after(mixer_rest, tokens_far, feed_first_beside), "mixer"
    )
    mixer_second, mixer_first = spread_far(mixer_joined)
    mixer_beside = flip(mixer_joined, 1, 0)
    result = to_plane(after(result,   mixer_first))
    feed_third_beside = flip(
        after(
            feed_third,
            mixer_joined,


        ),
        1,
        0,
    )
    tokens_own, tokens_passed = second_stage(
        after(
            tokens_sums[0],
            mixer_joined,


        ),
        tokens_sums[1],
        tokens_far,
        "tokens_far",
    )
    tokens_near = flip(tokens_passed, 0, 2)
    mixer_second = after(
        mixer_second,
        mixer_first,
        mixer_beside,
        feed_second_beside,
        tokens_near,
    )
    mixer_third = flip_z(mixer_second, 1)
    mixer_first_beside = flip(after(mixer_first, mixer_second), 1, 0)
    mixer_second_beside = flip(mixer_second, 1, 0)
    grad_tokens, persist = call(
        tokens_kernel,
        (),
        (after(own, mixer_second), gain_one, grad_residual, tokens_own, tokens_near),
        [(block, bf16), ((8, 1024), f32)],
        name="tokens",
    )
    grad_tokens = to_plane(grad_tokens)
    persist = persist + after(flip_z(persist, 1), mixer_third)
    feed_pieces = (
        feed_joined,
        feed_beside,
        feed_first,
        feed_first_beside,
        feed_second,
        feed_second_beside,
        feed_third,
        feed_third_beside,
    )

    grad_gu, grad_down, grad_ffn = call(
        feed_unpack_kernel,
        (idx,),
        (*feed_pieces, w_gu, after(ffn_gain.reshape(1, 256), mixer_second)),
        [((256, 2 * FF), f32), ((FF // 4, 1024), f32), ((1, 256), f32)],
        scratch=[((4, 8, 64, 768), bf16)],
        name="feed_unpack",
        spare=10,
        us=5.5,
    )
    mixer_third_beside = flip(
        after(
            mixer_third,
            grad_ffn,
            mixer_first_beside, mixer_second_beside,

        ),
        1,
        0,
    )
    persist = persist + flip_z(persist, 2)
    mixer_pieces = (
        mixer_joined,
        mixer_beside,
        mixer_first,
        mixer_first_beside,
        mixer_second,
        mixer_second_beside,
        mixer_third,
        mixer_third_beside,
    )
    grad_qkv, grad_gate, grad_out, grad_norm = call(
        mixer_unpack_kernel,
        (idx,),
        (*mixer_pieces, w_qkv, w_gate, after(norm_gain.reshape(1, 256))),
        [
            ((256, 3072), f32),
            ((256, 1024), f32),
            ((256, 1024), f32),
            ((1, 256), f32),
        ],
        name="mixer_unpack",
    )
    return (
        result[None],
        grad_tokens.astype(f32)[None],
        grad_qkv,
        grad_gate,
        grad_out,
        grad_gu,
        grad_down,
        persist[0:4],
        persist[4:8],
        grad_norm.reshape(256),
        grad_ffn.reshape(256),
    )


def solution(mesh):
    in_specs = (
        P("fsdp", "ctx", None),
        P("fsdp", "ctx", None),
        P("fsdp", None),
        P("fsdp", None, None),
        P("fsdp", None, None),
        P("fsdp", None),
        P("fsdp", None),
        P("fsdp", None),
        P("fsdp", None),
        P("fsdp", None),
        P("fsdp", None),
        P("fsdp", None),
        P("fsdp"),
        P("fsdp"),
    )
    out_specs = (
        P("fsdp", "ctx", None),
        P("fsdp", "ctx", None),
        P("fsdp", None),
        P("fsdp", None),
        P("fsdp", None),
        P("fsdp", None),
        P("fsdp", None),
        P("fsdp", None),
        P("fsdp", None),
        P("fsdp"),
        P("fsdp"),
    )
    planes = dict(mesh.shape) == {"ctx": HEADS, "fsdp": PLANES}
    return jax.shard_map(
        in_planes if planes else on_device, mesh=mesh, in_specs=in_specs, out_specs=out_specs, check_vma=False
    )
```

```python
import functools

import jax
import jax.numpy as jnp
import numpy as np
from jax import lax
from jax.experimental import pallas as pl
from jax.experimental.pallas import tpu as pltpu
from jax.sharding import PartitionSpec as P

HEADS = 8
HEAD_WIDTH_SIZE = 128
FF = 2816
GROUP = 64


epsilon = 1e-06
momentum = 0.9
masked_score = -1e30
highest_precision = lax.Precision.HIGHEST


def rms_scale(values):
    return lax.rsqrt(jnp.mean(values * values, axis=-1, keepdims=True) + epsilon)


def norm_back(values, inv_rms, gain_vec, grad_normed):
    scaled_grad = grad_normed * gain_vec
    grad_gain = jnp.sum(grad_normed * values * inv_rms, axis=0)
    grad_values = inv_rms * scaled_grad - values * inv_rms * inv_rms * inv_rms * jnp.mean(
        scaled_grad * values, axis=-1, keepdims=True
    )
    return (grad_values, grad_gain)


def place_rows(row_index, shard_rows, dev_count):
    half_rows = shard_rows // 2
    owner_dev = row_index // shard_rows
    inner_row = row_index % shard_rows
    block_id = jnp.where(inner_row < half_rows, owner_dev, 2 * dev_count - 1 - owner_dev)
    return block_id * half_rows + inner_row % half_rows


def position_order(stored, dev_count):
    rows = stored.shape[0]
    rest = stored.shape[1:]
    split = stored.reshape((dev_count, 2, rows // (2 * dev_count)) + rest)
    early = split[:, 0].reshape((-1,) + rest)
    late = split[::-1, 1].reshape((-1,) + rest)
    return jnp.concatenate([early, late], axis=0)


def key_mask(query_pos, query_seg, key_pos, key_seg):
    return (key_seg[None, :] == query_seg[:, None]) & (key_pos[None, :] <= query_pos[:, None])


def head_scores(queries, key_block):
    return jnp.einsum(
        "qhd,khd->hqk", queries, key_block, preferred_element_type=jnp.float32
    ) * HEAD_WIDTH_SIZE ** (-0.5)


def online_step(running, scores, value_block):
    run_max, run_total, accumulated = running
    new_max = jnp.maximum(run_max, jnp.max(scores, axis=-1))
    rescale = jnp.exp(run_max - new_max)
    weights = jnp.exp(scores - new_max[:, :, None])
    run_total = run_total * rescale + jnp.sum(weights, axis=-1)
    update = jnp.einsum(
        "hqk,khd->qhd",
        weights.astype(jnp.bfloat16),
        value_block,
        preferred_element_type=jnp.float32,
    )
    accumulated = accumulated * jnp.transpose(rescale)[:, :, None] + update
    return (new_max, run_total, accumulated)


def fold_keys(running, all_keys, all_values, context):
    queries, query_pos, query_seg, segment_all, shard_rows, dev_count = context
    total_rows = all_keys.shape[0]
    block_rows = min(512, total_rows)

    def fold_one_block(carried, block_index):
        offset_row = block_index * block_rows
        key_block = lax.dynamic_slice_in_dim(all_keys, offset_row, block_rows, 0).reshape(
            block_rows, HEADS, HEAD_WIDTH_SIZE
        )
        value_block = lax.dynamic_slice_in_dim(all_values, offset_row, block_rows, 0).reshape(
            block_rows, HEADS, HEAD_WIDTH_SIZE
        )
        key_pos = place_rows(
            offset_row + jnp.arange(block_rows, dtype=jnp.int32), shard_rows, dev_count
        )
        key_seg = jnp.take(segment_all, key_pos)
        allowed = key_mask(query_pos, query_seg, key_pos, key_seg)
        scores = jnp.where(allowed[None], head_scores(queries, key_block), masked_score)
        carried = online_step(carried, scores, value_block)
        return (carried, None)

    running, _ = lax.scan(
        fold_one_block, running, jnp.arange(total_rows // block_rows, dtype=jnp.int32)
    )
    return running


def back_every_key(grad_query, all_keys, all_values, context, grad_heads, log_total, row_delta):
    queries, query_pos, query_seg, segment_all, shard_rows, dev_count = context
    total_rows = all_keys.shape[0]
    block_rows = min(512, total_rows)
    scale_factor = HEAD_WIDTH_SIZE ** (-0.5)

    def back_one_block(carried, block_index):
        offset_row = block_index * block_rows
        key_block = lax.dynamic_slice_in_dim(all_keys, offset_row, block_rows, 0).reshape(
            block_rows, HEADS, HEAD_WIDTH_SIZE
        )
        value_block = lax.dynamic_slice_in_dim(all_values, offset_row, block_rows, 0).reshape(
            block_rows, HEADS, HEAD_WIDTH_SIZE
        )
        key_pos = place_rows(
            offset_row + jnp.arange(block_rows, dtype=jnp.int32), shard_rows, dev_count
        )
        key_seg = jnp.take(segment_all, key_pos)
        allowed = key_mask(query_pos, query_seg, key_pos, key_seg)
        scores = jnp.where(allowed[None], head_scores(queries, key_block), masked_score)
        prob_block = jnp.exp(scores - log_total[:, :, None])
        grad_prob = jnp.einsum(
            "qhd,khd->hqk", grad_heads, value_block, preferred_element_type=jnp.float32
        )
        grad_scores = (prob_block * (grad_prob - row_delta[:, :, None])).astype(jnp.bfloat16)
        query_grad = (
            carried
            + jnp.einsum("hqk,khd->qhd", grad_scores, key_block, preferred_element_type=jnp.float32)
            * scale_factor
        )
        key_grad = (
            jnp.einsum("hqk,qhd->khd", grad_scores, queries, preferred_element_type=jnp.float32)
            * scale_factor
        )
        value_grad = jnp.einsum(
            "hqk,qhd->khd",
            prob_block.astype(jnp.bfloat16),
            grad_heads,
            preferred_element_type=jnp.float32,
        )
        return (query_grad, (key_grad, value_grad))

    grad_query, (key_grads, value_grads) = lax.scan(
        back_one_block, grad_query, jnp.arange(total_rows // block_rows, dtype=jnp.int32)
    )
    return (
        grad_query,
        key_grads.reshape(total_rows, HEADS, HEAD_WIDTH_SIZE),
        value_grads.reshape(total_rows, HEADS, HEAD_WIDTH_SIZE),
    )


def group_step(stacked_rows, group_key_rows, group_value_rows, alpha_row, learning_rate_row):
    current_memory = stacked_rows[:, :HEAD_WIDTH_SIZE]
    moment_now = stacked_rows[:, HEAD_WIDTH_SIZE:]
    gram_matrix = (
        jnp.einsum("thk,thj->hkj", group_key_rows, group_key_rows, precision=highest_precision)
        * learning_rate_row[:, None, None]
    )
    mixed_product = (
        jnp.einsum("qgw,qgc->gwc", group_key_rows, group_value_rows, precision=highest_precision)
        * learning_rate_row[:, None, None]
    )
    memory_gradient = (
        jnp.einsum("fld,fdi->fli", gram_matrix, current_memory, precision=highest_precision)
        - mixed_product
    )
    moment_next = momentum * moment_now - memory_gradient
    memory_next = (1.0 - alpha_row)[:, None, None] * current_memory + moment_next
    return jnp.concatenate([memory_next, moment_next], axis=1)


def run_block(stacked_rows, query_part, key_part, value_part, alphas, thetas):
    scale_factor = HEAD_WIDTH_SIZE ** (-0.5)
    group_query_rows = query_part * scale_factor
    recalled_rows = [
        jnp.einsum(
            "ipb,pbx->ipx",
            group_query_rows,
            stacked_rows[:, :HEAD_WIDTH_SIZE],
            precision=highest_precision,
        )
    ]
    stacked_rows = group_step(
        stacked_rows, key_part * scale_factor, value_part, alphas[0], thetas[0]
    )
    return (jnp.concatenate(recalled_rows, axis=0), stacked_rows)


def states_before(key_order, value_order, alpha_all, theta_all, early_index, late_index):
    groups = alpha_all.shape[0]
    scale_factor = HEAD_WIDTH_SIZE ** (-0.5)
    key_groups = key_order.reshape(groups, GROUP, HEADS, HEAD_WIDTH_SIZE)
    value_groups = value_order.reshape(groups, GROUP, HEADS, HEAD_WIDTH_SIZE)
    zero_state = jnp.zeros((HEADS, 2 * HEAD_WIDTH_SIZE, HEAD_WIDTH_SIZE), jnp.float32)

    def states_one_group(carried, inputs):
        stacked_rows, into_early, into_late = carried
        group_key_rows, group_value_rows, alpha_row, learning_rate_row, group_index = inputs
        into_early = jnp.where(group_index == early_index, stacked_rows, into_early)
        into_late = jnp.where(group_index == late_index, stacked_rows, into_late)
        current_memory = stacked_rows[:, :HEAD_WIDTH_SIZE]
        moment_now = stacked_rows[:, HEAD_WIDTH_SIZE:]
        gram_matrix = (
            jnp.einsum(
                "thk,thj->hkj", group_key_rows, group_key_rows, preferred_element_type=jnp.float32
            )
            * (learning_rate_row / HEAD_WIDTH_SIZE)[:, None, None]
        )
        mixed_product = (
            jnp.einsum(
                "qgw,qgc->gwc", group_key_rows, group_value_rows, preferred_element_type=jnp.float32
            )
            * (learning_rate_row * scale_factor)[:, None, None]
        )
        memory_gradient = (
            jnp.einsum("fld,fdi->fli", gram_matrix, current_memory, precision=highest_precision)
            - mixed_product
        )
        moment_next = momentum * moment_now - memory_gradient
        memory_next = (1.0 - alpha_row)[:, None, None] * current_memory + moment_next
        stacked_rows = jnp.concatenate([memory_next, moment_next], axis=1)
        return ((stacked_rows, into_early, into_late), None)

    (_, into_early, into_late), _ = lax.scan(
        states_one_group,
        (zero_state, zero_state, zero_state),
        (key_groups, value_groups, alpha_all, theta_all, jnp.arange(groups, dtype=jnp.int32)),
    )
    return (into_early, into_late)


def adjoints_after(
    query_order, key_order, recall_grad_order, alpha_all, theta_all, early_end, late_end
):
    groups = alpha_all.shape[0]
    scale_factor = HEAD_WIDTH_SIZE ** (-0.5)
    query_groups = query_order.reshape(groups, GROUP, HEADS, HEAD_WIDTH_SIZE)
    key_groups = key_order.reshape(groups, GROUP, HEADS, HEAD_WIDTH_SIZE)
    grad_groups = recall_grad_order.reshape(groups, GROUP, HEADS, HEAD_WIDTH_SIZE)
    zero_state = jnp.zeros((HEADS, 2 * HEAD_WIDTH_SIZE, HEAD_WIDTH_SIZE), jnp.float32)

    def adjoints_one_group(carried, inputs):
        adjoint, out_early, out_late = carried
        (
            group_query_rows,
            group_key_rows,
            gradient_group_rows,
            alpha_row,
            learning_rate_row,
            group_index,
        ) = inputs
        out_early = jnp.where(group_index + 1 == early_end, adjoint, out_early)
        out_late = jnp.where(group_index + 1 == late_end, adjoint, out_late)
        gram_matrix = (
            jnp.einsum(
                "thk,thj->hkj", group_key_rows, group_key_rows, preferred_element_type=jnp.float32
            )
            * (learning_rate_row / HEAD_WIDTH_SIZE)[:, None, None]
        )
        query_term = (
            jnp.einsum(
                "qgw,qgc->gwc",
                group_query_rows,
                gradient_group_rows,
                preferred_element_type=jnp.float32,
            )
            * scale_factor
        )
        grad_m = adjoint[:, :HEAD_WIDTH_SIZE]
        summed_rows = grad_m + adjoint[:, HEAD_WIDTH_SIZE:]
        new_m = (
            (1.0 - alpha_row)[:, None, None] * grad_m
            + query_term
            - jnp.einsum("fld,fdi->fli", gram_matrix, summed_rows, precision=highest_precision)
        )
        adjoint = jnp.concatenate([new_m, momentum * summed_rows], axis=1)
        return ((adjoint, out_early, out_late), None)

    (_, out_early, out_late), _ = lax.scan(
        adjoints_one_group,
        (zero_state, zero_state, zero_state),
        (
            query_groups,
            key_groups,
            grad_groups,
            alpha_all,
            theta_all,
            jnp.arange(groups, dtype=jnp.int32),
        ),
        reverse=True,
    )
    return (out_early, out_late)


def on_device(
    tokens,
    cotangent,
    segments,
    decay_index,
    step_index,
    w_qkv,
    w_gate,
    w_out,
    w_gu,
    w_down,
    persist_keys,
    persist_values,
    norm_gain,
    ffn_gain,
):
    shard_rows = tokens.shape[1]
    model_width = tokens.shape[2]
    half_rows = shard_rows // 2
    dev_count = lax.axis_size("ctx")
    device = lax.axis_index("ctx")
    scale_factor = HEAD_WIDTH_SIZE ** (-0.5)
    full_weights = (
        lax.all_gather(w_qkv, "fsdp", axis=0, tiled=True),
        lax.all_gather(w_gate, "fsdp", axis=0, tiled=True),
        lax.all_gather(w_out, "fsdp", axis=0, tiled=True),
        lax.all_gather(w_gu, "fsdp", axis=0, tiled=True),
        lax.all_gather(w_down, "fsdp", axis=0, tiled=True),
        lax.all_gather(persist_keys, "fsdp", axis=0, tiled=True),
        lax.all_gather(persist_values, "fsdp", axis=0, tiled=True),
        lax.all_gather(norm_gain, "fsdp", axis=0, tiled=True),
        lax.all_gather(ffn_gain, "fsdp", axis=0, tiled=True),
    )
    wq_full, wg_full, wo_full, wgu_full, wd_full, pkeys_full, pvalues_full, gain_attn, gain_ffn = (
        full_weights
    )
    gain_attn32 = gain_attn.astype(jnp.float32)
    gain_ffn32 = gain_ffn.astype(jnp.float32)
    pkeys_heads = pkeys_full.reshape(-1, HEADS, HEAD_WIDTH_SIZE)
    pvalues_heads = pvalues_full.reshape(-1, HEADS, HEAD_WIDTH_SIZE)
    inputs32 = tokens[0].astype(jnp.float32)
    inv_rms_one = rms_scale(inputs32)
    normed_low = (inputs32 * inv_rms_one * gain_attn32).astype(jnp.bfloat16)
    projected = jnp.dot(normed_low, wq_full, preferred_element_type=jnp.float32)
    query_flat = projected[:, :model_width].astype(jnp.bfloat16)
    key_flat = projected[:, model_width : 2 * model_width].astype(jnp.bfloat16)
    value_flat = projected[:, 2 * model_width :].astype(jnp.bfloat16)
    query_heads = query_flat.reshape(shard_rows, HEADS, HEAD_WIDTH_SIZE)
    gate_open = jax.nn.sigmoid(jnp.dot(normed_low, wg_full, preferred_element_type=jnp.float32))
    local_rows = jnp.arange(shard_rows, dtype=jnp.int32)
    query_pos = place_rows(device * shard_rows + local_rows, shard_rows, dev_count)
    segment_all = segments[0]
    query_seg = jnp.take(segment_all, query_pos)
    context = (query_heads, query_pos, query_seg, segment_all, shard_rows, dev_count)
    all_keys, all_values = (
        lax.all_gather(key_flat, "ctx", axis=0, tiled=True),
        lax.all_gather(value_flat, "ctx", axis=0, tiled=True),
    )
    persist_scores = head_scores(query_heads, pkeys_heads)
    start_state = (
        jnp.full((HEADS, shard_rows), masked_score, jnp.float32),
        jnp.zeros((HEADS, shard_rows), jnp.float32),
        jnp.zeros((shard_rows, HEADS, HEAD_WIDTH_SIZE), jnp.float32),
    )
    running = online_step(start_state, persist_scores, pvalues_heads)
    running = fold_keys(running, all_keys, all_values, context)
    run_max, run_total, accumulated = running
    attended = accumulated / jnp.transpose(run_total)[:, :, None]
    log_total = run_max + jnp.log(run_total)
    group_count = half_rows // GROUP
    alpha_all = 0.6 * jnp.exp2(-decay_index[0].astype(jnp.float32))
    theta_all = 0.1 * jnp.exp2(-step_index[0].astype(jnp.float32))
    early_first = device * group_count
    late_first = (2 * dev_count - 1 - device) * group_count
    alpha_early = lax.dynamic_slice_in_dim(alpha_all, early_first, group_count, 0)
    theta_early = lax.dynamic_slice_in_dim(theta_all, early_first, group_count, 0)
    alpha_late = lax.dynamic_slice_in_dim(alpha_all, late_first, group_count, 0)
    theta_late = lax.dynamic_slice_in_dim(theta_all, late_first, group_count, 0)
    query_f = query_heads.astype(jnp.float32)
    key_f = key_flat.astype(jnp.float32).reshape(shard_rows, HEADS, HEAD_WIDTH_SIZE)
    value_f = value_flat.astype(jnp.float32).reshape(shard_rows, HEADS, HEAD_WIDTH_SIZE)
    early_parts = (query_f[:half_rows], key_f[:half_rows], value_f[:half_rows])
    late_parts = (query_f[half_rows:], key_f[half_rows:], value_f[half_rows:])

    def early_run(stacked_rows, query_part, key_part, value_part):
        return run_block(stacked_rows, query_part, key_part, value_part, alpha_early, theta_early)

    def late_run(stacked_rows, query_part, key_part, value_part):
        return run_block(stacked_rows, query_part, key_part, value_part, alpha_late, theta_late)

    into_early, into_late = states_before(
        position_order(all_keys, dev_count),
        position_order(all_values, dev_count),
        alpha_all,
        theta_all,
        early_first,
        late_first,
    )
    recall_early, _ = early_run(into_early, early_parts[0], early_parts[1], early_parts[2])
    recall_late, _ = late_run(into_late, late_parts[0], late_parts[1], late_parts[2])
    recall = jnp.concatenate([recall_early, recall_late], axis=0).reshape(shard_rows, model_width)
    mixed_low = (attended.reshape(shard_rows, model_width) + gate_open * recall).astype(
        jnp.bfloat16
    )
    residual = inputs32 + jnp.dot(mixed_low, wo_full, preferred_element_type=jnp.float32)
    inv_rms_two = rms_scale(residual)
    normed_two = (residual * inv_rms_two * gain_ffn32).astype(jnp.bfloat16)
    gate_up = jnp.dot(normed_two, wgu_full, preferred_element_type=jnp.float32)
    gate_part = gate_up[:, :FF]
    up_part = gate_up[:, FF:]
    active = (jax.nn.silu(gate_part) * up_part).astype(jnp.bfloat16)
    result = residual + jnp.dot(active, wd_full, preferred_element_type=jnp.float32)
    cot_low = cotangent[0]
    grad_w_down = jnp.einsum("tf,td->fd", active, cot_low, preferred_element_type=jnp.float32)
    grad_active = jnp.einsum("td,fd->tf", cot_low, wd_full, preferred_element_type=jnp.float32)
    sigma_gate = jax.nn.sigmoid(gate_part)
    grad_gate_part = grad_active * up_part * sigma_gate * (1.0 + gate_part * (1.0 - sigma_gate))
    grad_up_part = grad_active * gate_part * sigma_gate
    grad_gu_low = jnp.concatenate([grad_gate_part, grad_up_part], axis=1).astype(jnp.bfloat16)
    grad_w_gu = jnp.einsum("td,tf->df", normed_two, grad_gu_low, preferred_element_type=jnp.float32)
    grad_normed_two = jnp.einsum(
        "tf,df->td", grad_gu_low, wgu_full, preferred_element_type=jnp.float32
    )
    grad_res_norm, grad_ffn_gain = norm_back(residual, inv_rms_two, gain_ffn32, grad_normed_two)
    grad_residual = cot_low.astype(jnp.float32) + grad_res_norm
    grad_branch = grad_residual.astype(jnp.bfloat16)
    grad_w_out = jnp.einsum("td,te->de", mixed_low, grad_branch, preferred_element_type=jnp.float32)
    grad_mixed_low = jnp.einsum(
        "te,de->td", grad_branch, wo_full, preferred_element_type=jnp.float32
    ).astype(jnp.bfloat16)
    grad_mixed32 = grad_mixed_low.astype(jnp.float32)
    grad_gate_low = (grad_mixed32 * recall * gate_open * (1.0 - gate_open)).astype(jnp.bfloat16)
    grad_w_gate = jnp.einsum(
        "td,tf->df", normed_low, grad_gate_low, preferred_element_type=jnp.float32
    )
    recall_grad_low = (grad_mixed32 * gate_open).astype(jnp.bfloat16)
    grad_recall = recall_grad_low.astype(jnp.float32).reshape(shard_rows, HEADS, HEAD_WIDTH_SIZE)
    grad_heads = grad_mixed_low.reshape(shard_rows, HEADS, HEAD_WIDTH_SIZE)
    row_delta = jnp.transpose(jnp.sum(grad_heads.astype(jnp.float32) * attended, axis=-1))
    memory_queries, all_recall_grads = (
        lax.all_gather(query_flat, "ctx", axis=0, tiled=True),
        lax.all_gather(recall_grad_low, "ctx", axis=0, tiled=True),
    )
    out_early, out_late = adjoints_after(
        position_order(memory_queries, dev_count),
        position_order(all_keys, dev_count),
        position_order(all_recall_grads, dev_count),
        alpha_all,
        theta_all,
        early_first + group_count,
        late_first + group_count,
    )
    _, pull_early = jax.vjp(early_run, into_early, early_parts[0], early_parts[1], early_parts[2])
    _, grad_qe, grad_ke, grad_ve = pull_early((grad_recall[:half_rows], out_early))
    _, pull_late = jax.vjp(late_run, into_late, late_parts[0], late_parts[1], late_parts[2])
    _, grad_ql, grad_kl, grad_vl = pull_late((grad_recall[half_rows:], out_late))
    grad_q_mem = jnp.concatenate([grad_qe, grad_ql], axis=0).reshape(shard_rows, model_width)
    grad_k_mem = jnp.concatenate([grad_ke, grad_kl], axis=0).reshape(shard_rows, model_width)
    grad_v_mem = jnp.concatenate([grad_ve, grad_vl], axis=0).reshape(shard_rows, model_width)
    persist_probs = jnp.exp(persist_scores - log_total[:, :, None])
    persist_grad_prob = jnp.einsum(
        "qhd,phd->hqp", grad_heads, pvalues_heads, preferred_element_type=jnp.float32
    )
    persist_ds = (persist_probs * (persist_grad_prob - row_delta[:, :, None])).astype(jnp.bfloat16)
    grad_query_att = (
        jnp.einsum("hqp,phd->qhd", persist_ds, pkeys_heads, preferred_element_type=jnp.float32)
        * scale_factor
    )
    grad_pkeys = (
        jnp.einsum("hqp,qhd->phd", persist_ds, query_heads, preferred_element_type=jnp.float32)
        * scale_factor
    )
    grad_pvalues = jnp.einsum(
        "hqp,qhd->phd",
        persist_probs.astype(jnp.bfloat16),
        grad_heads,
        preferred_element_type=jnp.float32,
    )
    grad_query_att, key_grads_all, value_grads_all = back_every_key(
        grad_query_att, all_keys, all_values, context, grad_heads, log_total, row_delta
    )
    key_grad_att, value_grad_att = (
        lax.psum_scatter(key_grads_all, "ctx", scatter_dimension=0, tiled=True),
        lax.psum_scatter(value_grads_all, "ctx", scatter_dimension=0, tiled=True),
    )
    grad_query = grad_query_att.reshape(shard_rows, model_width) + grad_q_mem
    grad_key = key_grad_att.reshape(shard_rows, model_width) + grad_k_mem
    grad_value = value_grad_att.reshape(shard_rows, model_width) + grad_v_mem
    grad_qkv_low = jnp.concatenate([grad_query, grad_key, grad_value], axis=1).astype(jnp.bfloat16)
    grad_w_qkv = jnp.einsum(
        "td,tf->df", normed_low, grad_qkv_low, preferred_element_type=jnp.float32
    )
    grad_normed = jnp.einsum(
        "tf,df->td", grad_qkv_low, wq_full, preferred_element_type=jnp.float32
    ) + jnp.einsum("tf,df->td", grad_gate_low, wg_full, preferred_element_type=jnp.float32)
    grad_in_norm, grad_norm_gain = norm_back(inputs32, inv_rms_one, gain_attn32, grad_normed)
    grad_inputs = grad_residual + grad_in_norm
    local_grads = (
        grad_w_qkv,
        grad_w_gate,
        grad_w_out,
        grad_w_gu,
        grad_w_down,
        grad_pkeys.reshape(-1, model_width),
        grad_pvalues.reshape(-1, model_width),
        grad_norm_gain,
        grad_ffn_gain,
    )
    shares = (
        lax.psum_scatter(
            local_grads[0].astype(jnp.bfloat16), "fsdp", scatter_dimension=0, tiled=True
        ).astype(jnp.float32),
        lax.psum_scatter(
            local_grads[1].astype(jnp.bfloat16), "fsdp", scatter_dimension=0, tiled=True
        ).astype(jnp.float32),
        lax.psum_scatter(
            local_grads[2].astype(jnp.bfloat16), "fsdp", scatter_dimension=0, tiled=True
        ).astype(jnp.float32),
        lax.psum_scatter(
            local_grads[3].astype(jnp.bfloat16), "fsdp", scatter_dimension=0, tiled=True
        ).astype(jnp.float32),
        lax.psum_scatter(
            local_grads[4].astype(jnp.bfloat16), "fsdp", scatter_dimension=0, tiled=True
        ).astype(jnp.float32),
        lax.psum_scatter(
            local_grads[5].astype(jnp.bfloat16), "fsdp", scatter_dimension=0, tiled=True
        ).astype(jnp.float32),
        lax.psum_scatter(
            local_grads[6].astype(jnp.bfloat16), "fsdp", scatter_dimension=0, tiled=True
        ).astype(jnp.float32),
        lax.psum_scatter(
            local_grads[7].astype(jnp.bfloat16), "fsdp", scatter_dimension=0, tiled=True
        ).astype(jnp.float32),
        lax.psum_scatter(
            local_grads[8].astype(jnp.bfloat16), "fsdp", scatter_dimension=0, tiled=True
        ).astype(jnp.float32),
    )
    totals = lax.psum(
        (
            shares[0],
            shares[1],
            shares[2],
            shares[3],
            shares[4],
            shares[5],
            shares[6],
            shares[7],
            shares[8],
        ),
        "ctx",
    )
    return (
        result.astype(jnp.bfloat16)[None],
        grad_inputs[None],
        totals[0],
        totals[1],
        totals[2],
        totals[3],
        totals[4],
        totals[5],
        totals[6],
        totals[7],
        totals[8],
    )


PERSIST = 16
PLANES = 4
HIDDEN_PAD = 384
Z_HIDDEN = HIDDEN_PAD // PLANES
FIRST_LANES = 384
EXTRA = 16


def head_of(x, f, k):
    return 2 * (f ^ (k & 3)) + (x ^ (k >> 2))


def linear(z, x, f):
    return (2 * z + x) * 4 + f


def shift(value, move):
    pairs = []
    for z in range(4):
        for x in range(2):
            for f in range(4):
                pairs.append((linear(z, x, f), linear(*move(z, x, f))))
    return lax.ppermute(value, ("ctx", "fsdp"), pairs)


def to_plane(value):
    return shift(value, lambda z, x, f: (f, x, z))


def flip(value, dx, df):
    return shift(value, lambda z, x, f: (z, x ^ dx, f ^ df))


def flip_z(value, dz):
    return shift(value, lambda z, x, f: (z ^ dz, x, f))


def gather_chips(block, last=None):
    last = block if last is None else last
    return [block, flip(block, 0, 2), flip(block, 1, 0), flip(last, 1, 2)]


def gather_cores(near):
    far = [flip(b, 0, 1) for b in near]
    return [near[0], far[0], near[1], far[1], near[2], far[2], near[3], far[3]]


def dot_nn(a, b):
    return lax.dot_general(a, b, (((1,), (0,)), ((), ())), preferred_element_type=jnp.float32)


def dot_nt(a, b):
    return lax.dot_general(a, b, (((1,), (1,)), ((), ())), preferred_element_type=jnp.float32)


def dot_tn(a, b):
    return lax.dot_general(a, b, (((0,), (0,)), ((), ())), preferred_element_type=jnp.float32)


def split_two(value):
    high = value.astype(jnp.bfloat16)
    return high, (value - high.astype(jnp.float32)).astype(jnp.bfloat16)


def product_three(a, b_high, b_low):
    a_high, a_low = split_two(a)
    return dot_nn(a_high, b_high) + dot_nn(a_low, b_high) + dot_nn(a_high, b_low)


def vspec():
    return pl.BlockSpec(memory_space=pltpu.VMEM)


def sspec():
    return pl.BlockSpec(memory_space=pltpu.SMEM)


def padded_bytes(shape, dtype):
    size = jnp.dtype(dtype).itemsize
    lanes = -(-shape[-1] // 128) * 128
    rows = -(-shape[-2] // (32 // size)) * (32 // size)
    return int(np.prod(shape[:-2])) * rows * lanes * size


def call(kernel, smem, operands, outs, scratch=(), name=None, spare=6, us=0.5):
    held = [(o.shape, o.dtype) for o in operands] + list(outs) + list(scratch)
    limit = sum(padded_bytes(shape, dtype) for shape, dtype in held) + spare * 1024 * 1024
    return pl.pallas_call(
        kernel,
        out_shape=[jax.ShapeDtypeStruct(shape, dtype) for shape, dtype in outs],
        in_specs=[sspec()] * len(smem) + [vspec()] * len(operands),
        out_specs=[vspec()] * len(outs),
        scratch_shapes=[pltpu.VMEM(shape, dtype) for shape, dtype in scratch],
        compiler_params=pltpu.CompilerParams(vmem_limit_bytes=limit),
        cost_estimate=pl.CostEstimate(
            flops=int(us * 1.1e9), bytes_accessed=1000, transcendentals=0
        ),
        name=name,
    )(*smem, *operands)


def after(value, *others):
    return lax.optimization_barrier((value, *others))[0]


def pack_qkvg_kernel(idx, wq, wg, pk, pv, gains, o0, o1, o23, sems):
    x, f = idx[1], idx[2]
    copies = []
    for j, out in enumerate((o0, o1, o23.at[0], o23.at[1])):
        start = pl.multiple_of((2 * (f ^ j) + x) * 128, 128)
        for part in range(4):
            first = start if part == 3 else pl.multiple_of(part * 1024 + start, 128)
            source = wg if part == 3 else wq
            copies.append(
                pltpu.make_async_copy(
                    source.at[:, pl.ds(first, 128)],
                    out.at[pl.ds(0, 256), pl.ds(part * 128, 128)],
                    sems.at[4 * j + part],
                )
            )
    for copy in copies:
        copy.start()
    for j, out in enumerate((o0, o1, o23.at[0], o23.at[1])):
        start = pl.multiple_of((2 * (f ^ j) + x) * 128, 128)
        tail = [
            jnp.concatenate([pk[:, pl.ds(start, 128)], pv[:, pl.ds(start, 128)]], axis=1),
            gains[:, 0:256],
            gains[:, 256:512],
            jnp.zeros((EXTRA - 6, 256), jnp.bfloat16),
        ]
        tail = jnp.concatenate([t.astype(jnp.float32) for t in tail], axis=0)
        tail = jnp.concatenate([tail, jnp.zeros((EXTRA, 256), jnp.float32)], axis=1)
        out[256 : 256 + EXTRA, :] = tail.astype(jnp.bfloat16)
    for copy in copies:
        copy.wait()


def pack_gu_kernel(idx, wgu, o0, o1, o23):
    z, x, f = idx[0], idx[1], idx[2]
    width = FF // 8
    for j, out in enumerate((o0, o1, o23.at[0], o23.at[1])):
        head = 2 * (f ^ j) + x
        count = 256 if j < 2 else 128
        rows = pl.ds(0 if j < 2 else pl.multiple_of((z & 1) * 128, 128), count)
        pad = jnp.zeros((count, HIDDEN_PAD - width), jnp.bfloat16)
        for h in range(8):

            @pl.when(head == h)
            def _():
                for part in range(2):
                    first = part * FF + h * width
                    at = part * HIDDEN_PAD
                    out[:, at : at + HIDDEN_PAD] = jnp.concatenate(
                        [wgu[rows, first : first + width], pad], axis=1
                    )


def lay_weights(z, f, parts, w_full):
    own, beside, far, far_beside, next_far, next_beside = parts
    w_full[pl.ds(pl.multiple_of(f * 256, 256), 256), :] = own[...]
    w_full[pl.ds(pl.multiple_of((f ^ 1) * 256, 256), 256), :] = beside[...]
    halves = ((2, 0, far, 0), (3, 0, far_beside, 1), (2, 1, next_far, 0), (3, 1, next_beside, 1))
    for j, side, part, which in halves:
        rows = pl.multiple_of((f ^ j) * 256 + ((z ^ side) & 1) * 128, 128)
        w_full[pl.ds(rows, 128), :] = part[which]


def mixer_forward_kernel(idx, rates, ints, *refs):
    blocks = refs[0:8]
    parts = refs[8:12]
    w_out = refs[12]
    send, keep, normed, w_full, qkv, gate, att, rec, probs, pprobs, states, mixed = refs[13:25]
    gain_one, gain_two, pk, pv = refs[25:29]
    x, f = idx[1], idx[2]
    head = 2 * f + x
    scale = HEAD_WIDTH_SIZE ** (-0.5)
    wo = w_out[pl.ds(pl.multiple_of(x * 128, 128), 128), :]
    tails = []
    for j, part in enumerate((parts[0], parts[1], parts[2].at[0], parts[3].at[1])):
        rows = pl.multiple_of((f ^ j) * 256, 256)
        w_full[pl.ds(rows, 256), :] = part[0:256, :]
        tail = part[256 : 256 + EXTRA, 0:256].astype(jnp.float32)
        tails.append(tail)
        gain_one[:, pl.ds(rows, 256)] = tail[4:5]
        gain_two[:, pl.ds(rows, 256)] = tail[5:6]
    tails = jnp.concatenate([tail[0:4] for tail in tails], axis=0).astype(jnp.bfloat16)
    pk[...] = tails[:, 0:128]
    pv[...] = tails[:, 128:256]
    gain_row = gain_one[...]
    for k in range(8):
        values = blocks[k][...].astype(jnp.float32)
        normed_block = (values * rms_scale(values) * gain_row).astype(jnp.bfloat16)
        hk = head_of(x, f, k)
        normed[pl.ds(pl.multiple_of(hk * 64, 64), 64), :] = normed_block[:64]
        normed[pl.ds(pl.multiple_of((15 - hk) * 64, 64), 64), :] = normed_block[64:]
    state = jnp.zeros((128, 128), jnp.float32)
    moment = jnp.zeros((128, 128), jnp.float32)
    for t in range(8):
        if t % 2 == 0:
            rows = slice(t * 128, t * 128 + 256)
            product = dot_nn(normed[rows, :], w_full[...])
            qkv[rows, :] = product[:, :384].astype(jnp.bfloat16)
            gate[rows, :] = jax.nn.sigmoid(product[:, 384:])
        rows = slice(t * 128, t * 128 + 128)
        width = (t + 1) * 128
        query = qkv[rows, 0:128]
        scores = dot_nt(query, qkv[0:width, 128:256]) * scale
        row_seg = jnp.transpose(jnp.broadcast_to(ints[t : t + 1, :], (128, 128)))[:, 0:1]
        col_seg = jnp.concatenate([ints[u : u + 1, :] for u in range(t + 1)], axis=1)
        row_pos = lax.broadcasted_iota(jnp.int32, (128, width), 0) + t * 128
        col_pos = lax.broadcasted_iota(jnp.int32, (128, width), 1)
        allowed = (row_seg == col_seg) & (col_pos <= row_pos)
        scores = jnp.where(allowed, scores, masked_score)
        pscores = dot_nt(query, pk[...]) * scale
        top = jnp.maximum(
            jnp.max(scores, axis=-1, keepdims=True), jnp.max(pscores, axis=-1, keepdims=True)
        )
        weights = jnp.exp(scores - top)
        pweights = jnp.exp(pscores - top)
        inverse = 1.0 / (
            jnp.sum(weights, axis=-1, keepdims=True) + jnp.sum(pweights, axis=-1, keepdims=True)
        )
        weights = (weights * inverse).astype(jnp.bfloat16)
        pweights = (pweights * inverse).astype(jnp.bfloat16)
        probs[rows, 0:width] = weights
        pprobs[rows, :] = pweights
        att[rows, :] = dot_nn(weights, qkv[0:width, 256:384]) + dot_nn(pweights, pv[...])
        for c in (2 * t, 2 * t + 1):
            grows = slice(c * 64, c * 64 + 64)
            alpha = rates[0, c * 8 + head]
            theta = rates[1, c * 8 + head]
            high, low = split_two(state)
            states[c] = high
            recalled = dot_nt(qkv[grows, 0:128], high) + dot_nt(qkv[grows, 0:128], low)
            rec[grows, :] = recalled * scale
            both = dot_tn(qkv[grows, 128:384], qkv[grows, 128:256])
            gram_high, gram_low = split_two(both[:128] * (theta / HEAD_WIDTH_SIZE))
            change = (
                dot_nn(high, gram_high) + dot_nn(low, gram_high) + dot_nn(high, gram_low)
            ) - both[128:] * (theta * scale)
            moment = momentum * moment - change
            state = (1.0 - alpha) * state + moment
        mixed[rows, :] = (att[rows, :] + gate[rows, :] * rec[rows, :]).astype(jnp.bfloat16)
    for k in range(8):
        hk = head_of(x, f, k)
        piece = jnp.concatenate(
            [
                mixed[pl.ds(pl.multiple_of(hk * 64, 64), 64), :],
                mixed[pl.ds(pl.multiple_of((15 - hk) * 64, 64), 64), :],
            ],
            axis=0,
        )
        out = send if k & 1 else keep
        out[k >> 1] = dot_nn(piece, wo).astype(jnp.bfloat16)


def mixer_backward_kernel(idx, rates, *refs):
    blocks = refs[0:8]
    w_out, w_full, qkv, gate, att, rec, probs, pprobs, states, pk, pv = refs[8:19]
    send, keep, dqkvg, branch = refs[19:23]
    gm, ds, dk, dv, dsp = refs[23:28]
    x, f = idx[1], idx[2]
    head = 2 * f + x
    scale = HEAD_WIDTH_SIZE ** (-0.5)
    wo = w_out[pl.ds(pl.multiple_of(x * 128, 128), 128), :]
    for k in range(8):
        hk = head_of(x, f, k)
        early = pl.ds(pl.multiple_of(hk * 64, 64), 64)
        late = pl.ds(pl.multiple_of((15 - hk) * 64, 64), 64)
        block = blocks[k][...]
        grad = dot_nt(block, wo).astype(jnp.bfloat16)
        gm[early, :] = grad[:64]
        gm[late, :] = grad[64:]
        branch[early, :] = block[:64]
        branch[late, :] = block[64:]
    grad_state = jnp.zeros((128, 128), jnp.float32)
    grad_moment = jnp.zeros((128, 128), jnp.float32)
    for t in range(7, -1, -1):
        rows = slice(t * 128, t * 128 + 128)
        width = (t + 1) * 128
        grad_low = gm[rows, :]
        grad = grad_low.astype(jnp.float32)
        opened = gate[rows, :]
        dqkvg[rows, 384:512] = (grad * rec[rows, :] * opened * (1.0 - opened)).astype(jnp.bfloat16)
        dy_tile = (grad * opened).astype(jnp.bfloat16)
        row_delta = jnp.sum(grad * att[rows, :], axis=-1, keepdims=True)
        grad_probs = dot_nt(grad_low, qkv[0:width, 256:384])
        ds_tile = (probs[rows, 0:width].astype(jnp.float32) * (grad_probs - row_delta)).astype(
            jnp.bfloat16
        )
        ds[rows, 0:width] = ds_tile
        grad_pprobs = dot_nt(grad_low, pv[...])
        dsp_tile = (pprobs[rows, :].astype(jnp.float32) * (grad_pprobs - row_delta)).astype(
            jnp.bfloat16
        )
        dsp[rows, :] = dsp_tile
        query_grad = (
            dot_nn(ds_tile, qkv[0:width, 128:256]) + dot_nn(dsp_tile, pk[...])
        ) * scale
        for c in (2 * t + 1, 2 * t):
            grows = slice(c * 64, c * 64 + 64)
            local = slice((c - 2 * t) * 64, (c - 2 * t) * 64 + 64)
            alpha = rates[0, c * 8 + head]
            theta = rates[1, c * 8 + head]
            query, key, value = qkv[grows, 0:128], qkv[grows, 128:256], qkv[grows, 256:384]
            dy_rows = dy_tile[local]
            state = states[c]
            summed = grad_state + grad_moment
            high, low = split_two(summed)
            gram_high, gram_low = split_two(dot_tn(key, key) * (theta / HEAD_WIDTH_SIZE))
            product = dot_nn(high, gram_high) + dot_nn(low, gram_high) + dot_nn(high, gram_low)
            grad_state = (
                dot_tn(dy_rows, query) * scale + (1.0 - alpha) * grad_state - product
            )
            grad_moment = momentum * summed
            key_summed = dot_nt(key, high) * scale
            error = value.astype(jnp.float32) - dot_nt(key, state) * scale
            dv[grows, :] = theta * key_summed
            dk[grows, :] = (theta * scale) * (
                dot_nn(error.astype(jnp.bfloat16), high)
                - dot_nn(key_summed.astype(jnp.bfloat16), state)
            )
            dqkvg[grows, 0:128] = (
                query_grad[local] + dot_nn(dy_rows, state) * scale
            ).astype(jnp.bfloat16)
    grad_pk = dot_tn(dsp[...], qkv[:, 0:128]) * scale
    grad_pv = dot_tn(pprobs[...], gm[...])
    for t in range(8):
        rows = slice(t * 128, t * 128 + 128)
        rest = slice(t * 128, 1024)
        key_grad = dk[rows, :] + dot_tn(ds[rest, rows], qkv[rest, 0:128]) * scale
        value_grad = dv[rows, :] + dot_tn(probs[rest, rows], gm[rest, :])
        dqkvg[rows, 128:256] = key_grad.astype(jnp.bfloat16)
        dqkvg[rows, 256:384] = value_grad.astype(jnp.bfloat16)
    for k in range(8):
        hk = head_of(x, f, k)
        piece = jnp.concatenate(
            [
                dqkvg[pl.ds(pl.multiple_of(hk * 64, 64), 64), :],
                dqkvg[pl.ds(pl.multiple_of((15 - hk) * 64, 64), 64), :],
            ],
            axis=0,
        )
        out = send if k & 1 else keep
        out[k >> 1, 0:128, :] = dot_nt(piece, w_full[...]).astype(jnp.bfloat16)
        j = k & 3
        extra = jnp.concatenate(
            [
                grad_pk[4 * j : 4 * j + 4],
                grad_pv[4 * j : 4 * j + 4],
                jnp.zeros((EXTRA - 8, 128), jnp.float32),
            ],
            axis=0,
        )
        out[k >> 1, 128 : 128 + EXTRA, :] = jnp.zeros((EXTRA, 1024), jnp.bfloat16)
        out[k >> 1, 128 : 128 + EXTRA, pl.ds(pl.multiple_of(head * 128, 128), 128)] = extra.astype(
            jnp.bfloat16
        )


def lay_chunk(out, rows, count, width):
    out[256 : 256 + count, :] = rows[:, 0:width]
    left = 1024 - width
    part = count * left // width
    for i in range(count // part):
        out[256 + count : 256 + count + part, i * left : (i + 1) * left] = rows[
            i * part : (i + 1) * part, width:1024
        ]


def lay_chunks(z, outs, total_rows, count, width):
    for j in range(4):
        first = pl.multiple_of((z ^ j) * count, 32)
        rows = total_rows[pl.ds(first, count), :].astype(jnp.bfloat16)
        lay_chunk(outs[j & 1].at[j >> 1], rows, count, width)


def mixer_weights_kernel(idx, normed, dqkvg, mixed, branch, keep, send, total, total_o):
    z, f = idx[0], idx[2]
    outs = (keep, send)
    for t in range(4):
        total[...] = dot_tn(normed[:, t * 256 : t * 256 + 256], dqkvg[...])
        spot = pl.ds(pl.multiple_of((t ^ f) * 64, 64), 64)
        for j in range(4):
            outs[j & 1][j >> 1, spot, :] = total[
                pl.ds(pl.multiple_of((z ^ j) * 64, 64), 64), :
            ].astype(jnp.bfloat16)
    total_o[...] = dot_tn(mixed[...], branch[...])
    lay_chunks(z, outs, total_o, 32, 512)


def feed_kernel(idx, *refs):
    blocks, cots, parts = refs[0:8], refs[8:16], refs[16:22]
    w_down = refs[22]
    send_g, keep_g, send_d, keep_d, active, dgu = refs[23:29]
    w_full, wd = refs[29:31]
    z, x, f = idx[0], idx[1], idx[2]
    lay_weights(z, f, parts, w_full)
    wd[0:352, :] = w_down[pl.ds(pl.multiple_of(x * 352, 32), 352), :]
    wd[352:HIDDEN_PAD, :] = jnp.zeros((HIDDEN_PAD - 352, 1024), jnp.bfloat16)
    for k in range(4):
        rows = slice(k * 256, k * 256 + 256)
        feed = jnp.concatenate([blocks[2 * k][...], blocks[2 * k + 1][...]], axis=0)
        cot = jnp.concatenate([cots[2 * k][...], cots[2 * k + 1][...]], axis=0)
        gate_up = dot_nn(feed, w_full[...])
        g, u = gate_up[:, :HIDDEN_PAD], gate_up[:, HIDDEN_PAD:]
        sigma = jax.nn.sigmoid(g)
        active_low = (g * sigma * u).astype(jnp.bfloat16)
        active[rows, :] = active_low
        grad_active = dot_nt(cot, wd[...])
        grad_g = (grad_active * u * sigma * (1.0 + g * (1.0 - sigma))).astype(jnp.bfloat16)
        grad_u = (grad_active * g * sigma).astype(jnp.bfloat16)
        grad_low = jnp.concatenate([grad_g, grad_u], axis=1)
        dgu[rows, :] = grad_low
        grad_feed = dot_nt(grad_low, w_full[...]).astype(jnp.bfloat16)
        keep_g[k] = grad_feed[:128]
        send_g[k] = grad_feed[128:]
        down = dot_nn(active_low, wd[...]).astype(jnp.bfloat16)
        keep_d[k] = down[:128]
        send_d[k] = down[128:]


def feed_weights_kernel(idx, dgu, active, *refs):
    blocks, cot_blocks = refs[0:8], refs[8:16]
    keeps, sends = refs[16:18], refs[18:20]
    total, total_d, feeds, cots, laid = refs[20:25]
    z, f = idx[0], idx[2]
    for k in range(8):
        feeds[k * 128 : k * 128 + 128, :] = blocks[k][...]
        cots[k * 128 : k * 128 + 128, :] = cot_blocks[k][...]
    half = FIRST_LANES
    for t in range(4):
        total[...] = dot_tn(feeds[:, t * 256 : t * 256 + 256], dgu[...])
        spot = pl.ds(pl.multiple_of((t ^ f) * 64, 64), 64)
        for j in range(4):
            rows = total[pl.ds(pl.multiple_of((z ^ j) * 64, 64), 64), :].astype(jnp.bfloat16)
            outs = sends if j & 1 else keeps
            outs[0][j >> 1, spot, :] = rows[:, 0:half]
            outs[1][j >> 1, spot, :] = rows[:, half:]
    total_d[...] = dot_tn(active[...], cots[...])
    for j in range(4):
        first = pl.multiple_of((z ^ j) * Z_HIDDEN, 32)
        lay_chunk(laid, total_d[pl.ds(first, Z_HIDDEN), :].astype(jnp.bfloat16), Z_HIDDEN, 768)
        outs = sends if j & 1 else keeps
        outs[0][j >> 1, 256:, :] = laid[256:, 0:half]
        outs[1][j >> 1, 256:, :] = laid[256:, half:]


def add_kernel(keep, received, s0, s1, s2, s3):
    s0[...] = keep[0].astype(jnp.float32) + received[0].astype(jnp.float32)
    for k, out in ((1, s1), (2, s2), (3, s3)):
        out[...] = (keep[k].astype(jnp.float32) + received[k].astype(jnp.float32)).astype(
            jnp.bfloat16
        )


def total_of(refs):
    return (
        refs[0][...]
        + refs[1][...].astype(jnp.float32)
        + refs[2][...].astype(jnp.float32)
        + refs[3][...].astype(jnp.float32)
    )


def residual_kernel(x, gain, s0, r1, r2, r3, residual, feed):
    values = x[...].astype(jnp.float32) + total_of((s0, r1, r2, r3))
    residual[...] = values
    feed[...] = (values * rms_scale(values) * gain[...]).astype(jnp.bfloat16)


def norm_grad(values, gain, grad):
    inv = rms_scale(values)
    scaled = grad * gain
    return inv * scaled - values * (inv * inv * inv) * jnp.mean(
        scaled * values, axis=-1, keepdims=True
    )


def branch_kernel(residual, gain, cot, s0, r1, r2, r3, grad_residual, branch):
    grad = total_of((s0, r1, r2, r3))
    total = cot[...].astype(jnp.float32) + norm_grad(residual[...], gain[...], grad)
    grad_residual[...] = total
    branch[...] = total.astype(jnp.bfloat16)


def split_kernel(order, keep, received, own, beside, crossing):
    def total(k):
        return keep[k].astype(jnp.float32) + received[k].astype(jnp.float32)

    own[...] = total(order[0])
    beside[...] = total(order[1])
    for i in range(2):
        crossing[i] = total(order[2 + i]).astype(jnp.bfloat16)


def far_kernel(own, passed, received, out_own, out_passed):
    out_own[...] = own[...] + received[0].astype(jnp.float32)
    out_passed[...] = (passed[...] + received[1].astype(jnp.float32)).astype(jnp.bfloat16)


def tokens_kernel(x, gain, grad_residual, own_sum, received, out, persist):
    total = own_sum[...] + received[...].astype(jnp.float32)
    grad = total[0:128]
    persist[...] = total[128:136]
    values = x[...].astype(jnp.float32)
    out[...] = (grad_residual[...] + norm_grad(values, gain[...], grad)).astype(jnp.bfloat16)


def output_kernel(residual, own_sum, *refs):
    received, out = refs[:-1], refs[-1]
    total = residual[...] + own_sum[...]
    for piece in received:
        total = total + piece[...].astype(jnp.float32)
    out[...] = total.astype(jnp.bfloat16)


def half_kernel(keep, received, own, passed):
    own[...] = keep[0].astype(jnp.float32) + received[0].astype(jnp.float32)
    passed[...] = (keep[1].astype(jnp.float32) + received[1].astype(jnp.float32)).astype(
        jnp.bfloat16
    )


def whole_kernel(pieces, *refs):
    own, received, outs = refs[:pieces], refs[pieces : 2 * pieces], refs[2 * pieces :]
    total = [
        (a[...] + b[...].astype(jnp.float32)).astype(jnp.bfloat16) for a, b in zip(own, received)
    ]
    total = jnp.concatenate(total, axis=1)
    for j in range(4):
        outs[j][...] = total[j * 64 : j * 64 + 64]
    outs[4][...] = total[256:]


def join_kernel(*refs):
    parts, rest, out = refs[0:4], refs[4], refs[5]
    for j in range(4):
        out[j * 64 : j * 64 + 64, :] = parts[j][...]
    out[256:, :] = rest[...]


def row_sums(products, out):
    out[...] = jnp.sum(jnp.transpose(products), axis=0, keepdims=True)


def feed_unpack_kernel(idx, *refs):
    parts = refs[0:8]
    wgu, gain = refs[8:10]
    out_gu, out_down, out_gain = refs[10:13]
    laid = refs[13]
    z, x, f = idx[0], idx[1], idx[2]
    width = FF // 8
    for j in range(4):
        for dx in range(2):
            part = parts[2 * j + dx]
            zj, xj = z ^ j, x ^ dx
            for jf in range(4):
                head = 2 * (f ^ jf) + xj
                laid[zj, head] = part[jf * 64 : jf * 64 + 64, :]

            lower = part[256:352, :].astype(jnp.float32)
            upper = part[352:384, :].astype(jnp.float32)
            valid = 64
            base = pl.multiple_of(xj * 352 + zj * Z_HIDDEN, 32)

            def put(first, count):
                at = pl.ds(pl.multiple_of(base + first, 32), count)
                out_down[at, 0:768] = lower[first : first + count]
                for i in range(first // 32, (first + count) // 32):
                    spot = pl.ds(pl.multiple_of(base + 32 * i, 32), 32)
                    out_down[spot, 768:1024] = upper[:, i * 256 : (i + 1) * 256]

            put(0, valid)

            @pl.when(zj < 3)
            def _():
                put(64, 32)

    for zj in range(4):
        for side in range(2):
            rows = jnp.concatenate(
                [
                    laid[zj, head][:, side * HIDDEN_PAD : side * HIDDEN_PAD + width]
                    for head in range(8)
                ],
                axis=1,
            )
            out_gu[zj * 64 : zj * 64 + 64, side * FF : side * FF + FF] = rows.astype(jnp.float32)
    sums = jnp.zeros((256, 128), jnp.float32)
    for t in range(2 * FF // 128):
        cols = slice(t * 128, t * 128 + 128)
        sums = sums + out_gu[:, cols] * wgu[:, cols].astype(jnp.float32)
    row_sums(sums, out_gain)
    out_gain[...] = out_gain[...] / gain[...].astype(jnp.float32)


def mixer_unpack_kernel(idx, *refs):
    parts = refs[0:8]
    wq, wg, gain = refs[8:11]
    out_qkv, out_gate, out_out, out_gain = refs[11:15]
    z, x, f = idx[0], idx[1], idx[2]
    for j in range(4):
        for dx in range(2):
            part = parts[2 * j + dx]
            zj, xj = z ^ j, x ^ dx
            rows = pl.ds(pl.multiple_of(zj * 64, 64), 64)
            for jf in range(4):
                head = 2 * (f ^ jf) + xj
                start = pl.multiple_of(head * 128, 128)
                for side in range(3):
                    out_qkv[rows, pl.ds(pl.multiple_of(side * 1024 + start, 128), 128)] = part[
                        jf * 64 : jf * 64 + 64, side * 128 : side * 128 + 128
                    ].astype(jnp.float32)
                out_gate[rows, pl.ds(start, 128)] = part[jf * 64 : jf * 64 + 64, 384:512].astype(
                    jnp.float32
                )
            spot = pl.ds(pl.multiple_of(xj * 128 + zj * 32, 32), 32)
            out_out[spot, 0:512] = part[256:288, :].astype(jnp.float32)
            out_out[spot, 512:1024] = part[288:320, :].astype(jnp.float32)
    sums = jnp.zeros((256, 128), jnp.float32)
    for t in range(24):
        cols = slice(t * 128, t * 128 + 128)
        sums = sums + out_qkv[:, cols] * wq[:, cols].astype(jnp.float32)
    for t in range(8):
        cols = slice(t * 128, t * 128 + 128)
        sums = sums + out_gate[:, cols] * wg[:, cols].astype(jnp.float32)
    row_sums(sums, out_gain)
    out_gain[...] = out_gain[...] / gain[...].astype(jnp.float32)


def sum_cores(keep, send):
    block = keep.shape[1:]
    return call(
        add_kernel,
        (),
        (keep, flip(send, 0, 1)),
        [(block, jnp.float32)] + [(block, jnp.bfloat16)] * 3,
        name="core_sum",
    )


def split_sums(keep, received, order, name):
    rows = keep.shape[1:]
    return call(
        functools.partial(split_kernel, order),
        (),
        (keep, received),
        [(rows, jnp.float32), (rows, jnp.float32), ((2, *rows), jnp.bfloat16)],
        name=name,
    )


def second_stage(own, beside, received, name):
    rows = own.shape
    return call(
        far_kernel,
        (),
        (own, beside, received),
        [(rows, jnp.float32), (rows, jnp.bfloat16)],
        name=name,
    )


def cross_chips(s0, s1, s2, s3):
    return s0, flip(s1, 0, 2), flip(s2, 1, 0), flip(s3, 1, 2)


def half_sum(keep, received, name):
    _, rows, width = keep.shape
    return call(
        half_kernel,
        (),
        (keep, received),
        [((rows, width), jnp.float32), ((rows, width), jnp.bfloat16)],
        name=name + "_half",
    )


def whole_sum(own, moved, name):
    rows = own[0].shape[0]
    width = sum(piece.shape[1] for piece in own)
    return call(
        functools.partial(whole_kernel, len(own)),
        (),
        (*own, *moved),
        [((64, width), jnp.bfloat16)] * 4 + [((rows - 256, width), jnp.bfloat16)],
        name=name + "_whole",
    )


def hand_rows(parts):
    return [parts[0]] + [flip(parts[j], 0, j) for j in range(1, 4)]


def join(parts, rest, name):
    rows, width = 256 + rest.shape[0], rest.shape[1]
    (joined,) = call(
        join_kernel, (), (*parts, rest), [((rows, width), jnp.bfloat16)], name=name + "_join"
    )
    return joined


def spread_far(joined):
    return flip_z(joined, 2), flip_z(joined, 1)


def in_planes(
    tokens,
    cotangent,
    segments,
    decay_index,
    step_index,
    w_qkv,
    w_gate,
    w_out,
    w_gu,
    w_down,
    persist_keys,
    persist_values,
    norm_gain,
    ffn_gain,
):
    bf16, f32 = jnp.bfloat16, jnp.float32
    ctx = lax.axis_index("ctx")
    f = lax.axis_index("fsdp")
    z, x = ctx // 2, ctx % 2
    head = 2 * f + x
    idx = jnp.stack([z, x, f, head]).astype(jnp.int32)

    own = to_plane(tokens[0])
    anywhere = pl.BlockSpec(memory_space=pl.ANY)
    wq_parts = pl.pallas_call(
        pack_qkvg_kernel,
        out_shape=[jax.ShapeDtypeStruct((256 + EXTRA, 512), bf16)] * 2
        + [jax.ShapeDtypeStruct((2, 256 + EXTRA, 512), bf16)],
        in_specs=[sspec(), anywhere, anywhere] + [vspec()] * 3,
        out_specs=[vspec()] * 3,
        scratch_shapes=[pltpu.SemaphoreType.DMA((16,))],
        compiler_params=pltpu.CompilerParams(vmem_limit_bytes=60 * 1024 * 1024),
        cost_estimate=pl.CostEstimate(flops=1000, bytes_accessed=1000, transcendentals=0),
        name="pack_qkvg",
    )(
        idx,
        w_qkv,
        w_gate,
        persist_keys,
        persist_values,
        jnp.concatenate([norm_gain, ffn_gain]).reshape(1, 512),
    )
    gu_parts = call(
        pack_gu_kernel,
        (idx,),
        (w_gu,),
        [((256, 768), bf16)] * 2 + [((2, 128, 768), bf16)],
        name="pack_gu",
    )
    ints = jnp.concatenate([segments[0], decay_index[0].reshape(-1), step_index[0].reshape(-1)])
    ints = to_plane(after(ints.reshape(10, 128), wq_parts[0]))
    rates = jnp.stack(
        [0.6 * jnp.exp2(-ints[8].astype(f32)), 0.1 * jnp.exp2(-ints[9].astype(f32))]
    )
    far = flip(wq_parts[2], 0, 2)
    own = after(own, wq_parts[0])
    near = gather_chips(own)
    wq_beside = flip(wq_parts[1], 0, 1)
    wq_parts = [wq_parts[0], wq_beside, far, flip(far, 0, 1)]
    own_cot = to_plane(after(cotangent[0], own))
    gu_far = flip(after(gu_parts[2], own), 0, 2)
    blocks = gather_cores([near[0], *near[1:]])
    rates = after(rates, own_cot)
    ready = after(own_cot, near[2])
    cot_near = [own_cot, flip(ready, 0, 2), flip(ready, 1, 0)]
    cot_near += [flip(cot_near[1], 1, 0)]
    rates = rates
    block = (128, 1024)
    quad = ((4, 128, 1024), bf16)
    (
        send,
        keep,
        normed,
        w_full,
        qkv,
        gate,
        att,
        rec,
        probs,
        pprobs,
        states,
        mixed,
        gain_one,
        gain_two,
        pk,
        pv,
    ) = call(
        mixer_forward_kernel,
        (idx, rates),
        (ints, *blocks, *wq_parts, w_out),
        [
            quad,
            quad,
            ((1024, 1024), bf16),
            ((1024, 512), bf16),
            ((1024, 384), bf16),
            ((1024, 128), f32),
            ((1024, 128), f32),
            ((1024, 128), f32),
            ((1024, 1024), bf16),
            ((1024, 16), bf16),
            ((16, 128, 128), bf16),
            ((1024, 128), bf16),
            ((1, 1024), f32),
            ((1, 1024), f32),
            ((16, 128), bf16),
            ((16, 128), bf16),
        ],
        name="mixer_forward",
        spare=10,
        us=10.0,
    )
    send = after(send, *cot_near[1:], gu_far)
    sums = sum_cores(keep, send)
    shares = cross_chips(*sums)
    gu_next = flip_z(gu_far, 1)
    gu_parts = [gu_parts[0], flip(gu_parts[1], 0, 1), gu_far, flip(gu_far, 0, 1)]
    gu_parts += [gu_next, flip(after(gu_next, shares[3]), 0, 1)]
    cots = gather_cores(cot_near)
    residual, feed = call(
        residual_kernel,
        (),
        (own, gain_two, *shares),
        [(block, f32), (block, bf16)],
        name="residual",
    )
    feed_near = gather_chips(feed)
    feeds = gather_cores(feed_near)
    send_g, keep_g, send_d, keep_d, active, dgu = call(
        feed_kernel,
        (idx,),
        (*feeds, *cots, *gu_parts, w_down),
        [
            quad,
            quad,
            quad,
            quad,
            ((1024, HIDDEN_PAD), bf16),
            ((1024, 2 * HIDDEN_PAD), bf16),
        ],
        scratch=[((1024, 2 * HIDDEN_PAD), bf16), ((HIDDEN_PAD, 1024), bf16)],
        name="feed",
        spare=10,
        us=7.5,
    )
    feed_keep, feed_later_keep, feed_send, feed_later_send = call(
        feed_weights_kernel,
        (idx,),
        (dgu, active, *feeds, *cots),
        [
            ((2, 256 + 4 * Z_HIDDEN // 3, lanes), bf16)
            for lanes in (FIRST_LANES, 768 - FIRST_LANES) * 2
        ],
        scratch=[
            ((256, 768), f32),
            ((HIDDEN_PAD, 1024), f32),
            ((1024, 1024), bf16),
            ((1024, 1024), bf16),
            ((256 + 4 * Z_HIDDEN // 3, 768), bf16),
        ],
        name="feed_weights",
        spare=10,
        us=3.5,
    )
    sums = sum_cores(after(keep_g, feed_send), send_g)
    send_d = after(send_d, sums[0])
    shares = cross_chips(*sums)
    feed_received = flip_z(feed_send, 1)
    feed_later_received = flip_z(after(feed_later_send, sums[0]), 1)
    out_sums = split_sums(keep_d, flip(send_d, 0, 1), (0, 1, 2, 3), "output_cores")
    grad_residual, branch = call(
        branch_kernel,
        (),
        (residual, gain_two, after(own_cot, out_sums[0]), *shares),
        [(block, f32), (block, bf16)],
        name="branch",
    )
    feed_own, feed_passed = half_sum(after(feed_keep, branch), feed_received, "feed")
    branch_near = gather_chips(branch, after(branch, feed_passed))
    feed_moved = flip_z(feed_passed, 2)
    branches = gather_cores(branch_near)
    feed_later, feed_later_passed = half_sum(
        after(feed_later_keep, branch_near[3]), feed_later_received, "feed_later"
    )
    rates = after(rates, feed_later_passed, feed_moved)
    feed_later_moved = flip_z(feed_later_passed, 2)
    out_shares = (out_sums[0], flip(after(out_sums[2], branches[6]), 1, 0))
    send, keep, dqkvg, branch_all = call(
        mixer_backward_kernel,
        (idx, rates),
        (*branches, w_out, w_full, qkv, gate, att, rec, probs, pprobs, states, pk, pv),
        [
            ((4, 128 + EXTRA, 1024), bf16),
            ((4, 128 + EXTRA, 1024), bf16),
            ((1024, 512), bf16),
            ((1024, 1024), bf16),
        ],
        scratch=[
            ((1024, 128), bf16),
            ((1024, 1024), bf16),
            ((1024, 128), f32),
            ((1024, 128), f32),
            ((1024, 16), bf16),
        ],
        name="mixer_backward",
        spare=10,
        us=13.0,
    )
    send, dqkvg = lax.optimization_barrier(
        (send, dqkvg, feed_moved, feed_later_moved, *out_shares[1:])
    )[:2]
    *feed_parts, feed_rest = whole_sum(
        (after(feed_own, send), feed_later), (feed_moved, feed_later_moved), "feed"
    )
    feed_parts = hand_rows(feed_parts)
    dqkvg = after(dqkvg, feed_rest)
    mixer_keep, mixer_send = call(
        mixer_weights_kernel,
        (idx,),
        (normed, dqkvg, mixed, branch_all),
        [((2, 320, 512), bf16)] * 2,
        scratch=[((256, 512), f32), ((128, 1024), f32)],
        name="mixer_weights",
        spare=10,
        us=2.2,
    )
    out_own, out_passed = second_stage(
        after(out_sums[0], mixer_send), out_sums[1], out_shares[1], "output_far"
    )
    out_shares = (out_own, flip(out_passed, 0, 2))
    (result,) = call(output_kernel, (), (residual, *out_shares), [(block, bf16)], name="output")
    tokens_sums = split_sums(
        after(keep, feed_rest),
        flip(send, 0, 1),
        (0, 1, 2, 3),
        "tokens_cores",
    )
    feed_joined = join(feed_parts, after(feed_rest, mixer_send, tokens_sums[0]), "feed")
    feed_second = flip_z(feed_joined, 2)
    feed_beside = flip(feed_joined, 1, 0)
    mixer_own, mixer_passed = half_sum(
        after(mixer_keep, feed_joined, result), flip_z(mixer_send, 1), "mixer"
    )
    mixer_moved = flip_z(mixer_passed, 2)
    feed_first = flip_z(feed_joined, 1)
    tokens_far = flip(after(tokens_sums[2], mixer_passed), 1, 0)
    feed_first_beside = flip(after(feed_first, mixer_passed), 1, 0)
    mixer_own = after(mixer_own, feed_beside)
    *mixer_parts, mixer_rest = whole_sum((mixer_own,), (mixer_moved,), "mixer")
    feed_third = flip_z(feed_second, 1)
    feed_second_beside = flip(after(feed_second, mixer_rest), 1, 0)
    mixer_joined = join(
        hand_rows(mixer_parts), after(mixer_rest, tokens_far, feed_first_beside), "mixer"
    )
    mixer_second, mixer_first = spread_far(mixer_joined)
    mixer_beside = flip(mixer_joined, 1, 0)
    result = to_plane(after(result,   mixer_first))
    feed_third_beside = flip(
        after(
            feed_third,
            mixer_joined,


        ),
        1,
        0,
    )
    tokens_own, tokens_passed = second_stage(
        after(
            tokens_sums[0],
            mixer_joined,


        ),
        tokens_sums[1],
        tokens_far,
        "tokens_far",
    )
    tokens_near = flip(tokens_passed, 0, 2)
    mixer_second = after(
        mixer_second,
        mixer_first,
        mixer_beside,
        feed_second_beside,
        tokens_near,
    )
    mixer_third = flip_z(mixer_second, 1)
    mixer_first_beside = flip(after(mixer_first, mixer_second), 1, 0)
    mixer_second_beside = flip(mixer_second, 1, 0)
    grad_tokens, persist = call(
        tokens_kernel,
        (),
        (after(own, mixer_second), gain_one, grad_residual, tokens_own, tokens_near),
        [(block, bf16), ((8, 1024), f32)],
        name="tokens",
    )
    grad_tokens = to_plane(grad_tokens)
    persist = persist + after(flip_z(persist, 1), mixer_third)
    feed_pieces = (
        feed_joined,
        feed_beside,
        feed_first,
        feed_first_beside,
        feed_second,
        feed_second_beside,
        feed_third,
        feed_third_beside,
    )

    grad_gu, grad_down, grad_ffn = call(
        feed_unpack_kernel,
        (idx,),
        (*feed_pieces, w_gu, after(ffn_gain.reshape(1, 256), mixer_second)),
        [((256, 2 * FF), f32), ((FF // 4, 1024), f32), ((1, 256), f32)],
        scratch=[((4, 8, 64, 768), bf16)],
        name="feed_unpack",
        spare=10,
        us=5.5,
    )
    mixer_third_beside = flip(
        after(
            mixer_third,
            grad_ffn,
            mixer_first_beside, mixer_second_beside,

        ),
        1,
        0,
    )
    persist = persist + flip_z(persist, 2)
    mixer_pieces = (
        mixer_joined,
        mixer_beside,
        mixer_first,
        mixer_first_beside,
        mixer_second,
        mixer_second_beside,
        mixer_third,
        mixer_third_beside,
    )
    grad_qkv, grad_gate, grad_out, grad_norm = call(
        mixer_unpack_kernel,
        (idx,),
        (*mixer_pieces, w_qkv, w_gate, after(norm_gain.reshape(1, 256))),
        [
            ((256, 3072), f32),
            ((256, 1024), f32),
            ((256, 1024), f32),
            ((1, 256), f32),
        ],
        name="mixer_unpack",
    )
    return (
        result[None],
        grad_tokens.astype(f32)[None],
        grad_qkv,
        grad_gate,
        grad_out,
        grad_gu,
        grad_down,
        persist[0:4],
        persist[4:8],
        grad_norm.reshape(256),
        grad_ffn.reshape(256),
    )


def solution(mesh):
    in_specs = (
        P("fsdp", "ctx", None),
        P("fsdp", "ctx", None),
        P("fsdp", None),
        P("fsdp", None, None),
        P("fsdp", None, None),
        P("fsdp", None),
        P("fsdp", None),
        P("fsdp", None),
        P("fsdp", None),
        P("fsdp", None),
        P("fsdp", None),
        P("fsdp", None),
        P("fsdp"),
        P("fsdp"),
    )
    out_specs = (
        P("fsdp", "ctx", None),
        P("fsdp", "ctx", None),
        P("fsdp", None),
        P("fsdp", None),
        P("fsdp", None),
        P("fsdp", None),
        P("fsdp", None),
        P("fsdp", None),
        P("fsdp", None),
        P("fsdp"),
        P("fsdp"),
    )
    planes = dict(mesh.shape) == {"ctx": HEADS, "fsdp": PLANES}
    return jax.shard_map(
        in_planes if planes else on_device, mesh=mesh, in_specs=in_specs, out_specs=out_specs, check_vma=False
    )
```
